512 devices in a mesh: row: 32 (over y_lo, x, core), col: 16 (over z, y_hi).
Axes of the slice: x: 4, y: 8 (y_hi: 2, y_lo: 4; y = y_hi * 4 + y_lo), z: 8, core: 2. Of those that a mesh axis runs over, the one named last changes fastest.
Arguments:
- noise: bfloat16 [256, 65536], P('row', 'col')
- data: bfloat16 [512, 65536], P('col', 'row'), may hold values from -6 to 6
- noise_weight: int32 [256], P('row'), may hold values from 1 to 8, as said below
- data_weight: int32 [512], P('col'), may hold values from 1 to 8, as said below
Outputs:
- targets: bfloat16 [256, 65536], P('row', 'col')
- noise_potential: float32 [256], P('row')
- data_potential: float32 [512], P('col')
The draws below stay inside these ranges and needn't reach their ends.
Inputs may be any that keep to these rules, and one draw needn't show every extreme that they name: `noise_weight`: weights rise in range with the sample index; the last sample has weight 8. `data_weight`: weights rise in range with the sample index; the last sample has weight 8.
All inputs are finite; a program needn't handle non-finite values.
Results may differ from the reference program's by a relative error of at most 0.025.
Values may be sent and summed in bfloat16 or wider, within the bound.
A program may use at most 64 MiB of HBM per device.

```python
import math
import jax
import jax.numpy as jnp
from jax import lax

F = 65536
DATA_DEV = 32
HALVES = 4
NOISE = 256
DATA = 512


def rising_weights(key, count):
    index = jnp.arange(count)
    upper = 3 + 6 * index // count
    values = 1 + jax.random.randint(key, (count,), 0, 1000) % upper
    return values.at[count - 1].set(8).astype(jnp.int32)


def row_offsets(key):
    first, second, third, fourth = jax.random.split(key, 4)
    chosen = jax.random.uniform(first, (NOISE,), jnp.float32) < 0.25
    forced = jnp.arange(NOISE) == jax.random.randint(second, (), 0, NOISE)
    chosen = jnp.logical_or(chosen, forced)
    sizes = jax.random.uniform(third, (NOISE,), jnp.float32, 3.0, 4.5)
    signs = jnp.where(jax.random.uniform(fourth, (NOISE,), jnp.float32) < 0.5, -1.0, 1.0)
    return jnp.where(chosen, sizes * signs, 0.0)[:, None]


def draw_noise(key, part):
    key = jax.random.fold_in(key, 11)
    first = jax.random.fold_in(key, 0)
    third = jax.random.fold_in(key, 2)
    base = jnp.clip(jax.random.normal(first, (NOISE, F), jnp.float32), -6.0, 6.0)
    return (base + row_offsets(third)).astype(jnp.bfloat16)


def draw_noise_weight(key, part):
    key = jax.random.fold_in(key, 12)
    return rising_weights(key, NOISE)


def draw_data_weight(key, part):
    key = jax.random.fold_in(key, 13)
    return rising_weights(key, DATA)


def levels(own_key, extent, pieces, low, top_value):
    gain = 1.0
    for axis_at, shards_of in pieces:
        heights = jax.random.uniform(jax.random.fold_in(jax.random.fold_in(own_key, 6), axis_at), (shards_of,), jnp.float32, low / len(pieces), top_value / len(pieces))
        gain = gain * jnp.repeat(jnp.exp(heights), extent[axis_at] // shards_of).reshape((-1,) + (1,) * (len(extent) - 1 - axis_at))
    return gain


def scatter_about(key, extent, deviation, reach, cuts=(), held_as=jnp.bfloat16):
    result = deviation * jax.random.normal(key, extent, jnp.float32)
    if cuts:
        result = result * levels(key, extent, cuts, -0.22, 0.18)
    return jnp.clip(result, -reach, reach).astype(held_as)


def setup_inputs(seed: int = 0) -> dict:
    key_of = jax.random.split(jax.random.key(seed), 5)
    noise = draw_noise(jax.random.fold_in(key_of[4], 71), 0)
    data = scatter_about(key_of[1], (DATA, F), 1.0, 6.0, ((0, 16), (1, 32)))
    noise_weight = draw_noise_weight(jax.random.fold_in(key_of[4], 71), 0)
    data_weight = draw_data_weight(jax.random.fold_in(key_of[4], 71), 0)
    return dict(noise=noise, data=data, noise_weight=noise_weight, data_weight=data_weight)


def lse_last(z):
    peak = lax.optimization_barrier(jnp.max(z, axis=1, keepdims=True))
    return peak[:, 0] + jnp.log(lax.optimization_barrier(jnp.sum(jnp.exp(z - peak), axis=1)))

def reference(noise, data, noise_weight, data_weight):
    width = noise.shape[1]
    eps = 1.0 / math.sqrt(width)
    noise_sq = jnp.einsum('nf,nf->n', noise, noise, preferred_element_type=jnp.float32)
    data_sq = jnp.einsum('nf,nf->n', data, data, preferred_element_type=jnp.float32)
    cross = jnp.dot(noise, data.T, preferred_element_type=jnp.float32)
    cost = (noise_sq[:, None] + data_sq[None, :] - 2.0 * cross) / width
    wa = noise_weight.astype(jnp.float32)
    wb = data_weight.astype(jnp.float32)
    log_a = jnp.log(wa / jnp.sum(wa))
    log_b = jnp.log(wb / jnp.sum(wb))
    data_pot = jnp.zeros((data.shape[0],), jnp.float32)
    noise_pot = jnp.zeros((noise.shape[0],), jnp.float32)
    for rounds in range(HALVES // 2):
        noise_pot = eps * log_a - eps * lse_last((data_pot[None, :] - cost) / eps)
        data_pot = eps * log_b - eps * lse_last(((noise_pot[:, None] - cost) / eps).T)
    plan = jnp.exp((noise_pot[:, None] + data_pot[None, :] - cost) / eps)
    mass = lax.optimization_barrier(jnp.sum(plan, axis=1))
    plan_low = plan.astype(jnp.bfloat16)
    blocks = data.shape[0] // DATA_DEV
    data_blocks = data.reshape(blocks, DATA_DEV, width)
    plan_blocks = jnp.transpose(plan_low.reshape(noise.shape[0], blocks, DATA_DEV), (1, 0, 2))

    def accumulate(total, pair):
        part = jnp.dot(pair[0], pair[1], preferred_element_type=jnp.float32).astype(jnp.bfloat16)
        part = lax.optimization_barrier(part)
        return (total + part.astype(jnp.float32), 0)
    start = jnp.zeros((noise.shape[0], width), jnp.float32)
    summed, unused = lax.scan(accumulate, start, (plan_blocks, data_blocks))
    targets = (summed / mass[:, None]).astype(jnp.bfloat16)
    return (targets, noise_pot, data_pot)
```

```python
import functools
import math

import jax
import jax.numpy as jnp
from jax import lax
from jax.experimental import pallas as pl
from jax.experimental.pallas import tpu as pltpu
from jax.sharding import PartitionSpec as P

HALVES = 4
MESH = pl.DeviceIdType.MESH
F32 = jnp.float32
BF16 = jnp.bfloat16
LANES = 128


def kernel(
    Q, C, width,
    nw_ref, dw_ref, noise_ref, data_ref,
    out_ref, npot_ref, dpot_ref,
    stage, nbuf, dbuf, pbuf, abuf, bbuf, rbuf, cbuf, gbuf, gall, ubuf, labuf,
    massbuf, plow, tbuf, vbuf,
    ns, nr, ds_, dr, sib_s, sib_r, as_, ar, bs, br, cs, cr, gs, gr, os_, or_,
):
    FQ = width // (Q * C)
    half = C // 2
    eps = 1.0 / math.sqrt(width)
    row = lax.axis_index("row")
    c = lax.axis_index("col")
    q = row // 2
    k = row % 2
    other = 1 - k
    sibling = (q * 2 + other, c)

    def data_target(j):
        chunk = row * half + j
        return (chunk % Q) * 2 + c // half, chunk // Q

    source_row = (c * Q + q) // half

    def data_source(j):
        return source_row, k * half + j

    to_self = jnp.logical_and(source_row == row, c // half == k)
    n_self = jnp.where(to_self, 1, 0).astype(jnp.int32)

    barrier = pltpu.get_barrier_semaphore()

    def greet(device):
        pl.semaphore_signal(barrier, inc=1, device_id=device, device_id_type=MESH)

    def greet_row(s, carry):
        greet((lax.rem(q + s, Q) * 2 + k, c))
        return carry

    def greet_col(s, carry):
        greet((row, lax.rem(c + s, C)))
        return carry

    def greet_source(j, carry):
        sr, sc = data_source(j)

        @pl.when(jnp.logical_or(sr != row, sc != c))
        def _():
            greet((sr, sc))

        return carry

    greet(sibling)
    lax.fori_loop(1, Q, greet_row, 0)
    lax.fori_loop(0, half, greet_source, 0)
    lax.fori_loop(1, C, greet_col, 0)

    rows8 = lax.broadcasted_iota(jnp.int32, (8, LANES), 0)
    lanes1 = lax.broadcasted_iota(jnp.int32, (1, LANES), 1)
    own_w = jnp.zeros((8, LANES), jnp.int32)
    for i in range(8):
        own_w = jnp.where(rows8 == i, nw_ref[i], own_w)
    own_w = own_w.astype(F32).astype(BF16)
    for j in range(Q):
        stage[j, :, 0:FQ] = noise_ref[:, j * FQ:(j + 1) * FQ]
        stage[j, :, FQ:FQ + LANES] = own_w

    data_w = jnp.zeros((1, LANES), jnp.int32)
    base = (c % 4) * 32
    for i in range(32):
        data_w = jnp.where(lanes1 == base + i, dw_ref[i], data_w)
    cbuf[...] = jnp.zeros_like(cbuf)
    cbuf[2:3, :] = data_w.astype(F32)

    pl.semaphore_wait(barrier, (Q - 1) + (C - 1) + 1 + half - n_self)

    def send_data(j, carry):
        tr, tc = data_target(j)
        src = data_ref.at[:, pl.ds(pl.multiple_of(j * FQ, FQ), FQ)]
        is_self = jnp.logical_and(tr == row, tc == c)

        @pl.when(is_self)
        def _():
            pltpu.make_async_copy(src, dbuf.at[c], dr).start()

        @pl.when(jnp.logical_not(is_self))
        def _():
            pltpu.make_async_remote_copy(
                src, dbuf.at[c], ds_, dr, device_id=(tr, tc), device_id_type=MESH
            ).start()

        return carry

    lax.fori_loop(0, half, send_data, 0)

    def send_noise(s, carry):
        t = lax.rem(q + s, Q)
        pltpu.make_async_remote_copy(
            stage.at[t], nbuf.at[k, q], ns, nr,
            device_id=(t * 2 + k, c), device_id_type=MESH,
        ).start()
        return carry

    lax.fori_loop(1, Q, send_noise, 0)
    pltpu.make_async_copy(stage.at[q], nbuf.at[k, q], nr).start()
    pltpu.make_async_copy(nbuf.at[k], nbuf.at[k], nr).wait()

    noise_swap = pltpu.make_async_remote_copy(
        nbuf.at[k], nbuf.at[k], sib_s.at[0], sib_r.at[0],
        device_id=sibling, device_id_type=MESH,
    )
    noise_swap.start()

    own_data = dbuf.at[pl.ds(k * half, half)]
    pltpu.make_async_copy(own_data, own_data, dr).wait()
    data_swap = pltpu.make_async_remote_copy(
        own_data, own_data, sib_s.at[1], sib_r.at[1],
        device_id=sibling, device_id_type=MESH,
    )
    data_swap.start()
    dblock = dbuf[pl.ds(k * half, half)].reshape(half * 32, FQ)
    df = dblock.astype(F32)
    d2 = df * df
    d2_hi = d2.astype(BF16)
    d2_lo = (d2 - d2_hi.astype(F32)).astype(BF16)
    ones = jnp.ones((8, FQ), BF16)
    nt = (((1,), (1,)), ((), ()))
    dsq = lax.dot_general(ones, d2_hi, nt, preferred_element_type=F32)
    dsq = dsq + lax.dot_general(ones, d2_lo, nt, preferred_element_type=F32)
    dsq = dsq[0:1, :]

    pltpu.make_async_copy(nbuf.at[other], nbuf.at[other], sib_r.at[0]).wait()
    nf = nbuf[:, :, :, 0:FQ].astype(F32).reshape(16 * Q, FQ)
    wa = nbuf[:, :, :, FQ:FQ + LANES].astype(F32).reshape(16 * Q, LANES)
    nsq = jnp.sum(nf * nf, axis=1, keepdims=True)
    cross = lax.dot_general(nf.astype(BF16), dblock, nt, preferred_element_type=F32)
    part = nsq + dsq - 2.0 * cross
    for h in range(2):
        pbuf[:, h] = part[:, h * LANES:(h + 1) * LANES].reshape(Q, 16, LANES)

    def send_a(s, carry):
        t = lax.rem(q + s, Q)
        pltpu.make_async_remote_copy(
            pbuf.at[t], abuf.at[q], as_, ar,
            device_id=(t * 2 + k, c), device_id_type=MESH,
        ).start()
        return carry

    lax.fori_loop(1, Q, send_a, 0)
    pltpu.make_async_copy(pbuf.at[q], abuf.at[q], ar).start()
    w_sum = jnp.sum(wa, axis=0, keepdims=True)
    labuf[...] = jnp.log(wa / w_sum).reshape(Q, 16, LANES)
    pltpu.make_async_copy(abuf, abuf, ar).wait()
    total = abuf[0]
    for j in range(1, Q):
        total = total + abuf[j]

    for i in range(C):
        h, t = i // 8, i % 8
        bbuf[i] = total[h, 2 * t:2 * t + 2, :]

    def send_b(s, carry):
        t = lax.rem(c + s, C)
        pltpu.make_async_remote_copy(
            bbuf.at[t], rbuf.at[c], bs, br,
            device_id=(row, t), device_id_type=MESH,
        ).start()
        return carry

    lax.fori_loop(1, C, send_b, 0)
    pltpu.make_async_copy(bbuf.at[c], rbuf.at[c], br).start()
    pltpu.make_async_copy(rbuf, rbuf, br).wait()
    cbuf[0:2, :] = jnp.sum(rbuf[...], axis=0)

    def send_c(s, carry):
        t = lax.rem(c + s, C)
        pltpu.make_async_remote_copy(
            cbuf, gbuf.at[c], cs, cr, device_id=(row, t), device_id_type=MESH,
        ).start()
        return carry

    lax.fori_loop(1, C, send_c, 0)
    pltpu.make_async_copy(cbuf, gbuf.at[c], cr).start()
    pltpu.make_async_copy(gbuf, gbuf, cr).wait()
    for i in range(C):
        h, t = i // 8, i % 8
        gall[k, q, h, 2 * t:2 * t + 2, :] = gbuf[i, 0:2, :]

    def send_g(s, carry):
        t = lax.rem(q + s, Q)
        pltpu.make_async_remote_copy(
            gall.at[k, q], gall.at[k, q], gs, gr,
            device_id=(t * 2 + k, c), device_id_type=MESH,
        ).start()
        return carry

    lax.fori_loop(1, Q, send_g, 0)
    dw = [
        sum(gbuf[i, 2:3, :] for i in range(4 * b + 1, 4 * b + 4)) + gbuf[4 * b, 2:3, :]
        for b in range(C // 4)
    ]
    dw = jnp.concatenate(dw, axis=0)
    dw_sum = jnp.sum(jnp.sum(dw, axis=0, keepdims=True), axis=1, keepdims=True)
    log_b = jnp.log(dw / dw_sum).reshape(2, 2, 1, LANES)

    others = gall.at[k, pl.ds(0, Q - 1)]
    pltpu.make_async_copy(others, others, gr).wait()
    cost_swap = pltpu.make_async_remote_copy(
        gall.at[k], gall.at[k], sib_s.at[2], sib_r.at[2],
        device_id=sibling, device_id_type=MESH,
    )
    cost_swap.start()
    pltpu.make_async_copy(gall.at[other], gall.at[other], sib_r.at[2]).wait()

    scale = -1.0 / (width * eps)

    def scores(j):
        return gall[:, j] * scale

    v = jnp.zeros((2, 2, 1, LANES), F32)
    for rounds in range(HALVES // 2):

        def row_step(j, peak):
            s = scores(j)
            z = s + v
            m = jnp.max(jnp.max(z, axis=(0, 1)), axis=1, keepdims=True)
            e = jnp.sum(jnp.sum(jnp.exp(z - m), axis=(0, 1)), axis=1, keepdims=True)
            u = labuf[j] - (m + jnp.log(e))
            ubuf[j] = u
            return jnp.maximum(peak, jnp.max(s + u, axis=2, keepdims=True))

        peak = lax.fori_loop(
            0, Q, row_step, jnp.full((2, 2, 1, LANES), -jnp.inf, F32)
        )

        def col_step(j, acc):
            return acc + jnp.exp(scores(j) + ubuf[j] - peak)

        acc = lax.fori_loop(0, Q, col_step, jnp.zeros((2, 2, 16, LANES), F32))
        v = log_b - (peak + jnp.log(jnp.sum(acc, axis=2, keepdims=True)))

    def plan_step(j, carry):
        own = k * (Q // 2) + j
        p = jnp.exp(ubuf[own] + v + scores(own))
        massbuf[j] = jnp.broadcast_to(
            jnp.sum(jnp.sum(p, axis=(0, 1)), axis=1, keepdims=True), (16, LANES)
        )
        for b in range(4):
            plow[j, :, b * LANES:(b + 1) * LANES] = p[b // 2, b % 2].astype(BF16)
        return carry

    lax.fori_loop(0, Q // 2, plan_step, 0)

    pltpu.make_async_copy(
        dbuf.at[pl.ds(other * half, half)], dbuf.at[pl.ds(other * half, half)], sib_r.at[1]
    ).wait()
    value = jnp.dot(
        plow[...].reshape(8 * Q, C * 32), dbuf[...].reshape(C * 32, FQ),
        preferred_element_type=F32,
    )
    mass = massbuf[...].reshape(8 * Q, LANES)
    value = value / jnp.concatenate([mass] * (FQ // LANES), axis=1)
    tbuf[...] = value.reshape(Q, 8, FQ).astype(BF16)

    def send_t(s, carry):
        t = lax.rem(q + s, Q)
        pltpu.make_async_remote_copy(
            tbuf.at[t], out_ref.at[q], os_, or_,
            device_id=(t * 2 + k, c), device_id_type=MESH,
        ).start()
        return carry

    lax.fori_loop(1, Q, send_t, 0)
    pltpu.make_async_copy(tbuf.at[q], out_ref.at[q], or_).start()

    pair = ubuf[k * (Q // 2) + q // 2]
    own_u = jnp.where(q % 2 == 0, pair[0:8], pair[8:16])
    lanes8 = lax.broadcasted_iota(jnp.int32, (8, LANES), 1)
    own_u = jnp.sum(jnp.where(rows8 == lanes8, own_u, 0.0), axis=0, keepdims=True)
    npot_ref[...] = own_u[:, 0:8] * eps
    for b in range(4):
        vbuf[b] = v[b // 2, b % 2]
    block = vbuf[c // 4]
    own_v = block[:, 0:32]
    for t in range(1, 4):
        own_v = jnp.where(c % 4 == t, block[:, 32 * t:32 * t + 32], own_v)
    dpot_ref[...] = own_v * eps

    def sent(ref, sem):
        pltpu.make_async_copy(ref, ref, sem).wait()

    sent(stage.at[pl.ds(0, Q - 1)], ns)

    @pl.when(to_self)
    def _():
        sent(dbuf.at[pl.ds(0, half - 1)], ds_)

    @pl.when(jnp.logical_not(to_self))
    def _():
        sent(dbuf.at[pl.ds(0, half)], ds_)

    noise_swap.wait_send()
    data_swap.wait_send()
    cost_swap.wait_send()
    sent(pbuf.at[pl.ds(0, Q - 1)], as_)
    sent(bbuf.at[pl.ds(0, C - 1)], bs)
    sent(gbuf.at[pl.ds(0, C - 1)], cs)
    sent(others, gs)
    sent(tbuf.at[pl.ds(0, Q - 1)], os_)
    sent(out_ref, or_)


def per_device(Q, C, noise, data, noise_weight, data_weight):
    width = noise.shape[1] * C
    FQ = width // (Q * C)
    vmem = pl.BlockSpec(memory_space=pltpu.VMEM)
    smem = pl.BlockSpec(memory_space=pltpu.SMEM)
    anywhere = pl.BlockSpec(memory_space=pl.ANY)
    targets, noise_pot, data_pot = pl.pallas_call(
        functools.partial(kernel, Q, C, width),
        out_shape=(
            jax.ShapeDtypeStruct((Q, 8, FQ), BF16),
            jax.ShapeDtypeStruct((1, 8), F32),
            jax.ShapeDtypeStruct((1, 32), F32),
        ),
        in_specs=[smem, smem, vmem, anywhere],
        out_specs=(anywhere, vmem, vmem),
        scratch_shapes=[
            pltpu.VMEM((Q, 8, FQ + LANES), BF16),
            pltpu.VMEM((2, Q, 8, FQ + LANES), BF16),
            pltpu.VMEM((C, 32, FQ), BF16),
            pltpu.VMEM((Q, 2, 16, LANES), F32),
            pltpu.VMEM((Q, 2, 16, LANES), F32),
            pltpu.VMEM((C, 2, LANES), F32),
            pltpu.VMEM((C, 2, LANES), F32),
            pltpu.VMEM((4, LANES), F32),
            pltpu.VMEM((C, 4, LANES), F32),
            pltpu.VMEM((2, Q, 2, 16, LANES), F32),
            pltpu.VMEM((Q, 16, LANES), F32),
            pltpu.VMEM((Q, 16, LANES), F32),
            pltpu.VMEM((Q // 2, 16, LANES), F32),
            pltpu.VMEM((Q // 2, 16, C * 32), BF16),
            pltpu.VMEM((Q, 8, FQ), BF16),
            pltpu.VMEM((4, 1, LANES), F32),
        ] + [pltpu.SemaphoreType.DMA] * 4
        + [pltpu.SemaphoreType.DMA((3,))] * 2
        + [pltpu.SemaphoreType.DMA] * 10,
        compiler_params=pltpu.CompilerParams(
            collective_id=0, has_side_effects=True, vmem_limit_bytes=32 * 1024 * 1024
        ),
    )(noise_weight, data_weight, noise, data)
    targets = jnp.transpose(targets, (1, 0, 2)).reshape(8, Q * FQ)
    return (targets, noise_pot.reshape(8), data_pot.reshape(32))


def solution(mesh):
    placed = (P("row", "col"), P("col", "row"), P("row"), P("col"))
    return jax.shard_map(
        functools.partial(per_device, mesh.shape["row"] // 2, mesh.shape["col"]),
        mesh=mesh,
        in_specs=placed,
        out_specs=(P("row", "col"), P("row"), P("col")),
        check_vma=False,
    )
```

```python
import functools
import math

import jax
import jax.numpy as jnp
from jax import lax
from jax.experimental import pallas as pl
from jax.experimental.pallas import tpu as pltpu
from jax.sharding import PartitionSpec as P

HALVES = 4
MESH = pl.DeviceIdType.MESH
F32 = jnp.float32
BF16 = jnp.bfloat16
LANES = 128
X, YL, Z, YH = 4, 4, 8, 2
Y = YH * YL
Q = YL * X
C = Z * YH
NT = (((1,), (1,)), ((), ()))


def kernel(
    width,
    nw_hbm, dw_hbm, noise_ref, data_ref,
    out_ref, npot_ref, dpot_ref,
    nw_ref, dw_ref, nstage, dvm, dstage, wstage, nbuf, nmat, dcrit, dbuf, wbuf,
    pbuf, abuf, bbuf, rbuf, gall, lbuf, vbuf, plan, tbuf,
    load, ns, nr, cs, cr, ts, tr, ws, wr, sib_s, sib_r, as_, ar, bs, br,
    gs, gr, hs, hr, os_, or_,
):
    FQ = width // (Q * C)
    FS = X * FQ
    half = C // 2
    eps = 1.0 / math.sqrt(width)
    row = lax.axis_index("row")
    c = lax.axis_index("col")
    k = row % 2
    q = row // 2
    x = q % X
    yl = q // X
    z = c // YH
    yh = c % YH
    y = yh * YL + yl
    other = 1 - k

    def place(yl_, x_, k_):
        return (yl_ * X + x_) * 2 + k_

    sibling = (place(yl, x, other), c)

    def data_target(j):
        return (k * half + j) * 2 + c // half, q

    source_row = c * 2 + yl // 2
    to_self = jnp.logical_and(source_row == row, c // half == k)
    n_self = jnp.where(to_self, 1, 0).astype(jnp.int32)

    def finish():
        def sent(ref, sem):
            pltpu.make_async_copy(ref, ref, sem).wait()

        def sent_targets(ref, sem):
            @pl.when(to_self)
            def _():
                sent(ref.at[pl.ds(0, half - 1)], sem)

            @pl.when(jnp.logical_not(to_self))
            def _():
                sent(ref.at[pl.ds(0, half)], sem)

        sent_targets(dstage, cs)
        sent_targets(dbuf, ts)
        sent_targets(wbuf, ws)
        sent(nbuf.at[k, pl.ds(0, Q - 1)], ns)
        sent(nbuf.at[k], sib_s.at[0])
        sent(pbuf.at[pl.ds(0, Y - 1)], as_)
        sent(rbuf.at[pl.ds(0, Z - 1)], bs)
        sent(dbuf.at[pl.ds(0, half)], sib_s.at[1])
        sent(wbuf.at[pl.ds(0, half)], sib_s.at[2])
        sent(gall.at[k, x, pl.ds(0, Y - 1)], gs)
        sent(gall.at[k, pl.ds(0, X - 1)], hs)
        sent(gall.at[k], sib_s.at[3])
        sent(tbuf.at[pl.ds(0, Q - 1)], os_)
        sent(out_ref, or_)

    loads = [
        pltpu.make_async_copy(nw_hbm, nw_ref, load.at[0]),
        pltpu.make_async_copy(dw_hbm, dw_ref, load.at[1]),
        pltpu.make_async_copy(data_ref, dvm, load.at[2]),
    ] + [
        pltpu.make_async_copy(
            noise_ref.at[:, pl.ds(t * FS, FS)], nstage.at[t, :, pl.ds(0, FS)], load.at[3 + t]
        )
        for t in range(YL)
    ]

    barrier = pltpu.get_barrier_semaphore()

    def greet(device):
        pl.semaphore_signal(barrier, inc=1, device_id=device, device_id_type=MESH)

    def greet_source(j, carry):
        sc = k * half + j

        @pl.when(jnp.logical_or(source_row != row, sc != c))
        def _():
            greet((source_row, sc))

        return carry

    def greet_z(s, carry):
        greet((row, lax.rem(z + s, Z) * YH + yh))
        return carry

    def greet_y(t, carry):
        greet((place(t, x, k), z * YH + 1 - yh))
        return carry

    def greet_row(s, carry):
        greet((lax.rem(q + s, Q) * 2 + k, c))
        return carry

    lax.fori_loop(0, half, greet_source, 0)
    lax.fori_loop(1, Z, greet_z, 0)
    lax.fori_loop(0, YL, greet_y, 0)
    lax.fori_loop(1, Q, greet_row, 0)
    greet(sibling)
    for copy in loads:
        copy.start()

    for copy in loads:
        copy.wait()

    for j in range(2 * X):
        s, t = j // X, j % X
        dstage[j] = jnp.concatenate(
            [
                dvm[:, s * FS + f * FQ:s * FS + (f + 1) * FQ].astype(F32)[8 * t:8 * t + 8]
                for f in range(X)
            ],
            axis=0,
        ).astype(BF16)
    rows32 = lax.broadcasted_iota(jnp.int32, (32, LANES), 0)
    data_w = jnp.zeros((32, LANES), jnp.int32)
    for i in range(32):
        data_w = jnp.where(rows32 == i, dw_ref[i], data_w)
    wstage[...] = data_w.astype(F32).astype(BF16)

    rows8 = lax.broadcasted_iota(jnp.int32, (8, LANES), 0)
    lanes8 = lax.broadcasted_iota(jnp.int32, (8, LANES), 1)
    noise_w = jnp.zeros((8, LANES), jnp.int32)
    for i in range(8):
        noise_w = jnp.where(rows8 == i, nw_ref[i], noise_w)
    noise_w = noise_w.astype(F32)
    for t in range(YL):
        nf = nstage[t, :, 0:FS].astype(F32)
        sq = jnp.sum(nf * nf, axis=1, keepdims=True)
        hi = sq.astype(BF16).astype(F32)
        mid = (sq - hi).astype(BF16).astype(F32)
        lo = sq - hi - mid
        tail = jnp.where(lanes8 == 3, noise_w, 0.0)
        tail = jnp.where(lanes8 == 2, lo, tail)
        tail = jnp.where(lanes8 == 1, mid, tail)
        tail = jnp.where(lanes8 == 0, hi, tail)
        nstage[t, :, FS:FS + LANES] = tail.astype(BF16)

    pl.semaphore_wait(barrier, (Q - 1) + (Z - 1) + YL + 1 + half - n_self)

    def to_targets(src_of, dst, send, recv):
        def step(j, carry):
            device = data_target(j)
            is_self = jnp.logical_and(device[0] == row, device[1] == c)

            @pl.when(is_self)
            def _():
                pltpu.make_async_copy(src_of(j), dst, recv).start()

            @pl.when(jnp.logical_not(is_self))
            def _():
                pltpu.make_async_remote_copy(
                    src_of(j), dst, send, recv, device_id=device, device_id_type=MESH
                ).start()

            return carry

        lax.fori_loop(0, half, step, 0)

    to_targets(lambda j: dstage.at[j], dcrit.at[c % half], cs, cr)

    def send_noise(s, carry):
        t = lax.rem(q + s, Q)
        pltpu.make_async_remote_copy(
            nstage.at[t // X], nbuf.at[k, q], ns, nr,
            device_id=(t * 2 + k, c), device_id_type=MESH,
        ).start()
        return carry

    lax.fori_loop(1, Q, send_noise, 0)
    pltpu.make_async_copy(nstage.at[yl], nbuf.at[k, q], nr).start()

    to_targets(
        lambda j: data_ref.at[:, pl.ds(pl.multiple_of(j * FQ, FQ), FQ)], dbuf.at[c], ts, tr
    )
    to_targets(lambda j: wstage, wbuf.at[c], ws, wr)

    def arrived(ref, sem):
        pltpu.make_async_copy(ref, ref, sem).wait()

    def swap(ref, i):
        return pltpu.make_async_remote_copy(
            ref, ref, sib_s.at[i], sib_r.at[i], device_id=sibling, device_id_type=MESH
        )

    def noise_rows(core):
        for t in range(2):
            part = nbuf[core, t * (Q // 2):(t + 1) * (Q // 2)].astype(F32)
            nmat[core, t * 4 * Q:(t + 1) * 4 * Q, :] = part.reshape(4 * Q, FS + LANES).astype(BF16)

    arrived(nbuf.at[k], nr)
    noise_swap = swap(nbuf.at[k], 0)
    noise_swap.start()
    noise_rows(k)
    arrived(nbuf.at[other], sib_r.at[0])
    noise_rows(other)
    tail = nmat[:, :, FS:FS + LANES].reshape(16 * Q, LANES)
    pick_sq = jnp.where(lanes8 < 3, 1.0, 0.0).astype(BF16)
    pick_w = jnp.where(lanes8 == 3, 1.0, 0.0).astype(BF16)
    nsq = lax.dot_general(pick_sq, tail, NT, preferred_element_type=F32)[0:1, :]
    wa = lax.dot_general(pick_w, tail, NT, preferred_element_type=F32)[0:1, :]

    arrived(dcrit, cr)
    df = dcrit[...].astype(F32).reshape(half, X, 8, FQ)
    part = jnp.sum(
        jnp.sum(df * df, axis=1).reshape(half * 8, FQ), axis=1, keepdims=True
    ) + nsq
    dm = (df * -2.0)
    for f in range(X):
        part = part + lax.dot_general(
            dm[:, f].reshape(half * 8, FQ).astype(BF16),
            nmat[:, :, f * FQ:(f + 1) * FQ].reshape(16 * Q, FQ),
            NT, preferred_element_type=F32,
        )
    for h in range(2):
        pbuf[:, h] = part[:, h * LANES:(h + 1) * LANES].reshape(Y, 8, LANES)

    def y_peer(t):
        return place(t % YL, x, k), z * YH + t // YL

    def send_a(s, carry):
        t = lax.rem(y + s, Y)
        pltpu.make_async_remote_copy(
            pbuf.at[t], abuf.at[y], as_, ar, device_id=y_peer(t), device_id_type=MESH
        ).start()
        return carry

    lax.fori_loop(1, Y, send_a, 0)
    pltpu.make_async_copy(pbuf.at[y], abuf.at[y], ar).start()
    log_a = jnp.log(wa / jnp.sum(wa, axis=1, keepdims=True))
    log_a = [log_a[:, h * LANES:(h + 1) * LANES] for h in range(2)]
    arrived(abuf, ar)
    total = abuf[0]
    for j in range(1, Y):
        total = total + abuf[j]
    bbuf[...] = total

    def send_b(s, carry):
        t = lax.rem(z + s, Z)
        pltpu.make_async_remote_copy(
            bbuf, rbuf.at[z], bs, br, device_id=(row, t * YH + yh), device_id_type=MESH
        ).start()
        return carry

    lax.fori_loop(1, Z, send_b, 0)
    pltpu.make_async_copy(bbuf, rbuf.at[z], br).start()

    own_data = dbuf.at[pl.ds(k * half, half)]
    arrived(own_data, tr)
    data_swap = swap(own_data, 1)
    data_swap.start()
    own_w = wbuf.at[pl.ds(k * half, half)]
    arrived(own_w, wr)
    w_swap = swap(own_w, 2)
    w_swap.start()

    arrived(rbuf, br)
    total = rbuf[0]
    for j in range(1, Z):
        total = total + rbuf[j]
    gall[k, x, y] = total * (-1.0 / (width * eps))

    def send_g(s, carry):
        t = lax.rem(y + s, Y)
        pltpu.make_async_remote_copy(
            gall.at[k, x, y], gall.at[k, x, y], gs, gr,
            device_id=y_peer(t), device_id_type=MESH,
        ).start()
        return carry

    lax.fori_loop(1, Y, send_g, 0)

    arrived(wbuf.at[pl.ds(other * half, half)], sib_r.at[2])
    wb = wbuf[...].astype(F32)
    w_sum = jnp.sum(jnp.sum(wb, axis=0), axis=0, keepdims=True)
    log_b = jnp.log(wb / w_sum).reshape(2, half, X, 8, LANES)
    for t in range(X):
        lbuf[:, t] = log_b[:, :, t]

    arrived(gall.at[k, x, pl.ds(0, Y - 1)], gr)

    def send_h(s, carry):
        t = lax.rem(x + s, X)
        pltpu.make_async_remote_copy(
            gall.at[k, x], gall.at[k, x], hs, hr,
            device_id=(place(yl, t, k), c), device_id_type=MESH,
        ).start()
        return carry

    lax.fori_loop(1, X, send_h, 0)
    arrived(gall.at[k, pl.ds(0, X - 1)], hr)
    cost_swap = swap(gall.at[k], 3)
    cost_swap.start()
    arrived(gall.at[other], sib_r.at[3])

    def parts(i):
        return i // X, i % X

    def peak_step(i, peak):
        a, b = parts(i)
        return jnp.maximum(peak, jnp.max(gall[a, b], axis=0))

    peak = lax.fori_loop(0, 2 * X, peak_step, jnp.full((2, 8, LANES), -jnp.inf, F32))
    for rounds in range(HALVES // 2):
        top = jnp.max(peak, axis=1, keepdims=True)

        def noise_step(i, acc):
            a, b = parts(i)
            s = gall[a, b]
            if rounds:
                s = s + vbuf[a, b][:, None]
            return acc + jnp.sum(jnp.exp(s - top), axis=0)

        acc = lax.fori_loop(0, 2 * X, noise_step, jnp.zeros((2, 8, LANES), F32))
        lse = top + jnp.log(jnp.sum(acc, axis=1, keepdims=True))
        u = jnp.concatenate([(log_a[h] - lse[h])[None] for h in range(2)], axis=0)

        def data_step(i, peak):
            a, b = parts(i)
            s = gall[a, b]
            w = s + u
            m = jnp.max(jnp.max(w, axis=1), axis=2, keepdims=True)
            e = jnp.sum(jnp.sum(jnp.exp(w - m[:, None]), axis=1), axis=2, keepdims=True)
            v = lbuf[a, b] - (m + jnp.log(e))
            vbuf[a, b] = v
            return jnp.maximum(peak, jnp.max(s + v[:, None], axis=0))

        peak = lax.fori_loop(0, 2 * X, data_step, jnp.full((2, 8, LANES), -jnp.inf, F32))

    own_u = jnp.where(k == 0, u[0], u[1])
    for i in range(2 * X):
        a, b = parts(i)
        plan[a, :, b] = jnp.exp(gall[a, b, :, k] + own_u + vbuf[a, b])
    p = jnp.transpose(plan[...].reshape(C * 32, LANES), (1, 0))
    mass = jnp.sum(p, axis=1, keepdims=True)

    arrived(dbuf.at[pl.ds(other * half, half)], sib_r.at[1])
    value = jnp.dot(
        p.astype(BF16), dbuf[...].reshape(C * 32, FQ), preferred_element_type=F32
    ) / mass
    tbuf[...] = value.reshape(Q, 8, FQ).astype(BF16)

    def send_t(s, carry):
        t = lax.rem(q + s, Q)
        pltpu.make_async_remote_copy(
            tbuf.at[t], out_ref.at[q], os_, or_,
            device_id=(t * 2 + k, c), device_id_type=MESH,
        ).start()
        return carry

    lax.fori_loop(1, Q, send_t, 0)
    pltpu.make_async_copy(tbuf.at[q], out_ref.at[q], or_).start()

    mine = own_u[:, 0:8]
    for t in range(1, Q):
        mine = jnp.where(q == t, own_u[:, 8 * t:8 * t + 8], mine)
    npot_ref[...] = mine * eps
    lanes4 = lax.broadcasted_iota(jnp.int32, (X, 8, LANES), 2)
    index4 = lax.broadcasted_iota(jnp.int32, (X, 8, LANES), 0) * 8 + lax.broadcasted_iota(
        jnp.int32, (X, 8, LANES), 1
    )
    block = jnp.where(lanes4 == index4, vbuf[c // half, :, c % half], 0.0)
    block = jnp.sum(jnp.sum(block, axis=0), axis=0, keepdims=True)
    dpot_ref[...] = block[:, 0:32] * eps
    finish()


def per_device(noise, data, noise_weight, data_weight):
    width = noise.shape[1] * C
    FQ = width // (Q * C)
    FS = X * FQ
    vmem = pl.BlockSpec(memory_space=pltpu.VMEM)
    anywhere = pl.BlockSpec(memory_space=pl.ANY)
    dma = pltpu.SemaphoreType.DMA
    targets, noise_pot, data_pot = pl.pallas_call(
        functools.partial(kernel, width),
        out_shape=(
            jax.ShapeDtypeStruct((Q, 8, FQ), BF16),
            jax.ShapeDtypeStruct((1, 8), F32),
            jax.ShapeDtypeStruct((1, 32), F32),
        ),
        in_specs=[anywhere] * 4,
        out_specs=(anywhere, vmem, vmem),
        scratch_shapes=[
            pltpu.SMEM((8,), jnp.int32),
            pltpu.SMEM((32,), jnp.int32),
            pltpu.VMEM((YL, 8, FS + LANES), BF16),
            pltpu.VMEM((32, 2 * FS), BF16),
            pltpu.VMEM((2 * X, 32, FQ), BF16),
            pltpu.VMEM((32, LANES), BF16),
            pltpu.VMEM((2, Q, 8, FS + LANES), BF16),
            pltpu.VMEM((2, 8 * Q, FS + LANES), BF16),
            pltpu.VMEM((C // 2, 32, FQ), BF16),
            pltpu.VMEM((C, 32, FQ), BF16),
            pltpu.VMEM((C, 32, LANES), BF16),
            pltpu.VMEM((Y, 2, 8, LANES), F32),
            pltpu.VMEM((Y, 2, 8, LANES), F32),
            pltpu.VMEM((2, 8, LANES), F32),
            pltpu.VMEM((Z, 2, 8, LANES), F32),
            pltpu.VMEM((2, X, Y, 2, 8, LANES), F32),
            pltpu.VMEM((2, X, Y, 8, LANES), F32),
            pltpu.VMEM((2, X, Y, 8, LANES), F32),
            pltpu.VMEM((2, Y, X, 8, LANES), F32),
            pltpu.VMEM((Q, 8, FQ), BF16),
            dma((3 + YL,)),
        ] + [dma] * 8 + [dma((4,))] * 2 + [dma] * 10,
        compiler_params=pltpu.CompilerParams(
            collective_id=0, has_side_effects=True, vmem_limit_bytes=60 * 1024 * 1024
        ),
    )(noise_weight, data_weight, noise, data)
    targets = jnp.transpose(targets, (1, 0, 2)).reshape(8, Q * FQ)
    return (targets, noise_pot.reshape(8), data_pot.reshape(32))


def solution(mesh):
    placed = (P("row", "col"), P("col", "row"), P("row"), P("col"))
    return jax.shard_map(
        per_device,
        mesh=mesh,
        in_specs=placed,
        out_specs=(P("row", "col"), P("row"), P("col")),
        check_vma=False,
    )
```

```python
import functools
import math

import jax
import jax.numpy as jnp
from jax import lax
from jax.experimental import pallas as pl
from jax.experimental.pallas import tpu as pltpu
from jax.sharding import PartitionSpec as P

HALVES = 4
MESH = pl.DeviceIdType.MESH
F32 = jnp.float32
BF16 = jnp.bfloat16
LANES = 128
X, YL, Z, YH = 4, 4, 8, 2
Y = YH * YL
Q = YL * X
C = Z * YH
NT = (((1,), (1,)), ((), ()))


def kernel(
    width,
    nw_hbm, dw_hbm, noise_ref, data_ref,
    out_ref, npot_ref, dpot_ref,
    nw_ref, dw_ref, nstage, dvm, dstage, relay, wstage, nbuf, nmat, dcrit, tdata, dfull,
    wbuf, pbuf, abuf, bbuf, rbuf, gall, lbuf, vbuf, plan, tbuf,
    load, n1s, n1r, n2s, n2r, es, er, fs, fr, ts, tr, w1s, w1r, w2s, w2r, sib_s, sib_r,
    as_, ar, bs, br, gs, gr, hs, hr, os_, or_,
):
    FQ = width // (Q * C)
    FS = X * FQ
    eps = 1.0 / math.sqrt(width)
    row = lax.axis_index("row")
    c = lax.axis_index("col")
    k = row % 2
    q = row // 2
    x = q % X
    yl = q // X
    z = c // YH
    yh = c % YH
    y = yh * YL + yl
    other = 1 - k

    def place(yl_, x_, k_):
        return (yl_ * X + x_) * 2 + k_

    sibling = (place(yl, x, other), c)

    def relay_of(j):
        return place(2 * k + j // X, j % X, yh), z * YH + x % YH

    def relay_source(i):
        f = YH * i + yh
        return place(f // X, f % X, yl // 2), z * YH + k

    to_self = jnp.logical_and(jnp.logical_and(k == yl // 2, yh == k), x % YH == yh)
    n_self = jnp.where(to_self, 1, 0).astype(jnp.int32)

    def finish():
        def sent(ref, sem):
            pltpu.make_async_copy(ref, ref, sem).wait()

        @pl.when(to_self)
        def _():
            sent(dstage.at[pl.ds(0, 2 * X - 1)], es)

        @pl.when(jnp.logical_not(to_self))
        def _():
            sent(dstage, es)

        sent(relay.at[pl.ds(0, Z - 1)], fs)
        sent(nstage.at[pl.ds(0, YL - 1)], n1s)
        sent(nbuf.at[k, pl.ds(0, X - 1)], n2s)
        sent(nbuf.at[k], sib_s.at[0])
        sent(wbuf.at[pl.ds(0, Z - 1), 0], w1s)
        sent(wbuf.at[:, yh], w2s)
        sent(pbuf.at[pl.ds(0, Y - 1)], as_)
        sent(tdata.at[pl.ds(0, 2 * X - 1)], ts)
        sent(rbuf.at[pl.ds(0, Z - 1)], bs)
        sent(gall.at[k, x, pl.ds(0, Y - 1)], gs)
        sent(gall.at[k, pl.ds(0, X - 1)], hs)
        sent(gall.at[k], sib_s.at[1])
        sent(out_ref.at[pl.ds(0, Q - 1)], os_)
        sent(out_ref, or_)

    loads = [
        pltpu.make_async_copy(nw_hbm, nw_ref, load.at[0]),
        pltpu.make_async_copy(dw_hbm, dw_ref, load.at[1]),
        pltpu.make_async_copy(data_ref, dvm, load.at[2]),
    ] + [
        pltpu.make_async_copy(
            noise_ref.at[:, pl.ds(t * FS, FS)], nstage.at[t, :, pl.ds(0, FS)], load.at[3 + t]
        )
        for t in range(YL)
    ]

    barrier = pltpu.get_barrier_semaphore()

    def greet(device):
        pl.semaphore_signal(barrier, inc=1, device_id=device, device_id_type=MESH)

    def greet_source(i, carry):
        device = relay_source(i)

        @pl.when(jnp.logical_or(device[0] != row, device[1] != c))
        def _():
            greet(device)

        return carry

    def greet_core(t, carry):
        greet((place(yl, t, other), c))
        return carry

    def greet_z(s, carry):
        greet((row, lax.rem(z + s, Z) * YH + yh))
        return carry

    def greet_y(t, carry):
        greet((place(t, x, k), z * YH + 1 - yh))
        return carry

    def greet_row(s, carry):
        greet((lax.rem(q + s, Q) * 2 + k, c))
        return carry

    lax.fori_loop(0, Z, greet_source, 0)
    lax.fori_loop(1, Z, greet_z, 0)
    lax.fori_loop(0, YL, greet_y, 0)
    lax.fori_loop(1, Q, greet_row, 0)
    lax.fori_loop(0, X, greet_core, 0)
    for copy in loads:
        copy.start()

    for copy in loads:
        copy.wait()

    for j in range(2 * X):
        s, t = j // X, j % X
        for f in range(X):
            cut = dvm[:, s * FS + f * FQ:s * FS + (f + 1) * FQ].astype(F32)
            dstage[j, f] = cut[8 * t:8 * t + 8].astype(BF16)
    rows32 = lax.broadcasted_iota(jnp.int32, (32, LANES), 0)
    data_w = jnp.zeros((32, LANES), jnp.int32)
    for i in range(32):
        data_w = jnp.where(rows32 == i, dw_ref[i], data_w)
    wstage[...] = data_w.astype(F32).astype(BF16)

    rows8 = lax.broadcasted_iota(jnp.int32, (8, LANES), 0)
    lanes8 = lax.broadcasted_iota(jnp.int32, (8, LANES), 1)
    noise_w = jnp.zeros((8, LANES), jnp.int32)
    for i in range(8):
        noise_w = jnp.where(rows8 == i, nw_ref[i], noise_w)
    noise_w = noise_w.astype(F32)
    for t in range(YL):
        nf = nstage[t, :, 0:FS].astype(F32)
        sq = jnp.sum(nf * nf, axis=1, keepdims=True)
        hi = sq.astype(BF16).astype(F32)
        mid = (sq - hi).astype(BF16).astype(F32)
        lo = sq - hi - mid
        tail = jnp.where(lanes8 == 3, noise_w, 0.0)
        tail = jnp.where(lanes8 == 2, lo, tail)
        tail = jnp.where(lanes8 == 1, mid, tail)
        tail = jnp.where(lanes8 == 0, hi, tail)
        nstage[t, :, FS:FS + LANES] = tail.astype(BF16)

    pl.semaphore_wait(barrier, (Q - 1) + X + (Z - 1) + YL + 2 * X - n_self)

    def send_data(j, carry):
        device = relay_of(j)
        is_self = jnp.logical_and(device[0] == row, device[1] == c)
        slot = q // YH

        @pl.when(is_self)
        def _():
            pltpu.make_async_copy(dstage.at[j], relay.at[slot], er.at[slot]).start()

        @pl.when(jnp.logical_not(is_self))
        def _():
            pltpu.make_async_remote_copy(
                dstage.at[j], relay.at[slot], es, er.at[slot],
                device_id=device, device_id_type=MESH,
            ).start()

        return carry

    lax.fori_loop(0, 2 * X, send_data, 0)

    def send_noise_y(s, carry):
        t = lax.rem(yl + s, YL)
        pltpu.make_async_remote_copy(
            nstage.at[t], nbuf.at[k, x, yl], n1s, n1r,
            device_id=(place(t, x, k), c), device_id_type=MESH,
        ).start()
        return carry

    lax.fori_loop(1, YL, send_noise_y, 0)
    pltpu.make_async_copy(nstage.at[yl], nbuf.at[k, x, yl], n1r).start()

    def send_w(s, carry):
        t = lax.rem(z + s, Z)
        pltpu.make_async_remote_copy(
            wstage, wbuf.at[z, yh], w1s, w1r,
            device_id=(row, t * YH + yh), device_id_type=MESH,
        ).start()
        return carry

    lax.fori_loop(1, Z, send_w, 0)
    pltpu.make_async_copy(wstage, wbuf.at[z, yh], w1r).start()

    def arrived(ref, sem):
        pltpu.make_async_copy(ref, ref, sem).wait()

    def swap(ref, i):
        return pltpu.make_async_remote_copy(
            ref, ref, sib_s.at[i], sib_r.at[i], device_id=sibling, device_id_type=MESH
        )

    arrived(nbuf.at[k, x], n1r)

    def send_noise_x(s, carry):
        t = lax.rem(x + s, X)
        pltpu.make_async_remote_copy(
            nbuf.at[k, x], nbuf.at[k, x], n2s, n2r,
            device_id=(place(yl, t, k), c), device_id_type=MESH,
        ).start()
        return carry

    lax.fori_loop(1, X, send_noise_x, 0)

    def hand_on(i, carry):
        t = lax.rem(YH * yl + i, Z)
        arrived(relay.at[t], er.at[t])

        @pl.when(t == z)
        def _():
            pltpu.make_async_copy(relay.at[t], dcrit.at[z], fr).start()

        @pl.when(t != z)
        def _():
            pltpu.make_async_remote_copy(
                relay.at[t], dcrit.at[z], fs, fr,
                device_id=(row, t * YH + yh), device_id_type=MESH,
            ).start()

        return carry

    lax.fori_loop(0, Z, hand_on, 0)

    def noise_rows(core):
        for t in range(2):
            part = nbuf[core, 2 * t:2 * t + 2].astype(F32)
            nmat[core, t * 4 * Q:(t + 1) * 4 * Q, :] = part.reshape(4 * Q, FS + LANES).astype(BF16)

    arrived(nbuf.at[k, pl.ds(0, X - 1)], n2r)
    noise_swap = swap(nbuf.at[k], 0)
    noise_swap.start()
    noise_rows(k)
    arrived(nbuf.at[other], sib_r.at[0])
    noise_rows(other)
    tail = nmat[:, :, FS:FS + LANES].reshape(16 * Q, LANES)
    pick_sq = jnp.where(lanes8 < 3, 1.0, 0.0).astype(BF16)
    pick_w = jnp.where(lanes8 == 3, 1.0, 0.0).astype(BF16)
    nsq = lax.dot_general(pick_sq, tail, NT, preferred_element_type=F32)[0:1, :]
    wa = lax.dot_general(pick_w, tail, NT, preferred_element_type=F32)[0:1, :]

    arrived(wbuf.at[:, yh], w1r)
    pltpu.make_async_remote_copy(
        wbuf.at[:, yh], wbuf.at[:, yh], w2s, w2r,
        device_id=(row, z * YH + 1 - yh), device_id_type=MESH,
    ).start()

    arrived(dcrit, fr)
    df = dcrit[...].astype(F32)
    part = jnp.sum(
        jnp.sum(df * df, axis=1).reshape(Z * 8, FQ), axis=1, keepdims=True
    ) + nsq
    dm = (df * -2.0)
    for f in range(X):
        part = part + lax.dot_general(
            dm[:, f].reshape(Z * 8, FQ).astype(BF16),
            nmat[:, :, f * FQ:(f + 1) * FQ].reshape(16 * Q, FQ),
            NT, preferred_element_type=F32,
        )
    for h in range(2):
        pbuf[:, h] = part[:, h * LANES:(h + 1) * LANES].reshape(Y, 8, LANES)

    def y_peer(t):
        return place(t % YL, x, k), z * YH + t // YL

    def send_a(s, carry):
        t = lax.rem(y + s, Y)
        pltpu.make_async_remote_copy(
            pbuf.at[t], abuf.at[y], as_, ar, device_id=y_peer(t), device_id_type=MESH
        ).start()
        return carry

    lax.fori_loop(1, Y, send_a, 0)
    pltpu.make_async_copy(pbuf.at[y], abuf.at[y], ar).start()

    def send_features(j, carry):
        t, core = lax.rem(x + j // 2, X), lax.rem(k + j, 2)
        pltpu.make_async_remote_copy(
            dcrit.at[:, t], tdata.at[:, k * X + x], ts, tr,
            device_id=(place(yl, t, core), c), device_id_type=MESH,
        ).start()
        return carry

    lax.fori_loop(1, 2 * X, send_features, 0)
    pltpu.make_async_copy(dcrit.at[:, x], tdata.at[:, k * X + x], tr).start()

    log_a = jnp.log(wa / jnp.sum(wa, axis=1, keepdims=True))
    log_a = [log_a[:, h * LANES:(h + 1) * LANES] for h in range(2)]
    arrived(abuf, ar)
    total = abuf[0]
    for j in range(1, Y):
        total = total + abuf[j]
    bbuf[...] = total

    def send_b(s, carry):
        t = lax.rem(z + s, Z)
        pltpu.make_async_remote_copy(
            bbuf, rbuf.at[z], bs, br, device_id=(row, t * YH + yh), device_id_type=MESH
        ).start()
        return carry

    lax.fori_loop(1, Z, send_b, 0)
    pltpu.make_async_copy(bbuf, rbuf.at[z], br).start()

    arrived(rbuf, br)
    total = rbuf[0]
    for j in range(1, Z):
        total = total + rbuf[j]
    gall[k, x, y] = total * (-1.0 / (width * eps))

    def send_g(s, carry):
        t = lax.rem(y + s, Y)
        pltpu.make_async_remote_copy(
            gall.at[k, x, y], gall.at[k, x, y], gs, gr,
            device_id=y_peer(t), device_id_type=MESH,
        ).start()
        return carry

    lax.fori_loop(1, Y, send_g, 0)

    arrived(wbuf.at[:, 1 - yh], w2r)
    wb = wbuf[...].astype(F32).reshape(Z, YH, X, 8, LANES)
    w_sum = jnp.sum(jnp.sum(wb, axis=(0, 1, 2)), axis=0, keepdims=True)
    log_b = jnp.log(wb / w_sum)
    for a in range(YH):
        for b in range(X):
            lbuf[a, b] = log_b[:, a, b]
    arrived(tdata, tr)
    for t in range(Z):
        dfull[t * 64:(t + 1) * 64, :] = tdata[t].astype(F32).reshape(64, FQ).astype(BF16)

    arrived(gall.at[k, x, pl.ds(0, Y - 1)], gr)

    def send_h(s, carry):
        t = lax.rem(x + s, X)
        pltpu.make_async_remote_copy(
            gall.at[k, x], gall.at[k, x], hs, hr,
            device_id=(place(yl, t, k), c), device_id_type=MESH,
        ).start()
        return carry

    lax.fori_loop(1, X, send_h, 0)
    arrived(gall.at[k, pl.ds(0, X - 1)], hr)
    cost_swap = swap(gall.at[k], 1)
    cost_swap.start()
    arrived(gall.at[other], sib_r.at[1])

    def parts(i):
        return i // X, i % X

    def peak_step(i, peak):
        a, b = parts(i)
        return jnp.maximum(peak, jnp.max(gall[a, b], axis=0))

    peak = lax.fori_loop(0, 2 * X, peak_step, jnp.full((2, 8, LANES), -jnp.inf, F32))
    for rounds in range(HALVES // 2):
        top = jnp.max(peak, axis=1, keepdims=True)

        def noise_step(i, acc):
            a, b = parts(i)
            s = gall[a, b]
            if rounds:
                s = s + vbuf[a, b][:, None]
            return acc + jnp.sum(jnp.exp(s - top), axis=0)

        acc = lax.fori_loop(0, 2 * X, noise_step, jnp.zeros((2, 8, LANES), F32))
        lse = top + jnp.log(jnp.sum(acc, axis=1, keepdims=True))
        u = jnp.concatenate([(log_a[h] - lse[h])[None] for h in range(2)], axis=0)

        def data_step(i, peak):
            a, b = parts(i)
            s = gall[a, b]
            w = s + u
            m = jnp.max(jnp.max(w, axis=1), axis=2, keepdims=True)
            e = jnp.sum(jnp.sum(jnp.exp(w - m[:, None]), axis=1), axis=2, keepdims=True)
            v = lbuf[a, b] - (m + jnp.log(e))
            vbuf[a, b] = v
            return jnp.maximum(peak, jnp.max(s + v[:, None], axis=0))

        peak = lax.fori_loop(0, 2 * X, data_step, jnp.full((2, 8, LANES), -jnp.inf, F32))

    own_u = jnp.where(k == 0, u[0], u[1])
    for i in range(2 * X):
        a, b = parts(i)
        plan[:, a, b] = jnp.exp(gall[a, b, :, k] + own_u + vbuf[a, b])
    p = jnp.transpose(plan[...].reshape(C * 32, LANES), (1, 0))
    mass = jnp.sum(p, axis=1, keepdims=True)

    value = jnp.dot(
        p.astype(BF16), dfull[...], preferred_element_type=F32
    ) / mass
    tbuf[...] = value.reshape(X, YL, 8, FQ).astype(BF16)

    def send_t(s, carry):
        t = lax.rem(q + s, Q)
        pltpu.make_async_remote_copy(
            tbuf.at[t % X, t // X], out_ref.at[q], os_, or_,
            device_id=(t * 2 + k, c), device_id_type=MESH,
        ).start()
        return carry

    lax.fori_loop(1, Q, send_t, 0)
    pltpu.make_async_copy(tbuf.at[x, yl], out_ref.at[q], or_).start()

    mine = own_u[:, 0:8]
    for t in range(1, Q):
        mine = jnp.where(x * YL + yl == t, own_u[:, 8 * t:8 * t + 8], mine)
    npot_ref[...] = mine * eps
    lanes4 = lax.broadcasted_iota(jnp.int32, (X, 8, LANES), 2)
    index4 = lax.broadcasted_iota(jnp.int32, (X, 8, LANES), 0) * 8 + lax.broadcasted_iota(
        jnp.int32, (X, 8, LANES), 1
    )
    block = jnp.where(lanes4 == index4, vbuf[yh, :, z], 0.0)
    block = jnp.sum(jnp.sum(block, axis=0), axis=0, keepdims=True)
    dpot_ref[...] = block[:, 0:32] * eps
    finish()


def per_device(noise, data, noise_weight, data_weight):
    width = noise.shape[1] * C
    FQ = width // (Q * C)
    FS = X * FQ
    vmem = pl.BlockSpec(memory_space=pltpu.VMEM)
    anywhere = pl.BlockSpec(memory_space=pl.ANY)
    dma = pltpu.SemaphoreType.DMA
    targets, noise_pot, data_pot = pl.pallas_call(
        functools.partial(kernel, width),
        out_shape=(
            jax.ShapeDtypeStruct((Q, 8, FQ), BF16),
            jax.ShapeDtypeStruct((1, 8), F32),
            jax.ShapeDtypeStruct((1, 32), F32),
        ),
        in_specs=[anywhere] * 4,
        out_specs=(anywhere, vmem, vmem),
        scratch_shapes=[
            pltpu.SMEM((8,), jnp.int32),
            pltpu.SMEM((32,), jnp.int32),
            pltpu.VMEM((YL, 8, FS + LANES), BF16),
            pltpu.VMEM((32, 2 * FS), BF16),
            pltpu.VMEM((2 * X, X, 8, FQ), BF16),
            pltpu.VMEM((Z, X, 8, FQ), BF16),
            pltpu.VMEM((32, LANES), BF16),
            pltpu.VMEM((2, X, YL, 8, FS + LANES), BF16),
            pltpu.VMEM((2, 8 * Q, FS + LANES), BF16),
            pltpu.VMEM((Z, X, 8, FQ), BF16),
            pltpu.VMEM((Z, 2 * X, 8, FQ), BF16),
            pltpu.VMEM((C * 32, FQ), BF16),
            pltpu.VMEM((Z, YH, 32, LANES), BF16),
            pltpu.VMEM((Y, 2, 8, LANES), F32),
            pltpu.VMEM((Y, 2, 8, LANES), F32),
            pltpu.VMEM((2, 8, LANES), F32),
            pltpu.VMEM((Z, 2, 8, LANES), F32),
            pltpu.VMEM((2, X, Y, 2, 8, LANES), F32),
            pltpu.VMEM((2, X, Y, 8, LANES), F32),
            pltpu.VMEM((2, X, Y, 8, LANES), F32),
            pltpu.VMEM((Z, 2, X, 8, LANES), F32),
            pltpu.VMEM((X, YL, 8, FQ), BF16),
            dma((3 + YL,)),
        ] + [dma] * 5 + [dma((Z,))] + [dma] * 8 + [dma((2,))] * 2 + [dma] * 10,
        compiler_params=pltpu.CompilerParams(
            collective_id=0, has_side_effects=True, vmem_limit_bytes=60 * 1024 * 1024
        ),
    )(noise_weight, data_weight, noise, data)
    targets = jnp.transpose(targets, (1, 0, 2)).reshape(8, Q * FQ)
    return (targets, noise_pot.reshape(8), data_pot.reshape(32))


def solution(mesh):
    placed = (P("row", "col"), P("col", "row"), P("row"), P("col"))
    return jax.shard_map(
        per_device,
        mesh=mesh,
        in_specs=placed,
        out_specs=(P("row", "col"), P("row"), P("col")),
        check_vma=False,
    )
```

```python
import functools
import math

import jax
import jax.numpy as jnp
from jax import lax
from jax.experimental import pallas as pl
from jax.experimental.pallas import tpu as pltpu
from jax.sharding import PartitionSpec as P

HALVES = 4
MESH = pl.DeviceIdType.MESH
F32 = jnp.float32
BF16 = jnp.bfloat16
LANES = 128
X, YL, Z, YH = 4, 4, 8, 2
Y = YH * YL
Q = YL * X
C = Z * YH
NT = (((1,), (1,)), ((), ()))


def kernel(
    width,
    nw_hbm, dw_hbm, noise_ref, data_ref,
    out_ref, npot_ref, dpot_ref,
    nw_ref, dw_ref, nstage, dvm, dstage, relay, wstage, nbuf, nmat, dcrit, tdata, dfull,
    wbuf, pbuf, abuf, bbuf, rbuf, gall, lbuf, vbuf, plan, tbuf,
    load, n1s, n1r, n2s, n2r, es, er, fs, fr, ts, tr, w1s, w1r, w2s, w2r, sib_s, sib_r,
    as_, ar, bs, br, gs, gr, hs, hr, os_, or_,
):
    FQ = width // (Q * C)
    FS = X * FQ
    eps = 1.0 / math.sqrt(width)
    row = lax.axis_index("row")
    c = lax.axis_index("col")
    k = row % 2
    q = row // 2
    x = q % X
    yl = q // X
    z = c // YH
    yh = c % YH
    y = yh * YL + yl
    other = 1 - k

    def place(yl_, x_, k_):
        return (yl_ * X + x_) * 2 + k_

    sibling = (place(yl, x, other), c)

    def relay_of(j):
        return place(2 * k + j // X, j % X, yh), z * YH + x % YH

    def relay_source(i):
        f = YH * i + yh
        return place(f // X, f % X, yl // 2), z * YH + k

    to_self = jnp.logical_and(jnp.logical_and(k == yl // 2, yh == k), x % YH == yh)
    n_self = jnp.where(to_self, 1, 0).astype(jnp.int32)

    def finish():
        def sent(ref, sem):
            pltpu.make_async_copy(ref, ref, sem).wait()

        @pl.when(to_self)
        def _():
            sent(dstage.at[pl.ds(0, 2 * X - 1)], es)

        @pl.when(jnp.logical_not(to_self))
        def _():
            sent(dstage, es)

        sent(relay.at[pl.ds(0, Z - 1)], fs)
        sent(nstage.at[pl.ds(0, YL - 1)], n1s)
        sent(nbuf.at[k, pl.ds(0, X - 1)], n2s)
        sent(nbuf.at[k], sib_s.at[0])
        sent(wbuf.at[pl.ds(0, Z - 1), 0], w1s)
        sent(wbuf.at[:, yh], w2s)
        sent(pbuf.at[pl.ds(0, Y - 1)], as_)
        sent(tdata.at[pl.ds(0, 2 * X - 1)], ts)
        sent(rbuf.at[pl.ds(0, Z - 1)], bs)
        sent(gall.at[k, x, pl.ds(0, Y - 1)], gs)
        sent(gall.at[k, pl.ds(0, X - 1)], hs)
        sent(gall.at[k], sib_s.at[1])
        sent(out_ref.at[pl.ds(0, Q - 1)], os_)
        sent(out_ref, or_)

    loads = [
        pltpu.make_async_copy(nw_hbm, nw_ref, load.at[0]),
        pltpu.make_async_copy(dw_hbm, dw_ref, load.at[1]),
        pltpu.make_async_copy(data_ref, dvm, load.at[2]),
    ] + [
        pltpu.make_async_copy(
            noise_ref.at[:, pl.ds(t * FS, FS)], nstage.at[t, :, pl.ds(0, FS)], load.at[3 + t]
        )
        for t in range(YL)
    ]

    barrier = pltpu.get_barrier_semaphore()

    def greet(device):
        pl.semaphore_signal(barrier, inc=1, device_id=device, device_id_type=MESH)

    def greet_source(i, carry):
        device = relay_source(i)

        @pl.when(jnp.logical_or(device[0] != row, device[1] != c))
        def _():
            greet(device)

        return carry

    def greet_core(t, carry):
        greet((place(yl, t, other), c))
        return carry

    def greet_z(s, carry):
        greet((row, lax.rem(z + s, Z) * YH + yh))
        return carry

    def greet_y(t, carry):
        greet((place(t, x, k), z * YH + 1 - yh))
        return carry

    def greet_row(s, carry):
        greet((lax.rem(q + s, Q) * 2 + k, c))
        return carry

    lax.fori_loop(0, Z, greet_source, 0)
    lax.fori_loop(1, Z, greet_z, 0)
    lax.fori_loop(0, YL, greet_y, 0)
    lax.fori_loop(1, Q, greet_row, 0)
    lax.fori_loop(0, X, greet_core, 0)
    for copy in loads:
        copy.start()

    for copy in loads:
        copy.wait()

    for j in range(2 * X):
        s, t = j // X, j % X
        for f in range(X):
            cut = dvm[:, s * FS + f * FQ:s * FS + (f + 1) * FQ].astype(F32)
            dstage[j, f] = cut[8 * t:8 * t + 8].astype(BF16)
    lanes1 = lax.broadcasted_iota(jnp.int32, (1, LANES), 1)
    data_w = jnp.zeros((1, LANES), jnp.int32)
    for i in range(32):
        data_w = jnp.where(lanes1 == i, dw_ref[i], data_w)
    wstage[...] = data_w.astype(F32)

    rows8 = lax.broadcasted_iota(jnp.int32, (8, LANES), 0)
    lanes8 = lax.broadcasted_iota(jnp.int32, (8, LANES), 1)
    noise_w = jnp.zeros((8, LANES), jnp.int32)
    for i in range(8):
        noise_w = jnp.where(rows8 == i, nw_ref[i], noise_w)
    noise_w = noise_w.astype(F32)
    for t in range(YL):
        nf = nstage[t, :, 0:FS].astype(F32)
        sq = jnp.sum(nf * nf, axis=1, keepdims=True)
        hi = sq.astype(BF16).astype(F32)
        mid = (sq - hi).astype(BF16).astype(F32)
        lo = sq - hi - mid
        tail = jnp.where(lanes8 == 3, noise_w, 0.0)
        tail = jnp.where(lanes8 == 2, lo, tail)
        tail = jnp.where(lanes8 == 1, mid, tail)
        tail = jnp.where(lanes8 == 0, hi, tail)
        nstage[t, :, FS:FS + LANES] = tail.astype(BF16)

    pl.semaphore_wait(barrier, (Q - 1) + X + (Z - 1) + YL + 2 * X - n_self)

    def send_data(j, carry):
        device = relay_of(j)
        is_self = jnp.logical_and(device[0] == row, device[1] == c)
        slot = q // YH

        @pl.when(is_self)
        def _():
            pltpu.make_async_copy(dstage.at[j], relay.at[slot], er.at[slot]).start()

        @pl.when(jnp.logical_not(is_self))
        def _():
            pltpu.make_async_remote_copy(
                dstage.at[j], relay.at[slot], es, er.at[slot],
                device_id=device, device_id_type=MESH,
            ).start()

        return carry

    lax.fori_loop(0, 2 * X, send_data, 0)

    def send_noise_y(s, carry):
        t = lax.rem(yl + s, YL)
        pltpu.make_async_remote_copy(
            nstage.at[t], nbuf.at[k, x, yl], n1s, n1r,
            device_id=(place(t, x, k), c), device_id_type=MESH,
        ).start()
        return carry

    lax.fori_loop(1, YL, send_noise_y, 0)
    pltpu.make_async_copy(nstage.at[yl], nbuf.at[k, x, yl], n1r).start()

    def send_w(s, carry):
        t = lax.rem(z + s, Z)
        pltpu.make_async_remote_copy(
            wstage, wbuf.at[z, yh], w1s, w1r,
            device_id=(row, t * YH + yh), device_id_type=MESH,
        ).start()
        return carry

    lax.fori_loop(1, Z, send_w, 0)
    pltpu.make_async_copy(wstage, wbuf.at[z, yh], w1r).start()

    def arrived(ref, sem):
        pltpu.make_async_copy(ref, ref, sem).wait()

    def swap(ref, i):
        return pltpu.make_async_remote_copy(
            ref, ref, sib_s.at[i], sib_r.at[i], device_id=sibling, device_id_type=MESH
        )

    arrived(nbuf.at[k, x], n1r)

    def send_noise_x(s, carry):
        t = lax.rem(x + s, X)
        pltpu.make_async_remote_copy(
            nbuf.at[k, x], nbuf.at[k, x], n2s, n2r,
            device_id=(place(yl, t, k), c), device_id_type=MESH,
        ).start()
        return carry

    lax.fori_loop(1, X, send_noise_x, 0)

    def hand_on(i, carry):
        t = lax.rem(YH * yl + i, Z)
        arrived(relay.at[t], er.at[t])

        @pl.when(t == z)
        def _():
            pltpu.make_async_copy(relay.at[t], dcrit.at[z], fr).start()

        @pl.when(t != z)
        def _():
            pltpu.make_async_remote_copy(
                relay.at[t], dcrit.at[z], fs, fr,
                device_id=(row, t * YH + yh), device_id_type=MESH,
            ).start()

        return carry

    lax.fori_loop(0, Z, hand_on, 0)

    def noise_rows(core):
        for t in range(2):
            part = nbuf[core, 2 * t:2 * t + 2].astype(F32)
            nmat[core, t * 4 * Q:(t + 1) * 4 * Q, :] = part.reshape(4 * Q, FS + LANES).astype(BF16)

    arrived(nbuf.at[k, pl.ds(0, X - 1)], n2r)
    noise_swap = swap(nbuf.at[k], 0)
    noise_swap.start()
    noise_rows(k)
    arrived(nbuf.at[other], sib_r.at[0])
    noise_rows(other)
    tail = nmat[:, :, FS:FS + LANES].reshape(16 * Q, LANES)
    pick_sq = jnp.where(lanes8 < 3, 1.0, 0.0).astype(BF16)
    pick_w = jnp.where(lanes8 == 3, 1.0, 0.0).astype(BF16)
    nsq = lax.dot_general(pick_sq, tail, NT, preferred_element_type=F32)[0:1, :]
    wa = lax.dot_general(pick_w, tail, NT, preferred_element_type=F32)[0:1, :]

    arrived(wbuf.at[:, yh], w1r)
    pltpu.make_async_remote_copy(
        wbuf.at[:, yh], wbuf.at[:, yh], w2s, w2r,
        device_id=(row, z * YH + 1 - yh), device_id_type=MESH,
    ).start()

    arrived(dcrit, fr)
    df = dcrit[...].astype(F32)
    part = jnp.sum(
        jnp.sum(df * df, axis=1).reshape(Z * 8, FQ), axis=1, keepdims=True
    ) + nsq
    dm = (df * -2.0)
    for f in range(X):
        part = part + lax.dot_general(
            dm[:, f].reshape(Z * 8, FQ).astype(BF16),
            nmat[:, :, f * FQ:(f + 1) * FQ].reshape(16 * Q, FQ),
            NT, preferred_element_type=F32,
        )
    for h in range(2):
        pbuf[:, h] = part[:, h * LANES:(h + 1) * LANES].reshape(Y, 8, LANES)

    def y_peer(t):
        return place(t % YL, x, k), z * YH + t // YL

    def send_a(s, carry):
        t = lax.rem(y + s, Y)
        pltpu.make_async_remote_copy(
            pbuf.at[t], abuf.at[y], as_, ar, device_id=y_peer(t), device_id_type=MESH
        ).start()
        return carry

    lax.fori_loop(1, Y, send_a, 0)
    pltpu.make_async_copy(pbuf.at[y], abuf.at[y], ar).start()

    def send_features(j, carry):
        t, core = lax.rem(x + j // 2, X), lax.rem(k + j, 2)
        pltpu.make_async_remote_copy(
            dcrit.at[:, t], tdata.at[:, k * X + x], ts, tr,
            device_id=(place(yl, t, core), c), device_id_type=MESH,
        ).start()
        return carry

    lax.fori_loop(1, 2 * X, send_features, 0)
    pltpu.make_async_copy(dcrit.at[:, x], tdata.at[:, k * X + x], tr).start()

    log_a = jnp.log(wa / jnp.sum(wa, axis=1, keepdims=True))
    log_a = [log_a[:, h * LANES:(h + 1) * LANES] for h in range(2)]
    arrived(abuf, ar)
    total = abuf[0]
    for j in range(1, Y):
        total = total + abuf[j]
    bbuf[...] = total

    def send_b(s, carry):
        t = lax.rem(z + s, Z)
        pltpu.make_async_remote_copy(
            bbuf, rbuf.at[z], bs, br, device_id=(row, t * YH + yh), device_id_type=MESH
        ).start()
        return carry

    lax.fori_loop(1, Z, send_b, 0)
    pltpu.make_async_copy(bbuf, rbuf.at[z], br).start()

    arrived(rbuf, br)
    total = rbuf[0]
    for j in range(1, Z):
        total = total + rbuf[j]
    gall[k, x, y] = total * (-1.0 / (width * eps))

    def send_g(s, carry):
        t = lax.rem(y + s, Y)
        pltpu.make_async_remote_copy(
            gall.at[k, x, y], gall.at[k, x, y], gs, gr.at[y],
            device_id=y_peer(t), device_id_type=MESH,
        ).start()
        return carry

    lax.fori_loop(1, Y, send_g, 0)

    def send_x(piece):
        for s in range(1, X):
            t = lax.rem(x + s, X)
            pltpu.make_async_remote_copy(
                gall.at[k, x, piece], gall.at[k, x, piece], hs, hr.at[x],
                device_id=(place(yl, t, k), c), device_id_type=MESH,
            ).start()

    send_x(y)

    arrived(wbuf.at[:, 1 - yh], w2r)
    wb = wbuf[...].reshape(C, 1, LANES)
    w_sum = jnp.sum(jnp.sum(wb, axis=0), axis=1, keepdims=True)
    spot = lax.broadcasted_iota(jnp.int32, (C, 32, LANES), 1) == lax.broadcasted_iota(
        jnp.int32, (C, 32, LANES), 2
    )
    wb = jnp.where(spot, wb, 0.0).reshape(C * 32, LANES).astype(BF16)
    wb = jnp.dot(wb, jnp.ones((LANES, LANES), BF16), preferred_element_type=F32)
    log_b = jnp.log(wb / w_sum).reshape(Z, YH, X, 8, LANES)
    for a in range(YH):
        for b in range(X):
            lbuf[a, b] = log_b[:, a, b]
    arrived(tdata, tr)
    for t in range(Z):
        dfull[t * 64:(t + 1) * 64, :] = tdata[t].astype(F32).reshape(64, FQ).astype(BF16)

    def gather_y(i, carry):
        d = (i + 1) // 2
        t = lax.rem(y + jnp.where(i % 2 == 1, d, Y - d), Y)
        arrived(gall.at[k, x, t], gr.at[t])
        send_x(t)
        return carry

    lax.fori_loop(1, Y, gather_y, 0)

    def send_core(t):
        pltpu.make_async_remote_copy(
            gall.at[k, t], gall.at[k, t], sib_s.at[1], sib_r.at[1],
            device_id=sibling, device_id_type=MESH,
        ).start()

    send_core(x)

    def gather_x(s, carry):
        t = lax.rem(x + jnp.where(s == 2, 3, jnp.where(s == 3, 2, 1)), X)
        arrived(gall.at[k, t], hr.at[t])
        send_core(t)
        return carry

    lax.fori_loop(1, X, gather_x, 0)
    arrived(gall.at[other], sib_r.at[1])

    def parts(i):
        return i // X, i % X

    def peak_step(i, peak):
        a, b = parts(i)
        return jnp.maximum(peak, jnp.max(gall[a, b], axis=0))

    peak = lax.fori_loop(0, 2 * X, peak_step, jnp.full((2, 8, LANES), -jnp.inf, F32))
    for rounds in range(HALVES // 2):
        top = jnp.max(peak, axis=1, keepdims=True)

        def noise_step(i, acc):
            a, b = parts(i)
            s = gall[a, b]
            if rounds:
                s = s + vbuf[a, b][:, None]
            return acc + jnp.sum(jnp.exp(s - top), axis=0)

        acc = lax.fori_loop(0, 2 * X, noise_step, jnp.zeros((2, 8, LANES), F32))
        lse = top + jnp.log(jnp.sum(acc, axis=1, keepdims=True))
        u = jnp.concatenate([(log_a[h] - lse[h])[None] for h in range(2)], axis=0)

        def data_step(i, peak):
            a, b = parts(i)
            s = gall[a, b]
            w = s + u
            m = jnp.max(jnp.max(w, axis=1), axis=2, keepdims=True)
            e = jnp.sum(jnp.sum(jnp.exp(w - m[:, None]), axis=1), axis=2, keepdims=True)
            v = lbuf[a, b] - (m + jnp.log(e))
            vbuf[a, b] = v
            return jnp.maximum(peak, jnp.max(s + v[:, None], axis=0))

        peak = lax.fori_loop(0, 2 * X, data_step, jnp.full((2, 8, LANES), -jnp.inf, F32))

    own_u = jnp.where(k == 0, u[0], u[1])
    for i in range(2 * X):
        a, b = parts(i)
        plan[:, a, b] = jnp.exp(gall[a, b, :, k] + own_u + vbuf[a, b])
    p = jnp.transpose(plan[...].reshape(C * 32, LANES), (1, 0))
    mass = jnp.sum(p, axis=1, keepdims=True)

    value = jnp.dot(
        p.astype(BF16), dfull[...], preferred_element_type=F32
    ) / mass
    tbuf[...] = value.reshape(X, YL, 8, FQ).astype(BF16)

    def send_t(s, carry):
        t = lax.rem(q + s, Q)
        pltpu.make_async_remote_copy(
            tbuf.at[t % X, t // X], out_ref.at[q], os_, or_,
            device_id=(t * 2 + k, c), device_id_type=MESH,
        ).start()
        return carry

    lax.fori_loop(1, Q, send_t, 0)
    pltpu.make_async_copy(tbuf.at[x, yl], out_ref.at[q], or_).start()

    mine = own_u[:, 0:8]
    for t in range(1, Q):
        mine = jnp.where(x * YL + yl == t, own_u[:, 8 * t:8 * t + 8], mine)
    npot_ref[...] = mine * eps
    lanes4 = lax.broadcasted_iota(jnp.int32, (X, 8, LANES), 2)
    index4 = lax.broadcasted_iota(jnp.int32, (X, 8, LANES), 0) * 8 + lax.broadcasted_iota(
        jnp.int32, (X, 8, LANES), 1
    )
    block = jnp.where(lanes4 == index4, vbuf[yh, :, z], 0.0)
    block = jnp.sum(jnp.sum(block, axis=0), axis=0, keepdims=True)
    dpot_ref[...] = block[:, 0:32] * eps
    finish()


def per_device(noise, data, noise_weight, data_weight):
    width = noise.shape[1] * C
    FQ = width // (Q * C)
    FS = X * FQ
    vmem = pl.BlockSpec(memory_space=pltpu.VMEM)
    anywhere = pl.BlockSpec(memory_space=pl.ANY)
    dma = pltpu.SemaphoreType.DMA
    targets, noise_pot, data_pot = pl.pallas_call(
        functools.partial(kernel, width),
        out_shape=(
            jax.ShapeDtypeStruct((Q, 8, FQ), BF16),
            jax.ShapeDtypeStruct((1, 8), F32),
            jax.ShapeDtypeStruct((1, 32), F32),
        ),
        in_specs=[anywhere] * 4,
        out_specs=(anywhere, vmem, vmem),
        scratch_shapes=[
            pltpu.SMEM((8,), jnp.int32),
            pltpu.SMEM((32,), jnp.int32),
            pltpu.VMEM((YL, 8, FS + LANES), BF16),
            pltpu.VMEM((32, 2 * FS), BF16),
            pltpu.VMEM((2 * X, X, 8, FQ), BF16),
            pltpu.VMEM((Z, X, 8, FQ), BF16),
            pltpu.VMEM((1, LANES), F32),
            pltpu.VMEM((2, X, YL, 8, FS + LANES), BF16),
            pltpu.VMEM((2, 8 * Q, FS + LANES), BF16),
            pltpu.VMEM((Z, X, 8, FQ), BF16),
            pltpu.VMEM((Z, 2 * X, 8, FQ), BF16),
            pltpu.VMEM((C * 32, FQ), BF16),
            pltpu.VMEM((Z, YH, 1, LANES), F32),
            pltpu.VMEM((Y, 2, 8, LANES), F32),
            pltpu.VMEM((Y, 2, 8, LANES), F32),
            pltpu.VMEM((2, 8, LANES), F32),
            pltpu.VMEM((Z, 2, 8, LANES), F32),
            pltpu.VMEM((2, X, Y, 2, 8, LANES), F32),
            pltpu.VMEM((2, X, Y, 8, LANES), F32),
            pltpu.VMEM((2, X, Y, 8, LANES), F32),
            pltpu.VMEM((Z, 2, X, 8, LANES), F32),
            pltpu.VMEM((X, YL, 8, FQ), BF16),
            dma((3 + YL,)),
        ] + [dma] * 5 + [dma((Z,))] + [dma] * 8 + [dma((2,))] * 2 + [dma] * 5 + [dma((Y,)), dma, dma((X,)), dma, dma],
        compiler_params=pltpu.CompilerParams(
            collective_id=0, has_side_effects=True, vmem_limit_bytes=60 * 1024 * 1024
        ),
    )(noise_weight, data_weight, noise, data)
    targets = jnp.transpose(targets, (1, 0, 2)).reshape(8, Q * FQ)
    return (targets, noise_pot.reshape(8), data_pot.reshape(32))


def solution(mesh):
    placed = (P("row", "col"), P("col", "row"), P("row"), P("col"))
    return jax.shard_map(
        per_device,
        mesh=mesh,
        in_specs=placed,
        out_specs=(P("row", "col"), P("row"), P("col")),
        check_vma=False,
    )
```

```python
import functools
import math

import jax
import jax.numpy as jnp
from jax import lax
from jax.experimental import pallas as pl
from jax.experimental.pallas import tpu as pltpu
from jax.sharding import PartitionSpec as P

HALVES = 4
MESH = pl.DeviceIdType.MESH
F32 = jnp.float32
BF16 = jnp.bfloat16
LANES = 128
X, YL, Z, YH = 4, 4, 8, 2
Y = YH * YL
Q = YL * X
C = Z * YH
NT = (((1,), (1,)), ((), ()))


def kernel(
    width,
    nw_hbm, dw_hbm, noise_ref, data_ref,
    out_ref, npot_ref, dpot_ref,
    nw_ref, dw_ref, nstage, dvm, dstage, relay, wstage, nbuf, nmat, dcrit, tdata, dfull,
    wbuf, pbuf, abuf, bbuf, rbuf, gall, lbuf, vbuf, plan, tbuf,
    load, n1s, n1r, n2s, n2r, es, er, fs, fr, ts, tr, w1s, w1r, w2s, w2r, sib_s, sib_r,
    as_, ar, bs, br, gs, gr, hs, hr, os_, or_,
):
    FQ = width // (Q * C)
    FS = X * FQ
    eps = 1.0 / math.sqrt(width)
    row = lax.axis_index("row")
    c = lax.axis_index("col")
    k = row % 2
    q = row // 2
    x = q % X
    yl = q // X
    z = c // YH
    yh = c % YH
    y = yh * YL + yl
    other = 1 - k

    def place(yl_, x_, k_):
        return (yl_ * X + x_) * 2 + k_

    sibling = (place(yl, x, other), c)

    def relay_of(j):
        return place(2 * k + j // X, j % X, yh), z * YH + x % YH

    def relay_source(i):
        f = YH * i + yh
        return place(f // X, f % X, yl // 2), z * YH + k

    to_self = jnp.logical_and(jnp.logical_and(k == yl // 2, yh == k), x % YH == yh)
    n_self = jnp.where(to_self, 1, 0).astype(jnp.int32)

    def finish():
        def sent(ref, sem):
            pltpu.make_async_copy(ref, ref, sem).wait()

        @pl.when(to_self)
        def _():
            sent(dstage.at[pl.ds(0, 2 * X - 1)], es)

        @pl.when(jnp.logical_not(to_self))
        def _():
            sent(dstage, es)

        sent(relay.at[pl.ds(0, Z - 1)], fs)
        sent(nstage.at[pl.ds(0, YL - 1)], n1s)
        sent(nbuf.at[k, pl.ds(0, X - 1)], n2s)
        sent(nbuf.at[k], sib_s.at[0])
        sent(wbuf.at[pl.ds(0, Z - 1), 0], w1s)
        sent(wbuf.at[:, yh], w2s)
        sent(pbuf.at[pl.ds(0, Y - 1)], as_)
        sent(tdata.at[pl.ds(0, 2 * X - 1)], ts)
        sent(rbuf.at[pl.ds(0, Z - 1)], bs)
        sent(gall.at[k, x, pl.ds(0, Y - 1)], gs)
        sent(gall.at[k, pl.ds(0, X - 1)], hs)
        sent(gall.at[k], sib_s.at[1])
        sent(out_ref.at[pl.ds(0, Q - 1)], os_)
        sent(out_ref, or_)

    loads = [
        pltpu.make_async_copy(nw_hbm, nw_ref, load.at[0]),
        pltpu.make_async_copy(dw_hbm, dw_ref, load.at[1]),
        pltpu.make_async_copy(data_ref, dvm, load.at[2]),
    ] + [
        pltpu.make_async_copy(
            noise_ref.at[:, pl.ds(t * FS, FS)], nstage.at[t, :, pl.ds(0, FS)], load.at[3 + t]
        )
        for t in range(YL)
    ]

    barrier = pltpu.get_barrier_semaphore()

    def greet(device):
        pl.semaphore_signal(barrier, inc=1, device_id=device, device_id_type=MESH)

    def greet_source(i, carry):
        device = relay_source(i)

        @pl.when(jnp.logical_or(device[0] != row, device[1] != c))
        def _():
            greet(device)

        return carry

    def greet_core(t, carry):
        greet((place(yl, t, other), c))
        return carry

    def greet_z(s, carry):
        greet((row, lax.rem(z + s, Z) * YH + yh))
        return carry

    def greet_y(t, carry):
        greet((place(t, x, k), z * YH + 1 - yh))
        return carry

    def greet_row(s, carry):
        greet((lax.rem(q + s, Q) * 2 + k, c))
        return carry

    for copy in loads[2::-1]:
        copy.start()
    lax.fori_loop(0, Z, greet_source, 0)
    lax.fori_loop(1, Z, greet_z, 0)
    lax.fori_loop(0, YL, greet_y, 0)
    lax.fori_loop(1, Q, greet_row, 0)
    lax.fori_loop(0, X, greet_core, 0)
    for copy in loads[3:]:
        copy.start()

    loads[2].wait()
    for j in range(2 * X):
        s, t = j // X, j % X
        for f in range(X):
            cut = dvm[:, s * FS + f * FQ:s * FS + (f + 1) * FQ].astype(F32)
            dstage[j, f] = cut[8 * t:8 * t + 8].astype(BF16)
    pl.semaphore_wait(barrier, (Q - 1) + X + (Z - 1) + YL + 2 * X - n_self)

    def send_data(j, carry):
        device = relay_of(j)
        is_self = jnp.logical_and(device[0] == row, device[1] == c)
        slot = q // YH

        @pl.when(is_self)
        def _():
            pltpu.make_async_copy(dstage.at[j], relay.at[slot], er.at[slot]).start()

        @pl.when(jnp.logical_not(is_self))
        def _():
            pltpu.make_async_remote_copy(
                dstage.at[j], relay.at[slot], es, er.at[slot],
                device_id=device, device_id_type=MESH,
            ).start()

        return carry

    lax.fori_loop(0, 2 * X, send_data, 0)

    loads[0].wait()
    for copy in loads[3:]:
        copy.wait()

    rows8 = lax.broadcasted_iota(jnp.int32, (8, LANES), 0)
    lanes8 = lax.broadcasted_iota(jnp.int32, (8, LANES), 1)
    noise_w = jnp.zeros((8, LANES), jnp.int32)
    for i in range(8):
        noise_w = jnp.where(rows8 == i, nw_ref[i], noise_w)
    noise_w = noise_w.astype(F32)
    for t in range(YL):
        nf = nstage[t, :, 0:FS].astype(F32)
        sq = jnp.sum(nf * nf, axis=1, keepdims=True)
        hi = sq.astype(BF16).astype(F32)
        mid = (sq - hi).astype(BF16).astype(F32)
        lo = sq - hi - mid
        tail = jnp.where(lanes8 == 3, noise_w, 0.0)
        tail = jnp.where(lanes8 == 2, lo, tail)
        tail = jnp.where(lanes8 == 1, mid, tail)
        tail = jnp.where(lanes8 == 0, hi, tail)
        nstage[t, :, FS:FS + LANES] = tail.astype(BF16)

    def send_noise_y(s, carry):
        t = lax.rem(yl + s, YL)
        pltpu.make_async_remote_copy(
            nstage.at[t], nbuf.at[k, x, yl], n1s, n1r,
            device_id=(place(t, x, k), c), device_id_type=MESH,
        ).start()
        return carry

    lax.fori_loop(1, YL, send_noise_y, 0)
    pltpu.make_async_copy(nstage.at[yl], nbuf.at[k, x, yl], n1r).start()

    loads[1].wait()
    lanes1 = lax.broadcasted_iota(jnp.int32, (1, LANES), 1)
    data_w = jnp.zeros((1, LANES), jnp.int32)
    for i in range(32):
        data_w = jnp.where(lanes1 == i, dw_ref[i], data_w)
    wstage[...] = data_w.astype(F32)

    def send_w(s, carry):
        t = lax.rem(z + s, Z)
        pltpu.make_async_remote_copy(
            wstage, wbuf.at[z, yh], w1s, w1r,
            device_id=(row, t * YH + yh), device_id_type=MESH,
        ).start()
        return carry

    lax.fori_loop(1, Z, send_w, 0)
    pltpu.make_async_copy(wstage, wbuf.at[z, yh], w1r).start()

    def arrived(ref, sem):
        pltpu.make_async_copy(ref, ref, sem).wait()

    def swap(ref, i):
        return pltpu.make_async_remote_copy(
            ref, ref, sib_s.at[i], sib_r.at[i], device_id=sibling, device_id_type=MESH
        )

    arrived(nbuf.at[k, x], n1r)

    def send_noise_x(s, carry):
        t = lax.rem(x + s, X)
        pltpu.make_async_remote_copy(
            nbuf.at[k, x], nbuf.at[k, x], n2s, n2r,
            device_id=(place(yl, t, k), c), device_id_type=MESH,
        ).start()
        return carry

    lax.fori_loop(1, X, send_noise_x, 0)

    def hand_on(i, carry):
        t = lax.rem(YH * yl + i, Z)
        arrived(relay.at[t], er.at[t])

        @pl.when(t == z)
        def _():
            pltpu.make_async_copy(relay.at[t], dcrit.at[z], fr).start()

        @pl.when(t != z)
        def _():
            pltpu.make_async_remote_copy(
                relay.at[t], dcrit.at[z], fs, fr,
                device_id=(row, t * YH + yh), device_id_type=MESH,
            ).start()

        return carry

    lax.fori_loop(0, Z, hand_on, 0)

    def noise_rows(core):
        for t in range(2):
            part = nbuf[core, 2 * t:2 * t + 2].astype(F32)
            nmat[core, t * 4 * Q:(t + 1) * 4 * Q, :] = part.reshape(4 * Q, FS + LANES).astype(BF16)

    arrived(nbuf.at[k, pl.ds(0, X - 1)], n2r)
    noise_swap = swap(nbuf.at[k], 0)
    noise_swap.start()
    noise_rows(k)
    arrived(nbuf.at[other], sib_r.at[0])
    noise_rows(other)
    tail = nmat[:, :, FS:FS + LANES].reshape(16 * Q, LANES)
    pick_sq = jnp.where(lanes8 < 3, 1.0, 0.0).astype(BF16)
    pick_w = jnp.where(lanes8 == 3, 1.0, 0.0).astype(BF16)
    nsq = lax.dot_general(pick_sq, tail, NT, preferred_element_type=F32)[0:1, :]
    wa = lax.dot_general(pick_w, tail, NT, preferred_element_type=F32)[0:1, :]

    arrived(wbuf.at[:, yh], w1r)
    pltpu.make_async_remote_copy(
        wbuf.at[:, yh], wbuf.at[:, yh], w2s, w2r,
        device_id=(row, z * YH + 1 - yh), device_id_type=MESH,
    ).start()

    arrived(dcrit, fr)
    df = dcrit[...].astype(F32)
    part = jnp.sum(
        jnp.sum(df * df, axis=1).reshape(Z * 8, FQ), axis=1, keepdims=True
    ) + nsq
    dm = (df * -2.0)
    for f in range(X):
        part = part + lax.dot_general(
            dm[:, f].reshape(Z * 8, FQ).astype(BF16),
            nmat[:, :, f * FQ:(f + 1) * FQ].reshape(16 * Q, FQ),
            NT, preferred_element_type=F32,
        )
    for h in range(2):
        pbuf[:, h] = part[:, h * LANES:(h + 1) * LANES].reshape(Y, 8, LANES)

    def y_peer(t):
        return place(t % YL, x, k), z * YH + t // YL

    def send_a(s, carry):
        t = lax.rem(y + s, Y)
        pltpu.make_async_remote_copy(
            pbuf.at[t], abuf.at[y], as_, ar, device_id=y_peer(t), device_id_type=MESH
        ).start()
        return carry

    lax.fori_loop(1, Y, send_a, 0)
    pltpu.make_async_copy(pbuf.at[y], abuf.at[y], ar).start()

    def send_features(j, carry):
        t, core = lax.rem(x + j // 2, X), lax.rem(k + j, 2)
        pltpu.make_async_remote_copy(
            dcrit.at[:, t], tdata.at[:, k * X + x], ts, tr,
            device_id=(place(yl, t, core), c), device_id_type=MESH,
        ).start()
        return carry

    lax.fori_loop(1, 2 * X, send_features, 0)
    pltpu.make_async_copy(dcrit.at[:, x], tdata.at[:, k * X + x], tr).start()

    log_a = jnp.log(wa / jnp.sum(wa, axis=1, keepdims=True))
    log_a = [log_a[:, h * LANES:(h + 1) * LANES] for h in range(2)]
    arrived(abuf, ar)
    total = abuf[0]
    for j in range(1, Y):
        total = total + abuf[j]
    bbuf[...] = total

    def send_b(s, carry):
        t = lax.rem(z + s, Z)
        pltpu.make_async_remote_copy(
            bbuf, rbuf.at[z], bs, br, device_id=(row, t * YH + yh), device_id_type=MESH
        ).start()
        return carry

    lax.fori_loop(1, Z, send_b, 0)
    pltpu.make_async_copy(bbuf, rbuf.at[z], br).start()

    arrived(rbuf, br)
    total = rbuf[0]
    for j in range(1, Z):
        total = total + rbuf[j]
    gall[k, x, y] = total * (-1.0 / (width * eps))

    def send_g(s, carry):
        t = lax.rem(y + s, Y)
        pltpu.make_async_remote_copy(
            gall.at[k, x, y], gall.at[k, x, y], gs, gr.at[y],
            device_id=y_peer(t), device_id_type=MESH,
        ).start()
        return carry

    lax.fori_loop(1, Y, send_g, 0)

    def send_x(piece):
        for s in range(1, X):
            t = lax.rem(x + s, X)
            pltpu.make_async_remote_copy(
                gall.at[k, x, piece], gall.at[k, x, piece], hs, hr.at[x],
                device_id=(place(yl, t, k), c), device_id_type=MESH,
            ).start()

    send_x(y)

    arrived(wbuf.at[:, 1 - yh], w2r)
    wb = wbuf[...].reshape(C, 1, LANES)
    w_sum = jnp.sum(jnp.sum(wb, axis=0), axis=1, keepdims=True)
    spot = lax.broadcasted_iota(jnp.int32, (C, 32, LANES), 1) == lax.broadcasted_iota(
        jnp.int32, (C, 32, LANES), 2
    )
    wb = jnp.where(spot, wb, 0.0).reshape(C * 32, LANES).astype(BF16)
    wb = jnp.dot(wb, jnp.ones((LANES, LANES), BF16), preferred_element_type=F32)
    log_b = jnp.log(wb / w_sum).reshape(Z, YH, X, 8, LANES)
    for a in range(YH):
        for b in range(X):
            lbuf[a, b] = log_b[:, a, b]
    arrived(tdata, tr)
    for t in range(Z):
        dfull[t * 64:(t + 1) * 64, :] = tdata[t].astype(F32).reshape(64, FQ).astype(BF16)

    def gather_y(i, carry):
        d = (i + 1) // 2
        t = lax.rem(y + jnp.where(i % 2 == 1, d, Y - d), Y)
        arrived(gall.at[k, x, t], gr.at[t])
        send_x(t)
        return carry

    lax.fori_loop(1, Y, gather_y, 0)

    def send_core(t):
        pltpu.make_async_remote_copy(
            gall.at[k, t], gall.at[k, t], sib_s.at[1], sib_r.at[1],
            device_id=sibling, device_id_type=MESH,
        ).start()

    send_core(x)

    def gather_x(s, carry):
        t = lax.rem(x + jnp.where(s == 2, 3, jnp.where(s == 3, 2, 1)), X)
        arrived(gall.at[k, t], hr.at[t])
        send_core(t)
        return carry

    lax.fori_loop(1, X, gather_x, 0)
    arrived(gall.at[other], sib_r.at[1])

    def parts(i):
        return i // X, i % X

    def peak_step(i, peak):
        a, b = parts(i)
        return jnp.maximum(peak, jnp.max(gall[a, b], axis=0))

    peak = jnp.full((2, 8, LANES), -jnp.inf, F32)
    for i in range(2 * X):
        peak = peak_step(i, peak)
    for rounds in range(HALVES // 2):
        top = jnp.max(peak, axis=1, keepdims=True)

        def noise_step(i, acc):
            a, b = parts(i)
            s = gall[a, b]
            if rounds:
                s = s + vbuf[a, b][:, None]
            return acc + jnp.sum(jnp.exp(s - top), axis=0)

        acc = jnp.zeros((2, 8, LANES), F32)
        for i in range(2 * X):
            acc = noise_step(i, acc)
        lse = top + jnp.log(jnp.sum(acc, axis=1, keepdims=True))
        u = jnp.concatenate([(log_a[h] - lse[h])[None] for h in range(2)], axis=0)

        def data_step(i, peak):
            a, b = parts(i)
            s = gall[a, b]
            w = s + u
            m = jnp.max(jnp.max(w, axis=1), axis=2, keepdims=True)
            e = jnp.sum(jnp.sum(jnp.exp(w - m[:, None]), axis=1), axis=2, keepdims=True)
            v = lbuf[a, b] - (m + jnp.log(e))
            vbuf[a, b] = v
            return jnp.maximum(peak, jnp.max(s + v[:, None], axis=0))

        peak = jnp.full((2, 8, LANES), -jnp.inf, F32)
        for i in range(2 * X):
            peak = data_step(i, peak)

    own_u = jnp.where(k == 0, u[0], u[1])
    for i in range(2 * X):
        a, b = parts(i)
        plan[:, a, b] = jnp.exp(gall[a, b, :, k] + own_u + vbuf[a, b])
    p = jnp.transpose(plan[...].reshape(C * 32, LANES), (1, 0))
    mass = jnp.sum(p, axis=1, keepdims=True)

    value = jnp.dot(
        p.astype(BF16), dfull[...], preferred_element_type=F32
    ) / mass
    tbuf[...] = value.reshape(X, YL, 8, FQ).astype(BF16)

    def send_t(s, carry):
        t = lax.rem(q + s, Q)
        pltpu.make_async_remote_copy(
            tbuf.at[t % X, t // X], out_ref.at[q], os_, or_,
            device_id=(t * 2 + k, c), device_id_type=MESH,
        ).start()
        return carry

    lax.fori_loop(1, Q, send_t, 0)
    pltpu.make_async_copy(tbuf.at[x, yl], out_ref.at[q], or_).start()

    mine = own_u[:, 0:8]
    for t in range(1, Q):
        mine = jnp.where(x * YL + yl == t, own_u[:, 8 * t:8 * t + 8], mine)
    npot_ref[...] = mine * eps
    lanes4 = lax.broadcasted_iota(jnp.int32, (X, 8, LANES), 2)
    index4 = lax.broadcasted_iota(jnp.int32, (X, 8, LANES), 0) * 8 + lax.broadcasted_iota(
        jnp.int32, (X, 8, LANES), 1
    )
    block = jnp.where(lanes4 == index4, vbuf[yh, :, z], 0.0)
    block = jnp.sum(jnp.sum(block, axis=0), axis=0, keepdims=True)
    dpot_ref[...] = block[:, 0:32] * eps
    finish()


def per_device(noise, data, noise_weight, data_weight):
    width = noise.shape[1] * C
    FQ = width // (Q * C)
    FS = X * FQ
    vmem = pl.BlockSpec(memory_space=pltpu.VMEM)
    anywhere = pl.BlockSpec(memory_space=pl.ANY)
    dma = pltpu.SemaphoreType.DMA
    targets, noise_pot, data_pot = pl.pallas_call(
        functools.partial(kernel, width),
        out_shape=(
            jax.ShapeDtypeStruct((Q, 8, FQ), BF16),
            jax.ShapeDtypeStruct((1, 8), F32),
            jax.ShapeDtypeStruct((1, 32), F32),
        ),
        in_specs=[anywhere] * 4,
        out_specs=(anywhere, vmem, vmem),
        scratch_shapes=[
            pltpu.SMEM((8,), jnp.int32),
            pltpu.SMEM((32,), jnp.int32),
            pltpu.VMEM((YL, 8, FS + LANES), BF16),
            pltpu.VMEM((32, 2 * FS), BF16),
            pltpu.VMEM((2 * X, X, 8, FQ), BF16),
            pltpu.VMEM((Z, X, 8, FQ), BF16),
            pltpu.VMEM((1, LANES), F32),
            pltpu.VMEM((2, X, YL, 8, FS + LANES), BF16),
            pltpu.VMEM((2, 8 * Q, FS + LANES), BF16),
            pltpu.VMEM((Z, X, 8, FQ), BF16),
            pltpu.VMEM((Z, 2 * X, 8, FQ), BF16),
            pltpu.VMEM((C * 32, FQ), BF16),
            pltpu.VMEM((Z, YH, 1, LANES), F32),
            pltpu.VMEM((Y, 2, 8, LANES), F32),
            pltpu.VMEM((Y, 2, 8, LANES), F32),
            pltpu.VMEM((2, 8, LANES), F32),
            pltpu.VMEM((Z, 2, 8, LANES), F32),
            pltpu.VMEM((2, X, Y, 2, 8, LANES), F32),
            pltpu.VMEM((2, X, Y, 8, LANES), F32),
            pltpu.VMEM((2, X, Y, 8, LANES), F32),
            pltpu.VMEM((Z, 2, X, 8, LANES), F32),
            pltpu.VMEM((X, YL, 8, FQ), BF16),
            dma((3 + YL,)),
        ] + [dma] * 5 + [dma((Z,))] + [dma] * 8 + [dma((2,))] * 2 + [dma] * 5 + [dma((Y,)), dma, dma((X,)), dma, dma],
        compiler_params=pltpu.CompilerParams(
            collective_id=0, has_side_effects=True, vmem_limit_bytes=60 * 1024 * 1024
        ),
    )(noise_weight, data_weight, noise, data)
    targets = jnp.transpose(targets, (1, 0, 2)).reshape(8, Q * FQ)
    return (targets, noise_pot.reshape(8), data_pot.reshape(32))


def solution(mesh):
    placed = (P("row", "col"), P("col", "row"), P("row"), P("col"))
    return jax.shard_map(
        per_device,
        mesh=mesh,
        in_specs=placed,
        out_specs=(P("row", "col"), P("row"), P("col")),
        check_vma=False,
    )
```

```python
import functools
import math

import jax
import jax.numpy as jnp
from jax import lax
from jax.experimental import pallas as pl
from jax.experimental.pallas import tpu as pltpu
from jax.sharding import PartitionSpec as P

HALVES = 4
MESH = pl.DeviceIdType.MESH
F32 = jnp.float32
BF16 = jnp.bfloat16
LANES = 128
X, YL, Z, YH = 4, 4, 8, 2
Y = YH * YL
Q = YL * X
C = Z * YH
NT = (((1,), (1,)), ((), ()))


def kernel(
    width,
    nw_hbm, dw_hbm, noise_ref, data_ref,
    out_ref, pots_ref,
    nw_ref, dw_ref, nstage, dvm, dstage, relay, wstage, nbuf, nmat, dcrit, tdata, dfull,
    wbuf, pbuf, abuf, bbuf, rbuf, gall, lbuf, vbuf, plan, turned, tbuf, pots,
    load, n1s, n1r, n2s, n2r, es, er, fs, fr, ts, tr, w1s, w1r, w2s, w2r, sib_s, sib_r,
    as_, ar, bs, br, gs, gr, hs, hr, os_, or_, ps,
):
    FQ = width // (Q * C)
    FS = X * FQ
    eps = 1.0 / math.sqrt(width)
    row = lax.axis_index("row")
    c = lax.axis_index("col")
    k = row % 2
    q = row // 2
    x = q % X
    yl = q // X
    z = c // YH
    yh = c % YH
    y = yh * YL + yl
    other = 1 - k

    def place(yl_, x_, k_):
        return (yl_ * X + x_) * 2 + k_

    sibling = (place(yl, x, other), c)

    def relay_of(j):
        return place(2 * k + j // X, j % X, yh), z * YH + x % YH

    def relay_source(i):
        f = YH * i + yh
        return place(f // X, f % X, yl // 2), z * YH + k

    to_self = jnp.logical_and(jnp.logical_and(k == yl // 2, yh == k), x % YH == yh)
    n_self = jnp.where(to_self, 1, 0).astype(jnp.int32)

    def finish():
        def sent(ref, sem):
            pltpu.make_async_copy(ref, ref, sem).wait()

        @pl.when(to_self)
        def _():
            sent(dstage.at[pl.ds(0, 2 * X - 1)], es)

        @pl.when(jnp.logical_not(to_self))
        def _():
            sent(dstage, es)

        sent(relay.at[pl.ds(0, Z - 1)], fs)
        sent(nstage.at[pl.ds(0, YL - 1)], n1s)
        sent(nbuf.at[k, pl.ds(0, X - 1)], n2s)
        sent(nbuf.at[k], sib_s.at[0])
        sent(wbuf.at[pl.ds(0, Z - 1), 0], w1s)
        sent(wbuf.at[:, yh], w2s)
        sent(pbuf.at[pl.ds(0, Y - 1)], as_)
        sent(tdata.at[pl.ds(0, X - 1)], ts)
        sent(rbuf.at[pl.ds(0, Z - 1)], bs)
        sent(gall.at[k, x, pl.ds(0, Y - 1)], gs)
        sent(gall.at[k, pl.ds(0, X - 1)], hs)
        sent(gall.at[k], sib_s.at[1])
        sent(tdata.at[pl.ds(0, X)], sib_s.at[2])
        sent(out_ref.at[pl.ds(0, YL - 1)], os_)
        sent(out_ref, or_)
        sent(pots_ref, ps)

    loads = [
        pltpu.make_async_copy(nw_hbm, nw_ref, load.at[0]),
        pltpu.make_async_copy(dw_hbm, dw_ref, load.at[1]),
        pltpu.make_async_copy(data_ref, dvm, load.at[2]),
    ] + [
        pltpu.make_async_copy(
            noise_ref.at[:, pl.ds(t * FS, FS)], nstage.at[t, :, pl.ds(0, FS)], load.at[3 + t]
        )
        for t in range(YL)
    ]

    barrier = pltpu.get_barrier_semaphore()

    def greet(device):
        pl.semaphore_signal(barrier, inc=1, device_id=device, device_id_type=MESH)

    def greet_source(i, carry):
        device = relay_source(i)

        @pl.when(jnp.logical_or(device[0] != row, device[1] != c))
        def _():
            greet(device)

        return carry

    def greet_z(s, carry):
        greet((row, lax.rem(z + s, Z) * YH + yh))
        return carry

    def greet_y(s, carry):
        t = lax.rem(y + s, Y)
        greet((place(t % YL, x, k), z * YH + t // YL))
        return carry

    def greet_x(s, carry):
        greet((place(yl, lax.rem(x + s, X), k), c))
        return carry

    for copy in loads[2::-1]:
        copy.start()
    lax.fori_loop(0, Z, greet_source, 0)
    lax.fori_loop(1, Z, greet_z, 0)
    lax.fori_loop(1, Y, greet_y, 0)
    lax.fori_loop(1, X, greet_x, 0)
    greet(sibling)
    for copy in loads[3:]:
        copy.start()

    loads[2].wait()
    for j in range(2 * X):
        s, t = j // X, j % X
        for f in range(X):
            cut = dvm[:, s * FS + f * FQ:s * FS + (f + 1) * FQ].astype(F32)
            dstage[j, f] = cut[8 * t:8 * t + 8].astype(BF16)
    pl.semaphore_wait(barrier, (Y - 1) + (X - 1) + (Z - 1) + 1 + 2 * X - n_self)

    def send_data(j, carry):
        device = relay_of(j)
        is_self = jnp.logical_and(device[0] == row, device[1] == c)
        slot = q // YH

        @pl.when(is_self)
        def _():
            pltpu.make_async_copy(dstage.at[j], relay.at[slot], er.at[slot]).start()

        @pl.when(jnp.logical_not(is_self))
        def _():
            pltpu.make_async_remote_copy(
                dstage.at[j], relay.at[slot], es, er.at[slot],
                device_id=device, device_id_type=MESH,
            ).start()

        return carry

    lax.fori_loop(0, 2 * X, send_data, 0)

    loads[0].wait()
    for copy in loads[3:]:
        copy.wait()

    rows8 = lax.broadcasted_iota(jnp.int32, (8, LANES), 0)
    lanes8 = lax.broadcasted_iota(jnp.int32, (8, LANES), 1)
    noise_w = jnp.zeros((8, LANES), jnp.int32)
    for i in range(8):
        noise_w = jnp.where(rows8 == i, nw_ref[i], noise_w)
    noise_w = noise_w.astype(F32)
    for t in range(YL):
        nf = nstage[t, :, 0:FS].astype(F32)
        sq = jnp.sum(nf * nf, axis=1, keepdims=True)
        hi = sq.astype(BF16).astype(F32)
        mid = (sq - hi).astype(BF16).astype(F32)
        lo = sq - hi - mid
        tail = jnp.where(lanes8 == 3, noise_w, 0.0)
        tail = jnp.where(lanes8 == 2, lo, tail)
        tail = jnp.where(lanes8 == 1, mid, tail)
        tail = jnp.where(lanes8 == 0, hi, tail)
        nstage[t, :, FS:FS + LANES] = tail.astype(BF16)

    def send_noise_y(s, carry):
        t = lax.rem(yl + s, YL)
        pltpu.make_async_remote_copy(
            nstage.at[t], nbuf.at[k, x, yl], n1s, n1r,
            device_id=(place(t, x, k), c), device_id_type=MESH,
        ).start()
        return carry

    lax.fori_loop(1, YL, send_noise_y, 0)
    pltpu.make_async_copy(nstage.at[yl], nbuf.at[k, x, yl], n1r).start()

    loads[1].wait()
    lanes1 = lax.broadcasted_iota(jnp.int32, (1, LANES), 1)
    data_w = jnp.zeros((1, LANES), jnp.int32)
    for i in range(32):
        data_w = jnp.where(lanes1 == i, dw_ref[i], data_w)
    wstage[...] = data_w.astype(F32)

    def send_w(s, carry):
        t = lax.rem(z + s, Z)
        pltpu.make_async_remote_copy(
            wstage, wbuf.at[z, yh], w1s, w1r,
            device_id=(row, t * YH + yh), device_id_type=MESH,
        ).start()
        return carry

    lax.fori_loop(1, Z, send_w, 0)
    pltpu.make_async_copy(wstage, wbuf.at[z, yh], w1r).start()

    def arrived(ref, sem):
        pltpu.make_async_copy(ref, ref, sem).wait()

    def swap(ref, i):
        return pltpu.make_async_remote_copy(
            ref, ref, sib_s.at[i], sib_r.at[i], device_id=sibling, device_id_type=MESH
        )

    arrived(nbuf.at[k, x], n1r)

    def send_noise_x(s, carry):
        t = lax.rem(x + s, X)
        pltpu.make_async_remote_copy(
            nbuf.at[k, x], nbuf.at[k, x], n2s, n2r,
            device_id=(place(yl, t, k), c), device_id_type=MESH,
        ).start()
        return carry

    lax.fori_loop(1, X, send_noise_x, 0)

    def hand_on(i, carry):
        t = lax.rem(YH * yl + i, Z)
        arrived(relay.at[t], er.at[t])

        @pl.when(t == z)
        def _():
            pltpu.make_async_copy(relay.at[t], dcrit.at[z], fr).start()

        @pl.when(t != z)
        def _():
            pltpu.make_async_remote_copy(
                relay.at[t], dcrit.at[z], fs, fr,
                device_id=(row, t * YH + yh), device_id_type=MESH,
            ).start()

        return carry

    lax.fori_loop(0, Z, hand_on, 0)

    def noise_rows(core):
        for t in range(2):
            part = nbuf[core, 2 * t:2 * t + 2].astype(F32)
            nmat[core, t * 4 * Q:(t + 1) * 4 * Q, :] = part.reshape(4 * Q, FS + LANES).astype(BF16)

    arrived(nbuf.at[k, pl.ds(0, X - 1)], n2r)
    noise_swap = swap(nbuf.at[k], 0)
    noise_swap.start()
    noise_rows(k)
    arrived(nbuf.at[other], sib_r.at[0])
    noise_rows(other)
    tail = nmat[:, :, FS:FS + LANES].reshape(16 * Q, LANES)
    pick_sq = jnp.where(lanes8 < 3, 1.0, 0.0).astype(BF16)
    pick_w = jnp.where(lanes8 == 3, 1.0, 0.0).astype(BF16)
    nsq = lax.dot_general(pick_sq, tail, NT, preferred_element_type=F32)[0:1, :]
    wa = lax.dot_general(pick_w, tail, NT, preferred_element_type=F32)[0:1, :]

    arrived(wbuf.at[:, yh], w1r)
    pltpu.make_async_remote_copy(
        wbuf.at[:, yh], wbuf.at[:, yh], w2s, w2r,
        device_id=(row, z * YH + 1 - yh), device_id_type=MESH,
    ).start()

    arrived(dcrit, fr)
    df = dcrit[...].astype(F32)
    part = jnp.sum(
        jnp.sum(df * df, axis=1).reshape(Z * 8, FQ), axis=1, keepdims=True
    ) + nsq
    dm = (df * -2.0)
    for f in range(X):
        part = part + lax.dot_general(
            dm[:, f].reshape(Z * 8, FQ).astype(BF16),
            nmat[:, :, f * FQ:(f + 1) * FQ].reshape(16 * Q, FQ),
            NT, preferred_element_type=F32,
        )
    for h in range(2):
        pbuf[:, h] = part[:, h * LANES:(h + 1) * LANES].reshape(Y, 8, LANES)

    def y_peer(t):
        return place(t % YL, x, k), z * YH + t // YL

    def send_a(s, carry):
        t = lax.rem(y + s, Y)
        pltpu.make_async_remote_copy(
            pbuf.at[t], abuf.at[y], as_, ar, device_id=y_peer(t), device_id_type=MESH
        ).start()
        return carry

    lax.fori_loop(1, Y, send_a, 0)
    pltpu.make_async_copy(pbuf.at[y], abuf.at[y], ar).start()

    def send_features(s, carry):
        t = lax.rem(x + s, X)
        pltpu.make_async_remote_copy(
            dcrit, tdata.at[k * X + x], ts, tr,
            device_id=(place(yl, t, k), c), device_id_type=MESH,
        ).start()
        return carry

    lax.fori_loop(1, X, send_features, 0)
    pltpu.make_async_copy(dcrit, tdata.at[k * X + x], tr).start()

    log_a = jnp.log(wa / jnp.sum(wa, axis=1, keepdims=True))
    log_a = [log_a[:, h * LANES:(h + 1) * LANES] for h in range(2)]
    arrived(abuf, ar)
    total = abuf[0]
    for j in range(1, Y):
        total = total + abuf[j]
    bbuf[...] = total

    def send_b(s, carry):
        t = lax.rem(z + s, Z)
        pltpu.make_async_remote_copy(
            bbuf, rbuf.at[z], bs, br, device_id=(row, t * YH + yh), device_id_type=MESH
        ).start()
        return carry

    lax.fori_loop(1, Z, send_b, 0)
    pltpu.make_async_copy(bbuf, rbuf.at[z], br).start()

    arrived(rbuf, br)
    total = rbuf[0]
    for j in range(1, Z):
        total = total + rbuf[j]
    gall[k, x, y] = total * (-1.0 / (width * eps))

    def send_g(s, carry):
        t = lax.rem(y + s, Y)
        pltpu.make_async_remote_copy(
            gall.at[k, x, y], gall.at[k, x, y], gs, gr.at[y],
            device_id=y_peer(t), device_id_type=MESH,
        ).start()
        return carry

    lax.fori_loop(1, Y, send_g, 0)

    def send_x(piece):
        for s in range(1, X):
            t = lax.rem(x + s, X)
            pltpu.make_async_remote_copy(
                gall.at[k, x, piece], gall.at[k, x, piece], hs, hr.at[x],
                device_id=(place(yl, t, k), c), device_id_type=MESH,
            ).start()

    send_x(y)

    arrived(wbuf.at[:, 1 - yh], w2r)
    wb = wbuf[...].reshape(C, 1, LANES)
    w_sum = jnp.sum(jnp.sum(wb, axis=0), axis=1, keepdims=True)
    spot = lax.broadcasted_iota(jnp.int32, (C, 32, LANES), 1) == lax.broadcasted_iota(
        jnp.int32, (C, 32, LANES), 2
    )
    wb = jnp.where(spot, wb, 0.0).reshape(C * 32, LANES).astype(BF16)
    wb = jnp.dot(wb, jnp.ones((LANES, LANES), BF16), preferred_element_type=F32)
    log_b = jnp.log(wb / w_sum).reshape(Z, YH, X, 8, LANES)
    for a in range(YH):
        for b in range(X):
            lbuf[a, b] = log_b[:, a, b]
    def data_rows(core):
        def step(i, carry):
            g = core * X + i
            for f in range(X):
                cut = tdata[g, :, f].astype(F32).reshape(Z * 8, FQ)
                dfull[g, :, f * FQ:(f + 1) * FQ] = cut.astype(BF16)
            return carry

        lax.fori_loop(0, X, step, 0)

    own_rows = tdata.at[pl.ds(k * X, X)]
    other_rows = tdata.at[pl.ds(other * X, X)]
    arrived(own_rows, tr)
    rows_swap = swap(own_rows, 2)
    rows_swap.start()
    data_rows(k)

    def gather_y(i, carry):
        d = (i + 1) // 2
        t = lax.rem(y + jnp.where(i % 2 == 1, d, Y - d), Y)
        arrived(gall.at[k, x, t], gr.at[t])
        send_x(t)
        return carry

    lax.fori_loop(1, Y, gather_y, 0)

    def send_core(t):
        pltpu.make_async_remote_copy(
            gall.at[k, t], gall.at[k, t], sib_s.at[1], sib_r.at[1],
            device_id=sibling, device_id_type=MESH,
        ).start()

    send_core(x)

    def gather_x(s, carry):
        t = lax.rem(x + jnp.where(s == 2, 3, jnp.where(s == 3, 2, 1)), X)
        arrived(gall.at[k, t], hr.at[t])
        send_core(t)
        return carry

    lax.fori_loop(1, X, gather_x, 0)
    arrived(other_rows, sib_r.at[2])
    data_rows(other)
    arrived(gall.at[other], sib_r.at[1])

    def parts(i):
        return i // X, i % X

    def peak_step(i, peak):
        a, b = parts(i)
        return jnp.maximum(peak, jnp.max(gall[a, b], axis=0))

    peak = jnp.full((2, 8, LANES), -jnp.inf, F32)
    for i in range(2 * X):
        peak = peak_step(i, peak)
    for rounds in range(HALVES // 2):
        top = jnp.max(peak, axis=1, keepdims=True)

        def noise_step(i, acc):
            a, b = parts(i)
            s = gall[a, b]
            if rounds:
                s = s + vbuf[a, b][:, None]
            return acc + jnp.sum(jnp.exp(s - top), axis=0)

        acc = jnp.zeros((2, 8, LANES), F32)
        for i in range(2 * X):
            acc = noise_step(i, acc)
        lse = top + jnp.log(jnp.sum(acc, axis=1, keepdims=True))
        u = jnp.concatenate([(log_a[h] - lse[h])[None] for h in range(2)], axis=0)

        def data_step(i, peak):
            a, b = parts(i)
            s = gall[a, b]
            w = s + u
            m = jnp.max(jnp.max(w, axis=1), axis=2, keepdims=True)
            e = jnp.sum(jnp.sum(jnp.exp(w - m[:, None]), axis=1), axis=2, keepdims=True)
            v = lbuf[a, b] - (m + jnp.log(e))
            vbuf[a, b] = v
            return jnp.maximum(peak, jnp.max(s + v[:, None], axis=0))

        peak = jnp.full((2, 8, LANES), -jnp.inf, F32)
        for i in range(2 * X):
            peak = data_step(i, peak)

    pots[...] = jnp.zeros_like(pots)
    own_u = jnp.where(k == 0, u[0], u[1])
    for i in range(2 * X):
        a, b = parts(i)
        plan[a, b] = jnp.exp(gall[a, b, :, k] + own_u + vbuf[a, b])
    turned[...] = jnp.transpose(plan[...].reshape(C * 32, LANES), (1, 0))
    p = turned[pl.ds(pl.multiple_of(x * YL * 8, YL * 8), YL * 8), :]
    mass = jnp.sum(p, axis=1, keepdims=True)
    value = jnp.dot(
        p.astype(BF16), dfull[...].reshape(C * 32, FS), preferred_element_type=F32
    ) / mass
    tbuf[...] = value.reshape(YL, 8, FS).astype(BF16)

    def send_t(s, carry):
        t = lax.rem(yl + s, YL)
        pltpu.make_async_remote_copy(
            tbuf.at[t], out_ref.at[yl], os_, or_,
            device_id=(place(t, x, k), c), device_id_type=MESH,
        ).start()
        return carry

    lax.fori_loop(1, YL, send_t, 0)
    pltpu.make_async_copy(tbuf.at[yl], out_ref.at[yl], or_).start()

    mine = own_u[:, 0:8]
    for t in range(1, Q):
        mine = jnp.where(x * YL + yl == t, own_u[:, 8 * t:8 * t + 8], mine)
    pots[0:1, 0:8] = mine * eps
    lanes4 = lax.broadcasted_iota(jnp.int32, (X, 8, LANES), 2)
    index4 = lax.broadcasted_iota(jnp.int32, (X, 8, LANES), 0) * 8 + lax.broadcasted_iota(
        jnp.int32, (X, 8, LANES), 1
    )
    block = jnp.where(lanes4 == index4, vbuf[yh, :, z], 0.0)
    block = jnp.sum(jnp.sum(block, axis=0), axis=0, keepdims=True)
    pots[1:2, :] = block * eps
    pltpu.make_async_copy(pots, pots_ref, ps).start()
    finish()


def per_device(noise, data, noise_weight, data_weight):
    width = noise.shape[1] * C
    FQ = width // (Q * C)
    FS = X * FQ
    anywhere = pl.BlockSpec(memory_space=pl.ANY)
    dma = pltpu.SemaphoreType.DMA
    targets, pots = pl.pallas_call(
        functools.partial(kernel, width),
        out_shape=(
            jax.ShapeDtypeStruct((YL, 8, FS), BF16),
            jax.ShapeDtypeStruct((2, LANES), F32),
        ),
        in_specs=[anywhere] * 4,
        out_specs=(anywhere, anywhere),
        scratch_shapes=[
            pltpu.SMEM((8,), jnp.int32),
            pltpu.SMEM((32,), jnp.int32),
            pltpu.VMEM((YL, 8, FS + LANES), BF16),
            pltpu.VMEM((32, 2 * FS), BF16),
            pltpu.VMEM((2 * X, X, 8, FQ), BF16),
            pltpu.VMEM((Z, X, 8, FQ), BF16),
            pltpu.VMEM((1, LANES), F32),
            pltpu.VMEM((2, X, YL, 8, FS + LANES), BF16),
            pltpu.VMEM((2, 8 * Q, FS + LANES), BF16),
            pltpu.VMEM((Z, X, 8, FQ), BF16),
            pltpu.VMEM((2 * X, Z, X, 8, FQ), BF16),
            pltpu.VMEM((2 * X, Z * 8, FS), BF16),
            pltpu.VMEM((Z, YH, 1, LANES), F32),
            pltpu.VMEM((Y, 2, 8, LANES), F32),
            pltpu.VMEM((Y, 2, 8, LANES), F32),
            pltpu.VMEM((2, 8, LANES), F32),
            pltpu.VMEM((Z, 2, 8, LANES), F32),
            pltpu.VMEM((2, X, Y, 2, 8, LANES), F32),
            pltpu.VMEM((2, X, Y, 8, LANES), F32),
            pltpu.VMEM((2, X, Y, 8, LANES), F32),
            pltpu.VMEM((2, X, Z, 8, LANES), F32),
            pltpu.VMEM((LANES, C * 32), F32),
            pltpu.VMEM((YL, 8, FS), BF16),
            pltpu.VMEM((2, LANES), F32),
            dma((3 + YL,)),
        ] + [dma] * 5 + [dma((Z,))] + [dma] * 8 + [dma((3,))] * 2 + [dma] * 5 + [dma((Y,)), dma, dma((X,)), dma, dma, dma],
        compiler_params=pltpu.CompilerParams(
            collective_id=0, has_side_effects=True, vmem_limit_bytes=60 * 1024 * 1024
        ),
    )(noise_weight, data_weight, noise, data)
    targets = jnp.transpose(targets, (1, 0, 2)).reshape(8, YL * FS)
    return (targets, pots[0, 0:8], pots[1, 0:32])


def solution(mesh):
    placed = (P("row", "col"), P("col", "row"), P("row"), P("col"))
    return jax.shard_map(
        per_device,
        mesh=mesh,
        in_specs=placed,
        out_specs=(P("row", "col"), P("row"), P("col")),
        check_vma=False,
    )
```

```python
import functools
import math

import jax
import jax.numpy as jnp
from jax import lax
from jax.experimental import pallas as pl
from jax.experimental.pallas import tpu as pltpu
from jax.sharding import PartitionSpec as P

HALVES = 4
MESH = pl.DeviceIdType.MESH
F32 = jnp.float32
BF16 = jnp.bfloat16
LANES = 128
X, YL, Z, YH = 4, 4, 8, 2
Y = YH * YL
Q = YL * X
C = Z * YH
NT = (((1,), (1,)), ((), ()))


def kernel(
    width,
    nw_hbm, dw_hbm, noise_ref, data_ref,
    out_ref, npot_ref, dpot_ref,
    nw_ref, dw_ref, nstage, dvm, dstage, relay, wstage, nbuf, nmat, dcrit, tdata, dfull,
    wbuf, pbuf, abuf, bbuf, rbuf, gall, lbuf, vbuf, plan, turned, tbuf, npot, dpot,
    load, n1s, n1r, n2s, n2r, es, er, fs, fr, ts, tr, w1s, w1r, w2s, w2r, sib_s, sib_r,
    as_, ar, bs, br, gs, gr, hs, hr, os_, or_, ps,
):
    FQ = width // (Q * C)
    FS = X * FQ
    FH = FS // YH
    eps = 1.0 / math.sqrt(width)
    row = lax.axis_index("row")
    c = lax.axis_index("col")
    k = row % 2
    q = row // 2
    x = q % X
    yl = q // X
    z = c // YH
    yh = c % YH
    y = yh * YL + yl
    other = 1 - k

    def place(yl_, x_, k_):
        return (yl_ * X + x_) * 2 + k_

    sibling = (place(yl, x, other), c)

    def relay_of(j):
        return place(j // X, j % X, yh), z * YH + k

    def relay_source(i):
        return i * 2 + yh, z * YH + k

    to_self = k == yh
    n_self = jnp.where(to_self, 1, 0).astype(jnp.int32)

    def finish():
        def sent(ref, sem):
            pltpu.make_async_copy(ref, ref, sem).wait()

        @pl.when(to_self)
        def _():
            sent(dstage.at[pl.ds(0, Q - 1)], es)

        @pl.when(jnp.logical_not(to_self))
        def _():
            sent(dstage, es)

        sent(relay.at[pl.ds(0, Z - 1)], fs)
        sent(nstage.at[pl.ds(0, Y - 1)], n1s)
        sent(nbuf.at[k, pl.ds(0, X - 1)], n2s)
        sent(nbuf.at[k], sib_s.at[0])
        sent(wbuf.at[pl.ds(0, Z - 1), 0], w1s)
        sent(wbuf.at[:, yh], w2s)
        sent(pbuf.at[pl.ds(0, Y - 1)], as_)
        sent(tdata.at[pl.ds(0, X - 1)], ts)
        sent(rbuf.at[pl.ds(0, Z - 1)], bs)
        sent(gall.at[k, x, pl.ds(0, Y - 1)], gs)
        sent(gall.at[k, pl.ds(0, X - 1)], hs)
        sent(gall.at[k], sib_s.at[1])
        sent(tdata.at[pl.ds(0, X)], sib_s.at[2])
        sent(out_ref.at[pl.ds(0, Y - 1)], os_)
        sent(out_ref, or_)
        sent(npot_ref, ps.at[0])
        sent(dpot_ref, ps.at[1])

    loads = [
        pltpu.make_async_copy(nw_hbm, nw_ref, load.at[0]),
        pltpu.make_async_copy(dw_hbm, dw_ref, load.at[1]),
        pltpu.make_async_copy(data_ref, dvm, load.at[2]),
    ] + [
        pltpu.make_async_copy(
            noise_ref.at[:, pl.ds(t * FH, FH)], nstage.at[t, :, pl.ds(0, FH)], load.at[3 + t]
        )
        for t in range(Y)
    ]

    barrier = pltpu.get_barrier_semaphore()

    def greet(device):
        pl.semaphore_signal(barrier, inc=1, device_id=device, device_id_type=MESH)

    def greet_source(i, carry):
        device = relay_source(i)

        @pl.when(jnp.logical_or(device[0] != row, device[1] != c))
        def _():
            greet(device)

        return carry

    def greet_z(s, carry):
        greet((row, lax.rem(z + s, Z) * YH + yh))
        return carry

    def greet_y(s, carry):
        t = lax.rem(y + s, Y)
        greet((place(t % YL, x, k), z * YH + t // YL))
        return carry

    def greet_x(s, carry):
        greet((place(yl, lax.rem(x + s, X), k), c))
        return carry

    for copy in loads[2::-1]:
        copy.start()
    lax.fori_loop(0, Q, greet_source, 0)
    lax.fori_loop(1, Z, greet_z, 0)
    lax.fori_loop(1, Y, greet_y, 0)
    lax.fori_loop(1, X, greet_x, 0)
    greet(sibling)
    for copy in loads[3:]:
        copy.start()

    loads[2].wait()
    for j in range(Q):
        s, t = j // X, j % X
        for f in range(FH // FQ):
            at = s * FH + f * FQ
            dstage[j, f] = dvm[:, at:at + FQ].astype(F32)[8 * t:8 * t + 8].astype(BF16)

    pl.semaphore_wait(barrier, (Y - 1) + (X - 1) + (Z - 1) + 1 + Q - n_self)

    def send_data(j, carry):
        device = relay_of(j)
        is_self = jnp.logical_and(device[0] == row, device[1] == c)
        slot = q // YH

        @pl.when(is_self)
        def _():
            pltpu.make_async_copy(dstage.at[j], relay.at[slot, q % YH], er.at[slot]).start()

        @pl.when(jnp.logical_not(is_self))
        def _():
            pltpu.make_async_remote_copy(
                dstage.at[j], relay.at[slot, q % YH], es, er.at[slot],
                device_id=device, device_id_type=MESH,
            ).start()

        return carry

    lax.fori_loop(0, Q, send_data, 0)

    loads[0].wait()
    for copy in loads[3:]:
        copy.wait()

    rows8 = lax.broadcasted_iota(jnp.int32, (8, LANES), 0)
    lanes8 = lax.broadcasted_iota(jnp.int32, (8, LANES), 1)
    noise_w = jnp.zeros((8, LANES), jnp.int32)
    for i in range(8):
        noise_w = jnp.where(rows8 == i, nw_ref[i], noise_w)
    noise_w = noise_w.astype(F32)
    for t in range(Y):
        nf = nstage[t, :, 0:FH].astype(F32)
        sq = jnp.sum(nf * nf, axis=1, keepdims=True)
        hi = sq.astype(BF16).astype(F32)
        mid = (sq - hi).astype(BF16).astype(F32)
        lo = sq - hi - mid
        tail = jnp.where(lanes8 == 3, noise_w, 0.0)
        tail = jnp.where(lanes8 == 2, lo, tail)
        tail = jnp.where(lanes8 == 1, mid, tail)
        tail = jnp.where(lanes8 == 0, hi, tail)
        nstage[t, :, FH:FH + LANES] = tail.astype(BF16)

    def y_peer(t):
        return place(t % YL, x, k), z * YH + t // YL

    def send_noise_y(s, carry):
        t = lax.rem(y + s, Y)
        pltpu.make_async_remote_copy(
            nstage.at[t], nbuf.at[k, x, yl, yh], n1s, n1r,
            device_id=y_peer(t), device_id_type=MESH,
        ).start()
        return carry

    lax.fori_loop(1, Y, send_noise_y, 0)
    pltpu.make_async_copy(nstage.at[y], nbuf.at[k, x, yl, yh], n1r).start()

    loads[1].wait()
    lanes1 = lax.broadcasted_iota(jnp.int32, (1, LANES), 1)
    data_w = jnp.zeros((1, LANES), jnp.int32)
    for i in range(32):
        data_w = jnp.where(lanes1 == i, dw_ref[i], data_w)
    wstage[...] = data_w.astype(F32)

    def send_w(s, carry):
        t = lax.rem(z + s, Z)
        pltpu.make_async_remote_copy(
            wstage, wbuf.at[z, yh], w1s, w1r,
            device_id=(row, t * YH + yh), device_id_type=MESH,
        ).start()
        return carry

    lax.fori_loop(1, Z, send_w, 0)
    pltpu.make_async_copy(wstage, wbuf.at[z, yh], w1r).start()

    def arrived(ref, sem):
        pltpu.make_async_copy(ref, ref, sem).wait()

    def swap(ref, i):
        return pltpu.make_async_remote_copy(
            ref, ref, sib_s.at[i], sib_r.at[i], device_id=sibling, device_id_type=MESH
        )

    arrived(nbuf.at[k, x], n1r)

    def send_noise_x(s, carry):
        t = lax.rem(x + s, X)
        pltpu.make_async_remote_copy(
            nbuf.at[k, x], nbuf.at[k, x], n2s, n2r,
            device_id=(place(yl, t, k), c), device_id_type=MESH,
        ).start()
        return carry

    lax.fori_loop(1, X, send_noise_x, 0)

    def hand_on(i, carry):
        t = lax.rem(YH * yl + i, Z)
        arrived(relay.at[t], er.at[t])

        @pl.when(t == z)
        def _():
            pltpu.make_async_copy(relay.at[t], dcrit.at[z], fr).start()

        @pl.when(t != z)
        def _():
            pltpu.make_async_remote_copy(
                relay.at[t], dcrit.at[z], fs, fr,
                device_id=(row, t * YH + yh), device_id_type=MESH,
            ).start()

        return carry

    lax.fori_loop(0, Z, hand_on, 0)

    def noise_rows(core):
        for t in range(YH):
            part = nbuf[core, :, :, t].astype(F32).reshape(8 * Q, FH + LANES).astype(BF16)
            nmat[core, :, t * FH:(t + 1) * FH] = part[:, 0:FH]
            nmat[core, :, FS + t * LANES:FS + (t + 1) * LANES] = part[:, FH:FH + LANES]

    arrived(nbuf.at[k, pl.ds(0, X - 1)], n2r)
    noise_swap = swap(nbuf.at[k], 0)
    noise_swap.start()
    noise_rows(k)
    arrived(nbuf.at[other], sib_r.at[0])
    noise_rows(other)
    tail = nmat[:, :, FS:FS + YH * LANES].reshape(16 * Q, YH * LANES)
    tail_lane = lax.broadcasted_iota(jnp.int32, (8, YH * LANES), 1)
    pick_sq = jnp.where(tail_lane % LANES < 3, 1.0, 0.0).astype(BF16)
    pick_w = jnp.where(tail_lane == 3, 1.0, 0.0).astype(BF16)
    nsq = lax.dot_general(pick_sq, tail, NT, preferred_element_type=F32)[0:1, :]
    wa = lax.dot_general(pick_w, tail, NT, preferred_element_type=F32)[0:1, :]

    arrived(wbuf.at[:, yh], w1r)
    pltpu.make_async_remote_copy(
        wbuf.at[:, yh], wbuf.at[:, yh], w2s, w2r,
        device_id=(row, z * YH + 1 - yh), device_id_type=MESH,
    ).start()

    arrived(dcrit, fr)
    df = dcrit[...].astype(F32).reshape(Z, X, 8, FQ)
    part = jnp.sum(
        jnp.sum(df * df, axis=1).reshape(Z * 8, FQ), axis=1, keepdims=True
    ) + nsq
    dm = (df * -2.0)
    for f in range(X):
        part = part + lax.dot_general(
            dm[:, f].reshape(Z * 8, FQ).astype(BF16),
            nmat[:, :, f * FQ:(f + 1) * FQ].reshape(16 * Q, FQ),
            NT, preferred_element_type=F32,
        )
    for h in range(2):
        pbuf[:, h] = part[:, h * LANES:(h + 1) * LANES].reshape(Y, 8, LANES)

    def send_a(s, carry):
        t = lax.rem(y + s, Y)
        pltpu.make_async_remote_copy(
            pbuf.at[t], abuf.at[y], as_, ar, device_id=y_peer(t), device_id_type=MESH
        ).start()
        return carry

    lax.fori_loop(1, Y, send_a, 0)
    pltpu.make_async_copy(pbuf.at[y], abuf.at[y], ar).start()

    def send_features(s, carry):
        t = lax.rem(x + s, X)
        pltpu.make_async_remote_copy(
            dcrit, tdata.at[k * X + x], ts, tr,
            device_id=(place(yl, t, k), c), device_id_type=MESH,
        ).start()
        return carry

    lax.fori_loop(1, X, send_features, 0)
    pltpu.make_async_copy(dcrit, tdata.at[k * X + x], tr).start()

    log_a = jnp.log(wa / jnp.sum(wa, axis=1, keepdims=True))
    log_a = [log_a[:, h * LANES:(h + 1) * LANES] for h in range(2)]
    arrived(abuf, ar)
    total = abuf[0]
    for j in range(1, Y):
        total = total + abuf[j]
    bbuf[...] = total

    def send_b(s, carry):
        t = lax.rem(z + s, Z)
        pltpu.make_async_remote_copy(
            bbuf, rbuf.at[z], bs, br, device_id=(row, t * YH + yh), device_id_type=MESH
        ).start()
        return carry

    lax.fori_loop(1, Z, send_b, 0)
    pltpu.make_async_copy(bbuf, rbuf.at[z], br).start()

    arrived(rbuf, br)
    total = rbuf[0]
    for j in range(1, Z):
        total = total + rbuf[j]
    gall[k, x, y] = total * (-1.0 / (width * eps))

    def send_g(s, carry):
        t = lax.rem(y + s, Y)
        pltpu.make_async_remote_copy(
            gall.at[k, x, y], gall.at[k, x, y], gs, gr.at[y],
            device_id=y_peer(t), device_id_type=MESH,
        ).start()
        return carry

    lax.fori_loop(1, Y, send_g, 0)

    def send_x(piece):
        for s in range(1, X):
            t = lax.rem(x + s, X)
            pltpu.make_async_remote_copy(
                gall.at[k, x, piece], gall.at[k, x, piece], hs, hr.at[x],
                device_id=(place(yl, t, k), c), device_id_type=MESH,
            ).start()

    send_x(y)

    arrived(wbuf.at[:, 1 - yh], w2r)
    wb = wbuf[...].reshape(C, 1, LANES)
    w_sum = jnp.sum(jnp.sum(wb, axis=0), axis=1, keepdims=True)
    spot = lax.broadcasted_iota(jnp.int32, (C, 32, LANES), 1) == lax.broadcasted_iota(
        jnp.int32, (C, 32, LANES), 2
    )
    wb = jnp.where(spot, wb, 0.0).reshape(C * 32, LANES).astype(BF16)
    wb = jnp.dot(wb, jnp.ones((LANES, LANES), BF16), preferred_element_type=F32)
    log_b = jnp.log(wb / w_sum).reshape(Z, YH, X, 8, LANES)
    for a in range(YH):
        for b in range(X):
            lbuf[a, b] = log_b[:, a, b]
    def data_rows(core):
        def step(i, carry):
            g = core * X + i
            for f in range(X):
                cut = tdata[g, :, f // YH, f % YH].astype(F32).reshape(Z * 8, FQ)
                dfull[g, :, f * FQ:(f + 1) * FQ] = cut.astype(BF16)
            return carry

        lax.fori_loop(0, X, step, 0)

    own_rows = tdata.at[pl.ds(k * X, X)]
    other_rows = tdata.at[pl.ds(other * X, X)]
    arrived(own_rows, tr)
    rows_swap = swap(own_rows, 2)
    rows_swap.start()
    data_rows(k)

    def gather_y(i, carry):
        d = (i + 1) // 2
        t = lax.rem(y + jnp.where(i % 2 == 1, d, Y - d), Y)
        arrived(gall.at[k, x, t], gr.at[t])
        send_x(t)
        return carry

    lax.fori_loop(1, Y, gather_y, 0)

    def send_core(t):
        pltpu.make_async_remote_copy(
            gall.at[k, t], gall.at[k, t], sib_s.at[1], sib_r.at[1],
            device_id=sibling, device_id_type=MESH,
        ).start()

    send_core(x)

    def gather_x(s, carry):
        t = lax.rem(x + jnp.where(s == 2, 3, jnp.where(s == 3, 2, 1)), X)
        arrived(gall.at[k, t], hr.at[t])
        send_core(t)
        return carry

    lax.fori_loop(1, X, gather_x, 0)
    arrived(other_rows, sib_r.at[2])
    data_rows(other)
    arrived(gall.at[other], sib_r.at[1])

    def parts(i):
        return i // X, i % X

    def peak_step(i, peak):
        a, b = parts(i)
        return jnp.maximum(peak, jnp.max(gall[a, b], axis=0))

    peak = jnp.full((2, 8, LANES), -jnp.inf, F32)
    for i in range(2 * X):
        peak = peak_step(i, peak)
    for rounds in range(HALVES // 2):
        top = jnp.max(peak, axis=1, keepdims=True)

        def noise_step(i, acc):
            a, b = parts(i)
            s = gall[a, b]
            if rounds:
                s = s + vbuf[a, b][:, None]
            return acc + jnp.sum(jnp.exp(s - top), axis=0)

        acc = jnp.zeros((2, 8, LANES), F32)
        for i in range(2 * X):
            acc = noise_step(i, acc)
        lse = top + jnp.log(jnp.sum(acc, axis=1, keepdims=True))
        u = jnp.concatenate([(log_a[h] - lse[h])[None] for h in range(2)], axis=0)

        def data_step(i, peak):
            a, b = parts(i)
            s = gall[a, b]
            w = s + u
            m = jnp.max(jnp.max(w, axis=1), axis=2, keepdims=True)
            e = jnp.sum(jnp.sum(jnp.exp(w - m[:, None]), axis=1), axis=2, keepdims=True)
            v = lbuf[a, b] - (m + jnp.log(e))
            vbuf[a, b] = v
            return jnp.maximum(peak, jnp.max(s + v[:, None], axis=0))

        peak = jnp.full((2, 8, LANES), -jnp.inf, F32)
        for i in range(2 * X):
            peak = data_step(i, peak)

    own_u = jnp.where(k == 0, u[0], u[1])
    for i in range(2 * X):
        a, b = parts(i)
        plan[a, b] = jnp.exp(gall[a, b, :, k] + own_u + vbuf[a, b])
    turned[...] = jnp.transpose(plan[...].reshape(C * 32, LANES), (1, 0))
    p = turned[pl.ds(pl.multiple_of(x * YL * 8, YL * 8), YL * 8), :]
    mass = jnp.sum(p, axis=1, keepdims=True)
    value = jnp.dot(
        p.astype(BF16), dfull[...].reshape(C * 32, FS), preferred_element_type=F32
    ) / mass
    for t in range(YH):
        tbuf[t] = value[:, t * FH:(t + 1) * FH].reshape(YL, 8, FH).astype(BF16)

    def send_t(s, carry):
        t = lax.rem(y + s, Y)
        pltpu.make_async_remote_copy(
            tbuf.at[t // YL, t % YL], out_ref.at[y], os_, or_,
            device_id=y_peer(t), device_id_type=MESH,
        ).start()
        return carry

    lax.fori_loop(1, Y, send_t, 0)
    pltpu.make_async_copy(tbuf.at[yh, yl], out_ref.at[y], or_).start()

    mine = own_u[:, 0:8]
    for t in range(1, Q):
        mine = jnp.where(x * YL + yl == t, own_u[:, 8 * t:8 * t + 8], mine)
    npot[...] = mine * eps
    lanes4 = lax.broadcasted_iota(jnp.int32, (X, 8, LANES), 2)
    index4 = lax.broadcasted_iota(jnp.int32, (X, 8, LANES), 0) * 8 + lax.broadcasted_iota(
        jnp.int32, (X, 8, LANES), 1
    )
    block = jnp.where(lanes4 == index4, vbuf[yh, :, z], 0.0)
    block = jnp.sum(jnp.sum(block, axis=0), axis=0, keepdims=True)
    dpot[...] = block[:, 0:32] * eps
    pltpu.make_async_copy(npot, npot_ref, ps.at[0]).start()
    pltpu.make_async_copy(dpot, dpot_ref, ps.at[1]).start()
    finish()


def per_device(noise, data, noise_weight, data_weight):
    width = noise.shape[1] * C
    FQ = width // (Q * C)
    FS = X * FQ
    anywhere = pl.BlockSpec(memory_space=pl.ANY)
    dma = pltpu.SemaphoreType.DMA
    targets, noise_pot, data_pot = pl.pallas_call(
        functools.partial(kernel, width),
        out_shape=(
            jax.ShapeDtypeStruct((Y, 8, FS // YH), BF16),
            jax.ShapeDtypeStruct((1, 8), F32),
            jax.ShapeDtypeStruct((1, 32), F32),
        ),
        in_specs=[anywhere] * 4,
        out_specs=(anywhere, anywhere, anywhere),
        scratch_shapes=[
            pltpu.SMEM((8,), jnp.int32),
            pltpu.SMEM((32,), jnp.int32),
            pltpu.VMEM((Y, 8, FS // YH + LANES), BF16),
            pltpu.VMEM((32, 2 * FS), BF16),
            pltpu.VMEM((Q, X // YH, 8, FQ), BF16),
            pltpu.VMEM((Z, YH, X // YH, 8, FQ), BF16),
            pltpu.VMEM((1, LANES), F32),
            pltpu.VMEM((2, X, YL, YH, 8, FS // YH + LANES), BF16),
            pltpu.VMEM((2, 8 * Q, FS + YH * LANES), BF16),
            pltpu.VMEM((Z, YH, X // YH, 8, FQ), BF16),
            pltpu.VMEM((2 * X, Z, YH, X // YH, 8, FQ), BF16),
            pltpu.VMEM((2 * X, Z * 8, FS), BF16),
            pltpu.VMEM((Z, YH, 1, LANES), F32),
            pltpu.VMEM((Y, 2, 8, LANES), F32),
            pltpu.VMEM((Y, 2, 8, LANES), F32),
            pltpu.VMEM((2, 8, LANES), F32),
            pltpu.VMEM((Z, 2, 8, LANES), F32),
            pltpu.VMEM((2, X, Y, 2, 8, LANES), F32),
            pltpu.VMEM((2, X, Y, 8, LANES), F32),
            pltpu.VMEM((2, X, Y, 8, LANES), F32),
            pltpu.VMEM((2, X, Z, 8, LANES), F32),
            pltpu.VMEM((LANES, C * 32), F32),
            pltpu.VMEM((YH, YL, 8, FS // YH), BF16),
            pltpu.VMEM((1, 8), F32),
            pltpu.VMEM((1, 32), F32),
            dma((3 + Y,)),
        ] + [dma] * 5 + [dma((Z,))] + [dma] * 8 + [dma((3,))] * 2 + [dma] * 5 + [dma((Y,)), dma, dma((X,)), dma, dma, dma((2,))],
        compiler_params=pltpu.CompilerParams(
            collective_id=0, has_side_effects=True, vmem_limit_bytes=60 * 1024 * 1024
        ),
    )(noise_weight, data_weight, noise, data)
    targets = jnp.transpose(targets, (1, 0, 2)).reshape(8, YL * FS)
    return (targets, noise_pot.reshape(8), data_pot.reshape(32))


def solution(mesh):
    placed = (P("row", "col"), P("col", "row"), P("row"), P("col"))
    return jax.shard_map(
        per_device,
        mesh=mesh,
        in_specs=placed,
        out_specs=(P("row", "col"), P("row"), P("col")),
        check_vma=False,
    )
```

```python
import functools
import math

import jax
import jax.numpy as jnp
from jax import lax
from jax.experimental import pallas as pl
from jax.experimental.pallas import tpu as pltpu
from jax.sharding import PartitionSpec as P

HALVES = 4
MESH = pl.DeviceIdType.MESH
F32 = jnp.float32
BF16 = jnp.bfloat16
LANES = 128
X, YL, Z, YH = 4, 4, 8, 2
Y = YH * YL
Q = YL * X
C = Z * YH
NT = (((1,), (1,)), ((), ()))


def kernel(
    width,
    nw_hbm, dw_hbm, noise_ref, data_ref,
    out_ref, npot_ref, dpot_ref,
    nw_ref, dw_ref, nstage, dvm, dstage, relay, wstage, nbuf, nmat, dcrit, tdata, dfull,
    wbuf, pbuf, abuf, bbuf, rbuf, gall, lbuf, vbuf, plan, turned, tbuf, npot, dpot,
    load, n1s, n1r, n2s, n2r, es, er, fs, fr, ts, tr, w1s, w1r, w2s, w2r, sib_s, sib_r,
    as_, ar, bs, br, gs, gr, hs, hr, os_, or_, ps,
):
    FQ = width // (Q * C)
    FS = X * FQ
    eps = 1.0 / math.sqrt(width)
    row = lax.axis_index("row")
    c = lax.axis_index("col")
    k = row % 2
    q = row // 2
    x = q % X
    yl = q // X
    z = c // YH
    yh = c % YH
    y = yh * YL + yl
    other = 1 - k

    def place(yl_, x_, k_):
        return (yl_ * X + x_) * 2 + k_

    sibling = (place(yl, x, other), c)

    def relay_of(j):
        return place(2 * k + j // X, j % X, yh), z * YH + x % YH

    def relay_source(i):
        f = YH * i + yh
        return place(f // X, f % X, yl // 2), z * YH + k

    to_self = jnp.logical_and(jnp.logical_and(k == yl // 2, yh == k), x % YH == yh)
    n_self = jnp.where(to_self, 1, 0).astype(jnp.int32)

    def finish():
        def sent(ref, sem):
            pltpu.make_async_copy(ref, ref, sem).wait()

        @pl.when(to_self)
        def _():
            sent(dstage.at[pl.ds(0, 2 * X - 1)], es)

        @pl.when(jnp.logical_not(to_self))
        def _():
            sent(dstage, es)

        sent(relay.at[pl.ds(0, Z - 1)], fs)
        sent(nstage.at[pl.ds(0, YL - 1)], n1s)
        sent(nbuf.at[k, pl.ds(0, X - 1)], n2s)
        sent(nbuf.at[k], sib_s.at[0])
        sent(wbuf.at[pl.ds(0, Z - 1), 0], w1s)
        sent(wbuf.at[:, yh], w2s)
        sent(pbuf.at[pl.ds(0, Y - 1)], as_)
        sent(tdata.at[pl.ds(0, X - 1)], ts)
        sent(rbuf.at[pl.ds(0, Z - 1)], bs)
        sent(gall.at[k, x, pl.ds(0, Y - 1)], gs)
        sent(gall.at[k, pl.ds(0, X - 1)], hs)
        sent(gall.at[k], sib_s.at[1])
        sent(tdata.at[pl.ds(0, X)], sib_s.at[2])
        sent(out_ref.at[pl.ds(0, YL - 1)], os_)
        sent(out_ref, or_)
        sent(npot_ref, ps.at[0])
        sent(dpot_ref, ps.at[1])

    loads = [
        pltpu.make_async_copy(nw_hbm, nw_ref, load.at[0]),
        pltpu.make_async_copy(dw_hbm, dw_ref, load.at[1]),
        pltpu.make_async_copy(data_ref, dvm, load.at[2]),
    ] + [
        pltpu.make_async_copy(
            noise_ref.at[:, pl.ds(t * FS, FS)], nstage.at[t, :, pl.ds(0, FS)], load.at[3 + t]
        )
        for t in range(YL)
    ]

    barrier = pltpu.get_barrier_semaphore()

    def greet(device):
        pl.semaphore_signal(barrier, inc=1, device_id=device, device_id_type=MESH)

    def greet_source(i, carry):
        device = relay_source(i)

        @pl.when(jnp.logical_or(device[0] != row, device[1] != c))
        def _():
            greet(device)

        return carry

    def greet_z(s, carry):
        greet((row, lax.rem(z + s, Z) * YH + yh))
        return carry

    def greet_y(s, carry):
        t = lax.rem(y + s, Y)
        greet((place(t % YL, x, k), z * YH + t // YL))
        return carry

    def greet_x(s, carry):
        greet((place(yl, lax.rem(x + s, X), k), c))
        return carry

    for copy in loads[2::-1]:
        copy.start()
    lax.fori_loop(0, Z, greet_source, 0)
    lax.fori_loop(1, Z, greet_z, 0)
    lax.fori_loop(1, Y, greet_y, 0)
    lax.fori_loop(1, X, greet_x, 0)
    greet(sibling)
    for copy in loads[3:]:
        copy.start()

    loads[2].wait()
    for j in range(2 * X):
        s, t = j // X, j % X
        for f in range(X):
            cut = dvm[:, s * FS + f * FQ:s * FS + (f + 1) * FQ].astype(F32)
            dstage[j, f] = cut[8 * t:8 * t + 8].astype(BF16)
    pl.semaphore_wait(barrier, (Y - 1) + (X - 1) + (Z - 1) + 1 + 2 * X - n_self)

    def send_data(j, carry):
        device = relay_of(j)
        is_self = jnp.logical_and(device[0] == row, device[1] == c)
        slot = q // YH

        @pl.when(is_self)
        def _():
            pltpu.make_async_copy(dstage.at[j], relay.at[slot], er.at[slot]).start()

        @pl.when(jnp.logical_not(is_self))
        def _():
            pltpu.make_async_remote_copy(
                dstage.at[j], relay.at[slot], es, er.at[slot],
                device_id=device, device_id_type=MESH,
            ).start()

        return carry

    lax.fori_loop(0, 2 * X, send_data, 0)

    loads[0].wait()
    for copy in loads[3:]:
        copy.wait()

    rows8 = lax.broadcasted_iota(jnp.int32, (8, LANES), 0)
    lanes8 = lax.broadcasted_iota(jnp.int32, (8, LANES), 1)
    noise_w = jnp.zeros((8, LANES), jnp.int32)
    for i in range(8):
        noise_w = jnp.where(rows8 == i, nw_ref[i], noise_w)
    noise_w = noise_w.astype(F32)
    for t in range(YL):
        nf = nstage[t, :, 0:FS].astype(F32)
        sq = jnp.sum(nf * nf, axis=1, keepdims=True)
        hi = sq.astype(BF16).astype(F32)
        mid = (sq - hi).astype(BF16).astype(F32)
        lo = sq - hi - mid
        tail = jnp.where(lanes8 == 3, noise_w, 0.0)
        tail = jnp.where(lanes8 == 2, lo, tail)
        tail = jnp.where(lanes8 == 1, mid, tail)
        tail = jnp.where(lanes8 == 0, hi, tail)
        nstage[t, :, FS:FS + LANES] = tail.astype(BF16)

    def send_noise_y(s, carry):
        t = lax.rem(yl + s, YL)
        pltpu.make_async_remote_copy(
            nstage.at[t], nbuf.at[k, x, yl], n1s, n1r,
            device_id=(place(t, x, k), c), device_id_type=MESH,
        ).start()
        return carry

    lax.fori_loop(1, YL, send_noise_y, 0)
    pltpu.make_async_copy(nstage.at[yl], nbuf.at[k, x, yl], n1r).start()

    loads[1].wait()
    lanes1 = lax.broadcasted_iota(jnp.int32, (1, LANES), 1)
    data_w = jnp.zeros((1, LANES), jnp.int32)
    for i in range(32):
        data_w = jnp.where(lanes1 == i, dw_ref[i], data_w)
    wstage[...] = data_w.astype(F32)

    def send_w(s, carry):
        t = lax.rem(z + s, Z)
        pltpu.make_async_remote_copy(
            wstage, wbuf.at[z, yh], w1s, w1r,
            device_id=(row, t * YH + yh), device_id_type=MESH,
        ).start()
        return carry

    lax.fori_loop(1, Z, send_w, 0)
    pltpu.make_async_copy(wstage, wbuf.at[z, yh], w1r).start()

    def arrived(ref, sem):
        pltpu.make_async_copy(ref, ref, sem).wait()

    def swap(ref, i):
        return pltpu.make_async_remote_copy(
            ref, ref, sib_s.at[i], sib_r.at[i], device_id=sibling, device_id_type=MESH
        )

    arrived(nbuf.at[k, x], n1r)

    def send_noise_x(s, carry):
        t = lax.rem(x + s, X)
        pltpu.make_async_remote_copy(
            nbuf.at[k, x], nbuf.at[k, x], n2s, n2r,
            device_id=(place(yl, t, k), c), device_id_type=MESH,
        ).start()
        return carry

    lax.fori_loop(1, X, send_noise_x, 0)

    def hand_on(i, carry):
        t = lax.rem(YH * yl + i, Z)
        arrived(relay.at[t], er.at[t])

        @pl.when(t == z)
        def _():
            pltpu.make_async_copy(relay.at[t], dcrit.at[z], fr).start()

        @pl.when(t != z)
        def _():
            pltpu.make_async_remote_copy(
                relay.at[t], dcrit.at[z], fs, fr,
                device_id=(row, t * YH + yh), device_id_type=MESH,
            ).start()

        return carry

    lax.fori_loop(0, Z, hand_on, 0)

    def noise_rows(core):
        for t in range(2):
            part = nbuf[core, 2 * t:2 * t + 2].astype(F32)
            nmat[core, t * 4 * Q:(t + 1) * 4 * Q, :] = part.reshape(4 * Q, FS + LANES).astype(BF16)

    arrived(nbuf.at[k, pl.ds(0, X - 1)], n2r)
    noise_swap = swap(nbuf.at[k], 0)
    noise_swap.start()
    noise_rows(k)
    arrived(nbuf.at[other], sib_r.at[0])
    noise_rows(other)
    tail = nmat[:, :, FS:FS + LANES].reshape(16 * Q, LANES)
    pick_sq = jnp.where(lanes8 < 3, 1.0, 0.0).astype(BF16)
    pick_w = jnp.where(lanes8 == 3, 1.0, 0.0).astype(BF16)
    nsq = lax.dot_general(pick_sq, tail, NT, preferred_element_type=F32)[0:1, :]
    wa = lax.dot_general(pick_w, tail, NT, preferred_element_type=F32)[0:1, :]

    arrived(wbuf.at[:, yh], w1r)
    pltpu.make_async_remote_copy(
        wbuf.at[:, yh], wbuf.at[:, yh], w2s, w2r,
        device_id=(row, z * YH + 1 - yh), device_id_type=MESH,
    ).start()

    arrived(dcrit, fr)
    df = dcrit[...].astype(F32)
    part = jnp.sum(
        jnp.sum(df * df, axis=1).reshape(Z * 8, FQ), axis=1, keepdims=True
    ) + nsq
    dm = (df * -2.0)
    for f in range(X):
        part = part + lax.dot_general(
            dm[:, f].reshape(Z * 8, FQ).astype(BF16),
            nmat[:, :, f * FQ:(f + 1) * FQ].reshape(16 * Q, FQ),
            NT, preferred_element_type=F32,
        )
    for h in range(2):
        pbuf[:, h] = part[:, h * LANES:(h + 1) * LANES].reshape(Y, 8, LANES)

    def y_peer(t):
        return place(t % YL, x, k), z * YH + t // YL

    def send_a(s, carry):
        t = lax.rem(y + s, Y)
        pltpu.make_async_remote_copy(
            pbuf.at[t], abuf.at[y], as_, ar, device_id=y_peer(t), device_id_type=MESH
        ).start()
        return carry

    lax.fori_loop(1, Y, send_a, 0)
    pltpu.make_async_copy(pbuf.at[y], abuf.at[y], ar).start()

    def send_features(s, carry):
        t = lax.rem(x + s, X)
        pltpu.make_async_remote_copy(
            dcrit, tdata.at[k * X + x], ts, tr,
            device_id=(place(yl, t, k), c), device_id_type=MESH,
        ).start()
        return carry

    lax.fori_loop(1, X, send_features, 0)
    pltpu.make_async_copy(dcrit, tdata.at[k * X + x], tr).start()

    log_a = jnp.log(wa / jnp.sum(wa, axis=1, keepdims=True))
    log_a = [log_a[:, h * LANES:(h + 1) * LANES] for h in range(2)]
    arrived(abuf, ar)
    total = abuf[0]
    for j in range(1, Y):
        total = total + abuf[j]
    bbuf[...] = total

    def send_b(s, carry):
        t = lax.rem(z + s, Z)
        pltpu.make_async_remote_copy(
            bbuf, rbuf.at[z], bs, br, device_id=(row, t * YH + yh), device_id_type=MESH
        ).start()
        return carry

    lax.fori_loop(1, Z, send_b, 0)
    pltpu.make_async_copy(bbuf, rbuf.at[z], br).start()

    arrived(rbuf, br)
    total = rbuf[0]
    for j in range(1, Z):
        total = total + rbuf[j]
    gall[k, x, y] = total * (-1.0 / (width * eps))

    def send_g(s, carry):
        t = lax.rem(y + s, Y)
        pltpu.make_async_remote_copy(
            gall.at[k, x, y], gall.at[k, x, y], gs, gr.at[y],
            device_id=y_peer(t), device_id_type=MESH,
        ).start()
        return carry

    lax.fori_loop(1, Y, send_g, 0)

    def send_x(piece):
        for s in range(1, X):
            t = lax.rem(x + s, X)
            pltpu.make_async_remote_copy(
                gall.at[k, x, piece], gall.at[k, x, piece], hs, hr.at[x],
                device_id=(place(yl, t, k), c), device_id_type=MESH,
            ).start()

    send_x(y)

    arrived(wbuf.at[:, 1 - yh], w2r)
    wb = wbuf[...].reshape(C, 1, LANES)
    w_sum = jnp.sum(jnp.sum(wb, axis=0), axis=1, keepdims=True)
    spot = lax.broadcasted_iota(jnp.int32, (C, 32, LANES), 1) == lax.broadcasted_iota(
        jnp.int32, (C, 32, LANES), 2
    )
    wb = jnp.where(spot, wb, 0.0).reshape(C * 32, LANES).astype(BF16)
    wb = jnp.dot(wb, jnp.ones((LANES, LANES), BF16), preferred_element_type=F32)
    log_b = jnp.log(wb / w_sum).reshape(Z, YH, X, 8, LANES)
    for a in range(YH):
        for b in range(X):
            lbuf[a, b] = log_b[:, a, b]
    def data_rows(core):
        def step(i, carry):
            g = core * X + i
            for f in range(X):
                cut = tdata[g, :, f].astype(F32).reshape(Z * 8, FQ)
                dfull[g, :, f * FQ:(f + 1) * FQ] = cut.astype(BF16)
            return carry

        lax.fori_loop(0, X, step, 0)

    own_rows = tdata.at[pl.ds(k * X, X)]
    other_rows = tdata.at[pl.ds(other * X, X)]
    arrived(own_rows, tr)
    rows_swap = swap(own_rows, 2)
    rows_swap.start()
    data_rows(k)

    def gather_y(i, carry):
        d = (i + 1) // 2
        t = lax.rem(y + jnp.where(i % 2 == 1, d, Y - d), Y)
        arrived(gall.at[k, x, t], gr.at[t])
        send_x(t)
        return carry

    lax.fori_loop(1, Y, gather_y, 0)

    def send_core(t):
        pltpu.make_async_remote_copy(
            gall.at[k, t], gall.at[k, t], sib_s.at[1], sib_r.at[1],
            device_id=sibling, device_id_type=MESH,
        ).start()

    send_core(x)

    def gather_x(s, carry):
        t = lax.rem(x + jnp.where(s == 2, 3, jnp.where(s == 3, 2, 1)), X)
        arrived(gall.at[k, t], hr.at[t])
        send_core(t)
        return carry

    lax.fori_loop(1, X, gather_x, 0)
    arrived(other_rows, sib_r.at[2])
    data_rows(other)
    arrived(gall.at[other], sib_r.at[1])

    def parts(i):
        return i // X, i % X

    def peak_step(i, peak):
        a, b = parts(i)
        return jnp.maximum(peak, jnp.max(gall[a, b], axis=0))

    peak = jnp.full((2, 8, LANES), -jnp.inf, F32)
    for i in range(2 * X):
        peak = peak_step(i, peak)
    for rounds in range(HALVES // 2):
        top = jnp.max(peak, axis=1, keepdims=True)

        def noise_step(i, acc):
            a, b = parts(i)
            s = gall[a, b]
            if rounds:
                s = s + vbuf[a, b][:, None]
            return acc + jnp.sum(jnp.exp(s - top), axis=0)

        acc = jnp.zeros((2, 8, LANES), F32)
        for i in range(2 * X):
            acc = noise_step(i, acc)
        lse = top + jnp.log(jnp.sum(acc, axis=1, keepdims=True))
        u = jnp.concatenate([(log_a[h] - lse[h])[None] for h in range(2)], axis=0)

        def data_step(i, peak):
            a, b = parts(i)
            s = gall[a, b]
            w = s + u
            m = jnp.max(jnp.max(w, axis=1), axis=2, keepdims=True)
            e = jnp.sum(jnp.sum(jnp.exp(w - m[:, None]), axis=1), axis=2, keepdims=True)
            v = lbuf[a, b] - (m + jnp.log(e))
            vbuf[a, b] = v
            return jnp.maximum(peak, jnp.max(s + v[:, None], axis=0))

        peak = jnp.full((2, 8, LANES), -jnp.inf, F32)
        for i in range(2 * X):
            peak = data_step(i, peak)

    own_u = jnp.where(k == 0, u[0], u[1])
    for i in range(2 * X):
        a, b = parts(i)
        plan[a, b] = jnp.exp(gall[a, b, :, k] + own_u + vbuf[a, b])
    turned[...] = jnp.transpose(plan[...].reshape(C * 32, LANES), (1, 0))
    p = turned[pl.ds(pl.multiple_of(x * YL * 8, YL * 8), YL * 8), :]
    mass = jnp.sum(p, axis=1, keepdims=True)
    value = jnp.dot(
        p.astype(BF16), dfull[...].reshape(C * 32, FS), preferred_element_type=F32
    ) / mass
    tbuf[...] = value.reshape(YL, 8, FS).astype(BF16)

    def send_t(s, carry):
        t = lax.rem(yl + s, YL)
        pltpu.make_async_remote_copy(
            tbuf.at[t], out_ref.at[yl], os_, or_,
            device_id=(place(t, x, k), c), device_id_type=MESH,
        ).start()
        return carry

    lax.fori_loop(1, YL, send_t, 0)
    pltpu.make_async_copy(tbuf.at[yl], out_ref.at[yl], or_).start()

    mine = own_u[:, 0:8]
    for t in range(1, Q):
        mine = jnp.where(x * YL + yl == t, own_u[:, 8 * t:8 * t + 8], mine)
    npot[...] = mine * eps
    lanes4 = lax.broadcasted_iota(jnp.int32, (X, 8, LANES), 2)
    index4 = lax.broadcasted_iota(jnp.int32, (X, 8, LANES), 0) * 8 + lax.broadcasted_iota(
        jnp.int32, (X, 8, LANES), 1
    )
    block = jnp.where(lanes4 == index4, vbuf[yh, :, z], 0.0)
    block = jnp.sum(jnp.sum(block, axis=0), axis=0, keepdims=True)
    dpot[...] = block[:, 0:32] * eps
    pltpu.make_async_copy(npot, npot_ref, ps.at[0]).start()
    pltpu.make_async_copy(dpot, dpot_ref, ps.at[1]).start()
    finish()


def leave(targets_ref, npot_ref, dpot_ref, out_ref, nout_ref, dout_ref, held, npot, dpot, into, out):
    width = targets_ref.shape[2]
    sources = [npot_ref, dpot_ref] + [targets_ref.at[t] for t in range(YL)]
    places = [npot, dpot] + [held.at[t] for t in range(YL)]
    results = [nout_ref, dout_ref] + [
        out_ref.at[:, pl.ds(t * width, width)] for t in range(YL)
    ]
    count = len(places)
    first = [pltpu.make_async_copy(sources[i], places[i], into.at[i]) for i in range(count)]
    second = [pltpu.make_async_copy(places[i], results[i], out.at[i]) for i in range(count)]
    for copy in first:
        copy.start()
    for i in range(count):
        first[i].wait()
        second[i].start()
    for copy in second:
        copy.wait()


def per_device(noise, data, noise_weight, data_weight):
    width = noise.shape[1] * C
    FQ = width // (Q * C)
    FS = X * FQ
    anywhere = pl.BlockSpec(memory_space=pl.ANY)
    dma = pltpu.SemaphoreType.DMA
    targets, noise_pot, data_pot = pl.pallas_call(
        functools.partial(kernel, width),
        out_shape=(
            jax.ShapeDtypeStruct((YL, 8, FS), BF16),
            jax.ShapeDtypeStruct((1, 8), F32),
            jax.ShapeDtypeStruct((1, 32), F32),
        ),
        in_specs=[anywhere] * 4,
        out_specs=(anywhere, anywhere, anywhere),
        scratch_shapes=[
            pltpu.SMEM((8,), jnp.int32),
            pltpu.SMEM((32,), jnp.int32),
            pltpu.VMEM((YL, 8, FS + LANES), BF16),
            pltpu.VMEM((32, 2 * FS), BF16),
            pltpu.VMEM((2 * X, X, 8, FQ), BF16),
            pltpu.VMEM((Z, X, 8, FQ), BF16),
            pltpu.VMEM((1, LANES), F32),
            pltpu.VMEM((2, X, YL, 8, FS + LANES), BF16),
            pltpu.VMEM((2, 8 * Q, FS + LANES), BF16),
            pltpu.VMEM((Z, X, 8, FQ), BF16),
            pltpu.VMEM((2 * X, Z, X, 8, FQ), BF16),
            pltpu.VMEM((2 * X, Z * 8, FS), BF16),
            pltpu.VMEM((Z, YH, 1, LANES), F32),
            pltpu.VMEM((Y, 2, 8, LANES), F32),
            pltpu.VMEM((Y, 2, 8, LANES), F32),
            pltpu.VMEM((2, 8, LANES), F32),
            pltpu.VMEM((Z, 2, 8, LANES), F32),
            pltpu.VMEM((2, X, Y, 2, 8, LANES), F32),
            pltpu.VMEM((2, X, Y, 8, LANES), F32),
            pltpu.VMEM((2, X, Y, 8, LANES), F32),
            pltpu.VMEM((2, X, Z, 8, LANES), F32),
            pltpu.VMEM((LANES, C * 32), F32),
            pltpu.VMEM((YL, 8, FS), BF16),
            pltpu.VMEM((1, 8), F32),
            pltpu.VMEM((1, 32), F32),
            dma((3 + YL,)),
        ] + [dma] * 5 + [dma((Z,))] + [dma] * 8 + [dma((3,))] * 2 + [dma] * 5 + [dma((Y,)), dma, dma((X,)), dma, dma, dma((2,))],
        compiler_params=pltpu.CompilerParams(
            collective_id=0, has_side_effects=True, vmem_limit_bytes=60 * 1024 * 1024
        ),
    )(noise_weight, data_weight, noise, data)
    targets, noise_pot, data_pot = pl.pallas_call(
        leave,
        out_shape=(
            jax.ShapeDtypeStruct((8, YL * FS), BF16),
            jax.ShapeDtypeStruct((1, 8), F32),
            jax.ShapeDtypeStruct((1, 32), F32),
        ),
        in_specs=[anywhere] * 3,
        out_specs=(anywhere, anywhere, anywhere),
        scratch_shapes=[
            pltpu.VMEM((YL, 8, FS), BF16),
            pltpu.VMEM((1, 8), F32),
            pltpu.VMEM((1, 32), F32),
            dma((YL + 2,)),
            dma((YL + 2,)),
        ],
        compiler_params=pltpu.CompilerParams(vmem_limit_bytes=60 * 1024 * 1024),
    )(targets, noise_pot, data_pot)
    return (targets, noise_pot.reshape(8), data_pot.reshape(32))


def solution(mesh):
    placed = (P("row", "col"), P("col", "row"), P("row"), P("col"))
    return jax.shard_map(
        per_device,
        mesh=mesh,
        in_specs=placed,
        out_specs=(P("row", "col"), P("row"), P("col")),
        check_vma=False,
    )
```

```python
import functools
import math

import jax
import jax.numpy as jnp
from jax import lax
from jax.experimental import pallas as pl
from jax.experimental.pallas import tpu as pltpu
from jax.sharding import PartitionSpec as P

HALVES = 4
MESH = pl.DeviceIdType.MESH
F32 = jnp.float32
BF16 = jnp.bfloat16
LANES = 128
X, YL, Z, YH = 4, 4, 8, 2
Y = YH * YL
Q = YL * X
C = Z * YH
NT = (((1,), (1,)), ((), ()))


def kernel(
    width,
    nw_hbm, dw_hbm, noise_ref, data_ref,
    out_ref, npot_ref, dpot_ref,
    nw_ref, dw_ref, nstage, dvm, dstage, relay, wstage, nbuf, nmat, dcrit, tdata, dfull,
    wbuf, pbuf, abuf, bbuf, rbuf, gall, lbuf, vbuf, plan, turned, tbuf, npot, dpot,
    load, n1s, n1r, n2s, n2r, es, er, fs, fr, ts, tr, w1s, w1r, w2s, w2r, sib_s, sib_r,
    as_, ar, bs, br, gs, gr, hs, hr, os_, or_, ps,
):
    FQ = width // (Q * C)
    FS = X * FQ
    eps = 1.0 / math.sqrt(width)
    row = lax.axis_index("row")
    c = lax.axis_index("col")
    k = row % 2
    q = row // 2
    x = q % X
    yl = q // X
    z = c // YH
    yh = c % YH
    y = yh * YL + yl
    other = 1 - k

    def place(yl_, x_, k_):
        return (yl_ * X + x_) * 2 + k_

    sibling = (place(yl, x, other), c)

    def relay_of(j):
        return place(2 * k + j // X, j % X, yh), z * YH + x % YH

    def relay_source(i):
        f = YH * i + yh
        return place(f // X, f % X, yl // 2), z * YH + k

    to_self = jnp.logical_and(jnp.logical_and(k == yl // 2, yh == k), x % YH == yh)
    n_self = jnp.where(to_self, 1, 0).astype(jnp.int32)

    def finish():
        def sent(ref, sem):
            pltpu.make_async_copy(ref, ref, sem).wait()

        @pl.when(to_self)
        def _():
            sent(dstage.at[pl.ds(0, 2 * X - 1)], es)

        @pl.when(jnp.logical_not(to_self))
        def _():
            sent(dstage, es)

        sent(relay.at[pl.ds(0, Z - 1)], fs)
        sent(nstage.at[pl.ds(0, YL - 1)], n1s)
        sent(nbuf.at[k, pl.ds(0, X - 1)], n2s)
        sent(nbuf.at[k], sib_s.at[0])
        sent(wbuf.at[pl.ds(0, Z - 1), 0], w1s)
        sent(wbuf.at[:, yh], w2s)
        sent(pbuf.at[pl.ds(0, Y - 1)], as_)
        sent(tdata.at[pl.ds(0, X - 1)], ts)
        sent(rbuf.at[pl.ds(0, Z - 1)], bs)
        sent(gall.at[k, x, pl.ds(0, Y - 1)], gs)
        sent(gall.at[k, pl.ds(0, X - 1)], hs)
        sent(gall.at[k], sib_s.at[1])
        sent(tdata.at[pl.ds(0, X)], sib_s.at[2])
        sent(out_ref.at[pl.ds(0, YL - 1)], os_)
        sent(out_ref, or_)
        sent(npot_ref, ps.at[0])
        sent(dpot_ref, ps.at[1])

    loads = [
        pltpu.make_async_copy(nw_hbm, nw_ref, load.at[0]),
        pltpu.make_async_copy(dw_hbm, dw_ref, load.at[1]),
        pltpu.make_async_copy(data_ref, dvm, load.at[2]),
    ] + [
        pltpu.make_async_copy(
            noise_ref.at[:, pl.ds(t * FS, FS)], nstage.at[t, :, pl.ds(0, FS)], load.at[3 + t]
        )
        for t in range(YL)
    ]

    barrier = pltpu.get_barrier_semaphore()

    def greet(device):
        pl.semaphore_signal(barrier, inc=1, device_id=device, device_id_type=MESH)

    def greet_source(i, carry):
        device = relay_source(i)

        @pl.when(jnp.logical_or(device[0] != row, device[1] != c))
        def _():
            greet(device)

        return carry

    def greet_z(s, carry):
        greet((row, lax.rem(z + s, Z) * YH + yh))
        return carry

    def greet_y(s, carry):
        t = lax.rem(y + s, Y)
        greet((place(t % YL, x, k), z * YH + t // YL))
        return carry

    def greet_x(s, carry):
        greet((place(yl, lax.rem(x + s, X), k), c))
        return carry

    for copy in loads[2::-1]:
        copy.start()
    lax.fori_loop(0, Z, greet_source, 0)
    lax.fori_loop(1, Z, greet_z, 0)
    lax.fori_loop(1, Y, greet_y, 0)
    lax.fori_loop(1, X, greet_x, 0)
    greet(sibling)
    for copy in loads[3:]:
        copy.start()

    loads[2].wait()
    for j in range(2 * X):
        s, t = j // X, j % X
        for f in range(X):
            cut = dvm[:, s * FS + f * FQ:s * FS + (f + 1) * FQ].astype(F32)
            dstage[j, f] = cut[8 * t:8 * t + 8].astype(BF16)
    pl.semaphore_wait(barrier, (Y - 1) + (X - 1) + (Z - 1) + 1 + 2 * X - n_self)

    def send_data(i, carry):
        j = i // X * X + lax.rem(x + 2 + i, X)
        device = relay_of(j)
        is_self = jnp.logical_and(device[0] == row, device[1] == c)
        slot = q // YH

        @pl.when(is_self)
        def _():
            pltpu.make_async_copy(dstage.at[j], relay.at[slot], er.at[slot]).start()

        @pl.when(jnp.logical_not(is_self))
        def _():
            pltpu.make_async_remote_copy(
                dstage.at[j], relay.at[slot], es, er.at[slot],
                device_id=device, device_id_type=MESH,
            ).start()

        return carry

    lax.fori_loop(0, 2 * X, send_data, 0)

    loads[0].wait()
    for copy in loads[3:]:
        copy.wait()

    rows8 = lax.broadcasted_iota(jnp.int32, (8, LANES), 0)
    lanes8 = lax.broadcasted_iota(jnp.int32, (8, LANES), 1)
    noise_w = jnp.zeros((8, LANES), jnp.int32)
    for i in range(8):
        noise_w = jnp.where(rows8 == i, nw_ref[i], noise_w)
    noise_w = noise_w.astype(F32)
    for t in range(YL):
        nf = nstage[t, :, 0:FS].astype(F32)
        sq = jnp.sum(nf * nf, axis=1, keepdims=True)
        hi = sq.astype(BF16).astype(F32)
        mid = (sq - hi).astype(BF16).astype(F32)
        lo = sq - hi - mid
        tail = jnp.where(lanes8 == 3, noise_w, 0.0)
        tail = jnp.where(lanes8 == 2, lo, tail)
        tail = jnp.where(lanes8 == 1, mid, tail)
        tail = jnp.where(lanes8 == 0, hi, tail)
        nstage[t, :, FS:FS + LANES] = tail.astype(BF16)

    def send_noise_y(s, carry):
        t = lax.rem(yl + s, YL)
        pltpu.make_async_remote_copy(
            nstage.at[t], nbuf.at[k, x, yl], n1s, n1r,
            device_id=(place(t, x, k), c), device_id_type=MESH,
        ).start()
        return carry

    lax.fori_loop(1, YL, send_noise_y, 0)
    pltpu.make_async_copy(nstage.at[yl], nbuf.at[k, x, yl], n1r).start()

    loads[1].wait()
    lanes1 = lax.broadcasted_iota(jnp.int32, (1, LANES), 1)
    data_w = jnp.zeros((1, LANES), jnp.int32)
    for i in range(32):
        data_w = jnp.where(lanes1 == i, dw_ref[i], data_w)
    wstage[...] = data_w.astype(F32)

    def send_w(s, carry):
        t = lax.rem(z + s, Z)
        pltpu.make_async_remote_copy(
            wstage, wbuf.at[z, yh], w1s, w1r,
            device_id=(row, t * YH + yh), device_id_type=MESH,
        ).start()
        return carry

    lax.fori_loop(1, Z, send_w, 0)
    pltpu.make_async_copy(wstage, wbuf.at[z, yh], w1r).start()

    def far_first(s, count):
        d = s // 2
        return count // 2 + jnp.where(s % 2 == 1, d, -d)

    def arrived(ref, sem):
        pltpu.make_async_copy(ref, ref, sem).wait()

    def swap(ref, i):
        return pltpu.make_async_remote_copy(
            ref, ref, sib_s.at[i], sib_r.at[i], device_id=sibling, device_id_type=MESH
        )

    arrived(nbuf.at[k, x], n1r)

    def send_noise_x(s, carry):
        t = lax.rem(x + s, X)
        pltpu.make_async_remote_copy(
            nbuf.at[k, x], nbuf.at[k, x], n2s, n2r,
            device_id=(place(yl, t, k), c), device_id_type=MESH,
        ).start()
        return carry

    lax.fori_loop(1, X, send_noise_x, 0)

    def hand_on(i, carry):
        t = lax.rem(YH * yl + i, Z)
        arrived(relay.at[t], er.at[t])

        @pl.when(t == z)
        def _():
            pltpu.make_async_copy(relay.at[t], dcrit.at[z], fr).start()

        @pl.when(t != z)
        def _():
            pltpu.make_async_remote_copy(
                relay.at[t], dcrit.at[z], fs, fr,
                device_id=(row, t * YH + yh), device_id_type=MESH,
            ).start()

        return carry

    lax.fori_loop(0, Z, hand_on, 0)

    def noise_rows(core):
        for t in range(2):
            part = nbuf[core, 2 * t:2 * t + 2].astype(F32)
            nmat[core, t * 4 * Q:(t + 1) * 4 * Q, :] = part.reshape(4 * Q, FS + LANES).astype(BF16)

    arrived(nbuf.at[k, pl.ds(0, X - 1)], n2r)
    noise_swap = swap(nbuf.at[k], 0)
    noise_swap.start()
    noise_rows(k)
    arrived(nbuf.at[other], sib_r.at[0])
    noise_rows(other)
    tail = nmat[:, :, FS:FS + LANES].reshape(16 * Q, LANES)
    pick_sq = jnp.where(lanes8 < 3, 1.0, 0.0).astype(BF16)
    pick_w = jnp.where(lanes8 == 3, 1.0, 0.0).astype(BF16)
    nsq = lax.dot_general(pick_sq, tail, NT, preferred_element_type=F32)[0:1, :]
    wa = lax.dot_general(pick_w, tail, NT, preferred_element_type=F32)[0:1, :]

    arrived(wbuf.at[:, yh], w1r)
    pltpu.make_async_remote_copy(
        wbuf.at[:, yh], wbuf.at[:, yh], w2s, w2r,
        device_id=(row, z * YH + 1 - yh), device_id_type=MESH,
    ).start()

    arrived(dcrit, fr)
    df = dcrit[...].astype(F32)
    part = jnp.sum(
        jnp.sum(df * df, axis=1).reshape(Z * 8, FQ), axis=1, keepdims=True
    ) + nsq
    dm = (df * -2.0)
    for f in range(X):
        part = part + lax.dot_general(
            dm[:, f].reshape(Z * 8, FQ).astype(BF16),
            nmat[:, :, f * FQ:(f + 1) * FQ].reshape(16 * Q, FQ),
            NT, preferred_element_type=F32,
        )
    for h in range(2):
        pbuf[:, h] = part[:, h * LANES:(h + 1) * LANES].reshape(Y, 8, LANES)

    def y_peer(t):
        return place(t % YL, x, k), z * YH + t // YL

    def send_a(s, carry):
        t = lax.rem(y + far_first(s, Y), Y)
        pltpu.make_async_remote_copy(
            pbuf.at[t], abuf.at[y], as_, ar, device_id=y_peer(t), device_id_type=MESH
        ).start()
        return carry

    lax.fori_loop(1, Y, send_a, 0)
    pltpu.make_async_copy(pbuf.at[y], abuf.at[y], ar).start()

    def send_features(s, carry):
        t = lax.rem(x + s, X)
        pltpu.make_async_remote_copy(
            dcrit, tdata.at[k * X + x], ts, tr,
            device_id=(place(yl, t, k), c), device_id_type=MESH,
        ).start()
        return carry

    lax.fori_loop(1, X, send_features, 0)
    pltpu.make_async_copy(dcrit, tdata.at[k * X + x], tr).start()

    log_a = jnp.log(wa / jnp.sum(wa, axis=1, keepdims=True))
    log_a = [log_a[:, h * LANES:(h + 1) * LANES] for h in range(2)]
    arrived(abuf, ar)
    total = abuf[0]
    for j in range(1, Y):
        total = total + abuf[j]
    bbuf[...] = total

    def send_b(s, carry):
        t = lax.rem(z + far_first(s, Z), Z)
        pltpu.make_async_remote_copy(
            bbuf, rbuf.at[z], bs, br, device_id=(row, t * YH + yh), device_id_type=MESH
        ).start()
        return carry

    lax.fori_loop(1, Z, send_b, 0)
    pltpu.make_async_copy(bbuf, rbuf.at[z], br).start()

    arrived(rbuf, br)
    total = rbuf[0]
    for j in range(1, Z):
        total = total + rbuf[j]
    gall[k, x, y] = total * (-1.0 / (width * eps))

    def send_g(s, carry):
        t = lax.rem(y + far_first(s, Y), Y)
        pltpu.make_async_remote_copy(
            gall.at[k, x, y], gall.at[k, x, y], gs, gr.at[y],
            device_id=y_peer(t), device_id_type=MESH,
        ).start()
        return carry

    lax.fori_loop(1, Y, send_g, 0)

    def send_x(piece):
        for s in range(1, X):
            t = lax.rem(x + s, X)
            pltpu.make_async_remote_copy(
                gall.at[k, x, piece], gall.at[k, x, piece], hs, hr.at[x],
                device_id=(place(yl, t, k), c), device_id_type=MESH,
            ).start()

    send_x(y)

    arrived(wbuf.at[:, 1 - yh], w2r)
    wb = wbuf[...].reshape(C, 1, LANES)
    w_sum = jnp.sum(jnp.sum(wb, axis=0), axis=1, keepdims=True)
    spot = lax.broadcasted_iota(jnp.int32, (C, 32, LANES), 1) == lax.broadcasted_iota(
        jnp.int32, (C, 32, LANES), 2
    )
    wb = jnp.where(spot, wb, 0.0).reshape(C * 32, LANES).astype(BF16)
    wb = jnp.dot(wb, jnp.ones((LANES, LANES), BF16), preferred_element_type=F32)
    log_b = jnp.log(wb / w_sum).reshape(Z, YH, X, 8, LANES)
    for a in range(YH):
        for b in range(X):
            lbuf[a, b] = log_b[:, a, b]
    def data_rows(core):
        def step(i, carry):
            g = core * X + i
            for f in range(X):
                cut = tdata[g, :, f].astype(F32).reshape(Z * 8, FQ)
                dfull[g, :, f * FQ:(f + 1) * FQ] = cut.astype(BF16)
            return carry

        lax.fori_loop(0, X, step, 0)

    own_rows = tdata.at[pl.ds(k * X, X)]
    other_rows = tdata.at[pl.ds(other * X, X)]
    arrived(own_rows, tr)
    rows_swap = swap(own_rows, 2)
    rows_swap.start()
    data_rows(k)

    def gather_y(i, carry):
        d = (i + 1) // 2
        t = lax.rem(y + jnp.where(i % 2 == 1, d, Y - d), Y)
        arrived(gall.at[k, x, t], gr.at[t])
        send_x(t)
        return carry

    lax.fori_loop(1, Y, gather_y, 0)

    def send_core(t):
        pltpu.make_async_remote_copy(
            gall.at[k, t], gall.at[k, t], sib_s.at[1], sib_r.at[1],
            device_id=sibling, device_id_type=MESH,
        ).start()

    send_core(x)

    def gather_x(s, carry):
        t = lax.rem(x + jnp.where(s == 2, 3, jnp.where(s == 3, 2, 1)), X)
        arrived(gall.at[k, t], hr.at[t])
        send_core(t)
        return carry

    lax.fori_loop(1, X, gather_x, 0)
    arrived(other_rows, sib_r.at[2])
    data_rows(other)
    arrived(gall.at[other], sib_r.at[1])

    def parts(i):
        return i // X, i % X

    def peak_step(i, peak):
        a, b = parts(i)
        return jnp.maximum(peak, jnp.max(gall[a, b], axis=0))

    peak = jnp.full((2, 8, LANES), -jnp.inf, F32)
    for i in range(2 * X):
        peak = peak_step(i, peak)
    for rounds in range(HALVES // 2):
        top = jnp.max(peak, axis=1, keepdims=True)

        def noise_step(i, acc):
            a, b = parts(i)
            s = gall[a, b]
            if rounds:
                s = s + vbuf[a, b][:, None]
            return acc + jnp.sum(jnp.exp(s - top), axis=0)

        acc = jnp.zeros((2, 8, LANES), F32)
        for i in range(2 * X):
            acc = noise_step(i, acc)
        lse = top + jnp.log(jnp.sum(acc, axis=1, keepdims=True))
        u = jnp.concatenate([(log_a[h] - lse[h])[None] for h in range(2)], axis=0)

        def data_step(i, peak):
            a, b = parts(i)
            s = gall[a, b]
            w = s + u
            m = jnp.max(jnp.max(w, axis=1), axis=2, keepdims=True)
            e = jnp.sum(jnp.sum(jnp.exp(w - m[:, None]), axis=1), axis=2, keepdims=True)
            v = lbuf[a, b] - (m + jnp.log(e))
            vbuf[a, b] = v
            return jnp.maximum(peak, jnp.max(s + v[:, None], axis=0))

        peak = jnp.full((2, 8, LANES), -jnp.inf, F32)
        for i in range(2 * X):
            peak = data_step(i, peak)

    own_u = jnp.where(k == 0, u[0], u[1])
    for i in range(2 * X):
        a, b = parts(i)
        plan[a, b] = jnp.exp(gall[a, b, :, k] + own_u + vbuf[a, b])
    turned[...] = jnp.transpose(plan[...].reshape(C * 32, LANES), (1, 0))
    p = turned[pl.ds(pl.multiple_of(x * YL * 8, YL * 8), YL * 8), :]
    mass = jnp.sum(p, axis=1, keepdims=True)
    value = jnp.dot(
        p.astype(BF16), dfull[...].reshape(C * 32, FS), preferred_element_type=F32
    ) / mass
    tbuf[...] = value.reshape(YL, 8, FS).astype(BF16)

    def send_t(s, carry):
        t = lax.rem(yl + s, YL)
        pltpu.make_async_remote_copy(
            tbuf.at[t], out_ref.at[yl], os_, or_,
            device_id=(place(t, x, k), c), device_id_type=MESH,
        ).start()
        return carry

    lax.fori_loop(1, YL, send_t, 0)
    pltpu.make_async_copy(tbuf.at[yl], out_ref.at[yl], or_).start()

    mine = own_u[:, 0:8]
    for t in range(1, Q):
        mine = jnp.where(x * YL + yl == t, own_u[:, 8 * t:8 * t + 8], mine)
    npot[...] = mine * eps
    lanes4 = lax.broadcasted_iota(jnp.int32, (X, 8, LANES), 2)
    index4 = lax.broadcasted_iota(jnp.int32, (X, 8, LANES), 0) * 8 + lax.broadcasted_iota(
        jnp.int32, (X, 8, LANES), 1
    )
    block = jnp.where(lanes4 == index4, vbuf[yh, :, z], 0.0)
    block = jnp.sum(jnp.sum(block, axis=0), axis=0, keepdims=True)
    dpot[...] = block[:, 0:32] * eps
    pltpu.make_async_copy(npot, npot_ref, ps.at[0]).start()
    pltpu.make_async_copy(dpot, dpot_ref, ps.at[1]).start()
    finish()


def leave(targets_ref, npot_ref, dpot_ref, out_ref, nout_ref, dout_ref, held, npot, dpot, into, out):
    width = targets_ref.shape[2]
    sources = [npot_ref, dpot_ref] + [targets_ref.at[t] for t in range(YL)]
    places = [npot, dpot] + [held.at[t] for t in range(YL)]
    results = [nout_ref, dout_ref] + [
        out_ref.at[:, pl.ds(t * width, width)] for t in range(YL)
    ]
    count = len(places)
    first = [pltpu.make_async_copy(sources[i], places[i], into.at[i]) for i in range(count)]
    second = [pltpu.make_async_copy(places[i], results[i], out.at[i]) for i in range(count)]
    for copy in first:
        copy.start()
    for i in range(count):
        first[i].wait()
        second[i].start()
    for copy in second:
        copy.wait()


def per_device(noise, data, noise_weight, data_weight):
    width = noise.shape[1] * C
    FQ = width // (Q * C)
    FS = X * FQ
    anywhere = pl.BlockSpec(memory_space=pl.ANY)
    dma = pltpu.SemaphoreType.DMA
    targets, noise_pot, data_pot = pl.pallas_call(
        functools.partial(kernel, width),
        out_shape=(
            jax.ShapeDtypeStruct((YL, 8, FS), BF16),
            jax.ShapeDtypeStruct((1, 8), F32),
            jax.ShapeDtypeStruct((1, 32), F32),
        ),
        in_specs=[anywhere] * 4,
        out_specs=(anywhere, anywhere, anywhere),
        scratch_shapes=[
            pltpu.SMEM((8,), jnp.int32),
            pltpu.SMEM((32,), jnp.int32),
            pltpu.VMEM((YL, 8, FS + LANES), BF16),
            pltpu.VMEM((32, 2 * FS), BF16),
            pltpu.VMEM((2 * X, X, 8, FQ), BF16),
            pltpu.VMEM((Z, X, 8, FQ), BF16),
            pltpu.VMEM((1, LANES), F32),
            pltpu.VMEM((2, X, YL, 8, FS + LANES), BF16),
            pltpu.VMEM((2, 8 * Q, FS + LANES), BF16),
            pltpu.VMEM((Z, X, 8, FQ), BF16),
            pltpu.VMEM((2 * X, Z, X, 8, FQ), BF16),
            pltpu.VMEM((2 * X, Z * 8, FS), BF16),
            pltpu.VMEM((Z, YH, 1, LANES), F32),
            pltpu.VMEM((Y, 2, 8, LANES), F32),
            pltpu.VMEM((Y, 2, 8, LANES), F32),
            pltpu.VMEM((2, 8, LANES), F32),
            pltpu.VMEM((Z, 2, 8, LANES), F32),
            pltpu.VMEM((2, X, Y, 2, 8, LANES), F32),
            pltpu.VMEM((2, X, Y, 8, LANES), F32),
            pltpu.VMEM((2, X, Y, 8, LANES), F32),
            pltpu.VMEM((2, X, Z, 8, LANES), F32),
            pltpu.VMEM((LANES, C * 32), F32),
            pltpu.VMEM((YL, 8, FS), BF16),
            pltpu.VMEM((1, 8), F32),
            pltpu.VMEM((1, 32), F32),
            dma((3 + YL,)),
        ] + [dma] * 5 + [dma((Z,))] + [dma] * 8 + [dma((3,))] * 2 + [dma] * 5 + [dma((Y,)), dma, dma((X,)), dma, dma, dma((2,))],
        compiler_params=pltpu.CompilerParams(
            collective_id=0, has_side_effects=True, vmem_limit_bytes=60 * 1024 * 1024
        ),
    )(noise_weight, data_weight, noise, data)
    targets, noise_pot, data_pot = pl.pallas_call(
        leave,
        out_shape=(
            jax.ShapeDtypeStruct((8, YL * FS), BF16),
            jax.ShapeDtypeStruct((1, 8), F32),
            jax.ShapeDtypeStruct((1, 32), F32),
        ),
        in_specs=[anywhere] * 3,
        out_specs=(anywhere, anywhere, anywhere),
        scratch_shapes=[
            pltpu.VMEM((YL, 8, FS), BF16),
            pltpu.VMEM((1, 8), F32),
            pltpu.VMEM((1, 32), F32),
            dma((YL + 2,)),
            dma((YL + 2,)),
        ],
        compiler_params=pltpu.CompilerParams(vmem_limit_bytes=60 * 1024 * 1024),
    )(targets, noise_pot, data_pot)
    return (targets, noise_pot.reshape(8), data_pot.reshape(32))


def solution(mesh):
    placed = (P("row", "col"), P("col", "row"), P("row"), P("col"))
    return jax.shard_map(
        per_device,
        mesh=mesh,
        in_specs=placed,
        out_specs=(P("row", "col"), P("row"), P("col")),
        check_vma=False,
    )
```

```python
import functools
import math

import jax
import jax.numpy as jnp
from jax import lax
from jax.experimental import pallas as pl
from jax.experimental.pallas import tpu as pltpu
from jax.sharding import PartitionSpec as P

HALVES = 4
MESH = pl.DeviceIdType.MESH
F32 = jnp.float32
BF16 = jnp.bfloat16
LANES = 128
X, YL, Z, YH = 4, 4, 8, 2
Y = YH * YL
Q = YL * X
C = Z * YH
NT = (((1,), (1,)), ((), ()))


def kernel(
    width,
    nw_hbm, dw_hbm, noise_ref, data_ref,
    out_ref, npot_ref, dpot_ref,
    nw_ref, dw_ref, nstage, dvm, dstage, relay, wstage, nbuf, nmat, dcrit, tdata, dfull,
    wbuf, pbuf, abuf, bbuf, rbuf, gall, lbuf, vbuf, plan, turned, tbuf, npot, dpot,
    load, n1s, n1r, n2s, n2r, es, er, fs, fr, ts, tr, w1s, w1r, w2s, w2r, sib_s, sib_r,
    as_, ar, bs, br, gs, gr, hs, hr, os_, or_, ps,
):
    FQ = width // (Q * C)
    FS = X * FQ
    eps = 1.0 / math.sqrt(width)
    row = lax.axis_index("row")
    c = lax.axis_index("col")
    k = row % 2
    q = row // 2
    x = q % X
    yl = q // X
    z = c // YH
    yh = c % YH
    y = yh * YL + yl
    other = 1 - k

    def place(yl_, x_, k_):
        return (yl_ * X + x_) * 2 + k_

    sibling = (place(yl, x, other), c)

    def relay_of(j):
        return place(2 * k + j // X, j % X, yh), z * YH + x % YH

    def relay_source(i):
        f = YH * i + yh
        return place(f // X, f % X, yl // 2), z * YH + k

    to_self = jnp.logical_and(jnp.logical_and(k == yl // 2, yh == k), x % YH == yh)
    n_self = jnp.where(to_self, 1, 0).astype(jnp.int32)

    def finish():
        def sent(ref, sem):
            pltpu.make_async_copy(ref, ref, sem).wait()

        @pl.when(to_self)
        def _():
            sent(dstage.at[pl.ds(0, 2 * X - 1)], es)

        @pl.when(jnp.logical_not(to_self))
        def _():
            sent(dstage, es)

        sent(relay.at[pl.ds(0, Z - 1)], fs)
        sent(nstage.at[pl.ds(0, YL - 1)], n1s)
        sent(nbuf.at[k, pl.ds(0, X - 1)], n2s)
        sent(nbuf.at[k], sib_s.at[0])
        sent(wbuf.at[pl.ds(0, Z - 1), 0], w1s)
        sent(wbuf.at[:, yh], w2s)
        sent(pbuf.at[pl.ds(0, Y - 1)], as_)
        sent(tdata.at[pl.ds(0, X - 1)], ts)
        sent(rbuf.at[pl.ds(0, Z - 1)], bs)
        sent(gall.at[k, x, pl.ds(0, Y - 1)], gs)
        sent(gall.at[k, pl.ds(0, X - 1)], hs)
        sent(gall.at[k], sib_s.at[1])
        sent(tdata.at[pl.ds(0, X)], sib_s.at[2])
        sent(out_ref.at[pl.ds(0, YL - 1)], os_)
        sent(out_ref, or_)
        sent(npot_ref, ps.at[0])
        sent(dpot_ref, ps.at[1])

    loads = [
        pltpu.make_async_copy(nw_hbm, nw_ref, load.at[0]),
        pltpu.make_async_copy(dw_hbm, dw_ref, load.at[1]),
        pltpu.make_async_copy(data_ref, dvm, load.at[2]),
    ] + [
        pltpu.make_async_copy(
            noise_ref.at[:, pl.ds(t * FS, FS)], nstage.at[t, :, pl.ds(0, FS)], load.at[3 + t]
        )
        for t in range(YL)
    ]

    barrier = pltpu.get_barrier_semaphore()

    def greet(device):
        pl.semaphore_signal(barrier, inc=1, device_id=device, device_id_type=MESH)

    def greet_source(i, carry):
        device = relay_source(i)

        @pl.when(jnp.logical_or(device[0] != row, device[1] != c))
        def _():
            greet(device)

        return carry

    def greet_z(s, carry):
        greet((row, lax.rem(z + lax.rem(s + 2, Z - 1) + 1, Z) * YH + yh))
        return carry

    def greet_y(s, carry):
        t = lax.rem(y + lax.rem(s + 2, Y - 1) + 1, Y)
        greet((place(t % YL, x, k), z * YH + t // YL))
        return carry

    def greet_x(s, carry):
        greet((place(yl, lax.rem(x + s, X), k), c))
        return carry

    for copy in loads[2::-1]:
        copy.start()
    lax.fori_loop(0, Z, greet_source, 0)
    lax.fori_loop(1, Z, greet_z, 0)
    lax.fori_loop(1, Y, greet_y, 0)
    lax.fori_loop(1, X, greet_x, 0)
    greet(sibling)
    for copy in loads[3:]:
        copy.start()

    loads[2].wait()
    for j in range(2 * X):
        s, t = j // X, j % X
        for f in range(X):
            cut = dvm[:, s * FS + f * FQ:s * FS + (f + 1) * FQ].astype(F32)
            dstage[j, f] = cut[8 * t:8 * t + 8].astype(BF16)
    pl.semaphore_wait(barrier, (Y - 1) + (X - 1) + (Z - 1) + 1 + 2 * X - n_self)

    def send_data(i, carry):
        j = i // X * X + lax.rem(x + 2 + i, X)
        device = relay_of(j)
        is_self = jnp.logical_and(device[0] == row, device[1] == c)
        slot = q // YH

        @pl.when(is_self)
        def _():
            pltpu.make_async_copy(dstage.at[j], relay.at[slot], er.at[slot]).start()

        @pl.when(jnp.logical_not(is_self))
        def _():
            pltpu.make_async_remote_copy(
                dstage.at[j], relay.at[slot], es, er.at[slot],
                device_id=device, device_id_type=MESH,
            ).start()

        return carry

    lax.fori_loop(0, 2 * X, send_data, 0)

    loads[0].wait()
    for copy in loads[3:]:
        copy.wait()

    rows8 = lax.broadcasted_iota(jnp.int32, (8, LANES), 0)
    lanes8 = lax.broadcasted_iota(jnp.int32, (8, LANES), 1)
    noise_w = jnp.zeros((8, LANES), jnp.int32)
    for i in range(8):
        noise_w = jnp.where(rows8 == i, nw_ref[i], noise_w)
    noise_w = noise_w.astype(F32)
    for t in range(YL):
        nf = nstage[t, :, 0:FS].astype(F32)
        sq = jnp.sum(nf * nf, axis=1, keepdims=True)
        hi = sq.astype(BF16).astype(F32)
        mid = (sq - hi).astype(BF16).astype(F32)
        lo = sq - hi - mid
        tail = jnp.where(lanes8 == 3, noise_w, 0.0)
        tail = jnp.where(lanes8 == 2, lo, tail)
        tail = jnp.where(lanes8 == 1, mid, tail)
        tail = jnp.where(lanes8 == 0, hi, tail)
        nstage[t, :, FS:FS + LANES] = tail.astype(BF16)

    def send_noise_y(s, carry):
        t = lax.rem(yl + s, YL)
        pltpu.make_async_remote_copy(
            nstage.at[t], nbuf.at[k, x, yl], n1s, n1r,
            device_id=(place(t, x, k), c), device_id_type=MESH,
        ).start()
        return carry

    lax.fori_loop(1, YL, send_noise_y, 0)
    pltpu.make_async_copy(nstage.at[yl], nbuf.at[k, x, yl], n1r).start()

    loads[1].wait()
    lanes1 = lax.broadcasted_iota(jnp.int32, (1, LANES), 1)
    data_w = jnp.zeros((1, LANES), jnp.int32)
    for i in range(32):
        data_w = jnp.where(lanes1 == i, dw_ref[i], data_w)
    wstage[...] = data_w.astype(F32)

    def send_w(s, carry):
        t = lax.rem(z + s, Z)
        pltpu.make_async_remote_copy(
            wstage, wbuf.at[z, yh], w1s, w1r,
            device_id=(row, t * YH + yh), device_id_type=MESH,
        ).start()
        return carry

    lax.fori_loop(1, Z, send_w, 0)
    pltpu.make_async_copy(wstage, wbuf.at[z, yh], w1r).start()

    def far_first(s, count):
        d = s // 2
        return count // 2 + jnp.where(s % 2 == 1, d, -d)

    def arrived(ref, sem):
        pltpu.make_async_copy(ref, ref, sem).wait()

    def swap(ref, i):
        return pltpu.make_async_remote_copy(
            ref, ref, sib_s.at[i], sib_r.at[i], device_id=sibling, device_id_type=MESH
        )

    arrived(nbuf.at[k, x], n1r)

    def send_noise_x(s, carry):
        t = lax.rem(x + s, X)
        pltpu.make_async_remote_copy(
            nbuf.at[k, x], nbuf.at[k, x], n2s, n2r,
            device_id=(place(yl, t, k), c), device_id_type=MESH,
        ).start()
        return carry

    lax.fori_loop(1, X, send_noise_x, 0)

    def hand_on(i, carry):
        t = lax.rem(YH * yl + i, Z)
        arrived(relay.at[t], er.at[t])

        @pl.when(t == z)
        def _():
            pltpu.make_async_copy(relay.at[t], dcrit.at[z], fr).start()

        @pl.when(t != z)
        def _():
            pltpu.make_async_remote_copy(
                relay.at[t], dcrit.at[z], fs, fr,
                device_id=(row, t * YH + yh), device_id_type=MESH,
            ).start()

        return carry

    lax.fori_loop(0, Z, hand_on, 0)

    def noise_rows(core):
        for t in range(2):
            part = nbuf[core, 2 * t:2 * t + 2].astype(F32)
            nmat[core, t * 4 * Q:(t + 1) * 4 * Q, :] = part.reshape(4 * Q, FS + LANES).astype(BF16)

    arrived(nbuf.at[k, pl.ds(0, X - 1)], n2r)
    noise_swap = swap(nbuf.at[k], 0)
    noise_swap.start()
    noise_rows(k)
    arrived(nbuf.at[other], sib_r.at[0])
    noise_rows(other)
    tail = nmat[:, :, FS:FS + LANES].reshape(16 * Q, LANES)
    pick_sq = jnp.where(lanes8 < 3, 1.0, 0.0).astype(BF16)
    pick_w = jnp.where(lanes8 == 3, 1.0, 0.0).astype(BF16)
    nsq = lax.dot_general(pick_sq, tail, NT, preferred_element_type=F32)[0:1, :]
    wa = lax.dot_general(pick_w, tail, NT, preferred_element_type=F32)[0:1, :]

    arrived(wbuf.at[:, yh], w1r)
    pltpu.make_async_remote_copy(
        wbuf.at[:, yh], wbuf.at[:, yh], w2s, w2r,
        device_id=(row, z * YH + 1 - yh), device_id_type=MESH,
    ).start()

    arrived(dcrit, fr)
    df = dcrit[...].astype(F32)
    part = jnp.sum(
        jnp.sum(df * df, axis=1).reshape(Z * 8, FQ), axis=1, keepdims=True
    ) + nsq
    dm = (df * -2.0)
    for f in range(X):
        part = part + lax.dot_general(
            dm[:, f].reshape(Z * 8, FQ).astype(BF16),
            nmat[:, :, f * FQ:(f + 1) * FQ].reshape(16 * Q, FQ),
            NT, preferred_element_type=F32,
        )
    for h in range(2):
        pbuf[:, h] = part[:, h * LANES:(h + 1) * LANES].reshape(Y, 8, LANES)

    def y_peer(t):
        return place(t % YL, x, k), z * YH + t // YL

    def send_a(s, carry):
        t = lax.rem(y + far_first(s, Y), Y)
        pltpu.make_async_remote_copy(
            pbuf.at[t], abuf.at[y], as_, ar, device_id=y_peer(t), device_id_type=MESH
        ).start()
        return carry

    lax.fori_loop(1, Y, send_a, 0)
    pltpu.make_async_copy(pbuf.at[y], abuf.at[y], ar).start()

    def send_features(s, carry):
        t = lax.rem(x + s, X)
        pltpu.make_async_remote_copy(
            dcrit, tdata.at[k * X + x], ts, tr,
            device_id=(place(yl, t, k), c), device_id_type=MESH,
        ).start()
        return carry

    lax.fori_loop(1, X, send_features, 0)
    pltpu.make_async_copy(dcrit, tdata.at[k * X + x], tr).start()

    log_a = jnp.log(wa / jnp.sum(wa, axis=1, keepdims=True))
    log_a = [log_a[:, h * LANES:(h + 1) * LANES] for h in range(2)]
    arrived(abuf, ar)
    total = abuf[0]
    for j in range(1, Y):
        total = total + abuf[j]
    bbuf[...] = total

    def send_b(s, carry):
        t = lax.rem(z + far_first(s, Z), Z)
        pltpu.make_async_remote_copy(
            bbuf, rbuf.at[z], bs, br, device_id=(row, t * YH + yh), device_id_type=MESH
        ).start()
        return carry

    lax.fori_loop(1, Z, send_b, 0)
    pltpu.make_async_copy(bbuf, rbuf.at[z], br).start()

    arrived(rbuf, br)
    total = rbuf[0]
    for j in range(1, Z):
        total = total + rbuf[j]
    gall[k, x, y] = total * (-1.0 / (width * eps))

    def send_g(s, carry):
        t = lax.rem(y + far_first(s, Y), Y)
        pltpu.make_async_remote_copy(
            gall.at[k, x, y], gall.at[k, x, y], gs, gr.at[y],
            device_id=y_peer(t), device_id_type=MESH,
        ).start()
        return carry

    lax.fori_loop(1, Y, send_g, 0)

    def send_x(piece):
        for s in range(1, X):
            t = lax.rem(x + s, X)
            pltpu.make_async_remote_copy(
                gall.at[k, x, piece], gall.at[k, x, piece], hs, hr.at[x],
                device_id=(place(yl, t, k), c), device_id_type=MESH,
            ).start()

    send_x(y)

    arrived(wbuf.at[:, 1 - yh], w2r)
    wb = wbuf[...].reshape(C, 1, LANES)
    w_sum = jnp.sum(jnp.sum(wb, axis=0), axis=1, keepdims=True)
    spot = lax.broadcasted_iota(jnp.int32, (C, 32, LANES), 1) == lax.broadcasted_iota(
        jnp.int32, (C, 32, LANES), 2
    )
    wb = jnp.where(spot, wb, 0.0).reshape(C * 32, LANES).astype(BF16)
    wb = jnp.dot(wb, jnp.ones((LANES, LANES), BF16), preferred_element_type=F32)
    log_b = jnp.log(wb / w_sum).reshape(Z, YH, X, 8, LANES)
    for a in range(YH):
        for b in range(X):
            lbuf[a, b] = log_b[:, a, b]
    def data_rows(core):
        def step(i, carry):
            g = core * X + i
            for f in range(X):
                cut = tdata[g, :, f].astype(F32).reshape(Z * 8, FQ)
                dfull[g, :, f * FQ:(f + 1) * FQ] = cut.astype(BF16)
            return carry

        lax.fori_loop(0, X, step, 0)

    own_rows = tdata.at[pl.ds(k * X, X)]
    other_rows = tdata.at[pl.ds(other * X, X)]
    arrived(own_rows, tr)
    rows_swap = swap(own_rows, 2)
    rows_swap.start()
    data_rows(k)

    def gather_y(i, carry):
        d = (i + 1) // 2
        t = lax.rem(y + jnp.where(i % 2 == 1, d, Y - d), Y)
        arrived(gall.at[k, x, t], gr.at[t])
        send_x(t)
        return carry

    lax.fori_loop(1, Y, gather_y, 0)

    def send_core(t):
        pltpu.make_async_remote_copy(
            gall.at[k, t], gall.at[k, t], sib_s.at[1], sib_r.at[1],
            device_id=sibling, device_id_type=MESH,
        ).start()

    send_core(x)

    def gather_x(s, carry):
        t = lax.rem(x + jnp.where(s == 2, 3, jnp.where(s == 3, 2, 1)), X)
        arrived(gall.at[k, t], hr.at[t])
        send_core(t)
        return carry

    lax.fori_loop(1, X, gather_x, 0)
    arrived(other_rows, sib_r.at[2])
    data_rows(other)
    arrived(gall.at[other], sib_r.at[1])

    def parts(i):
        return i // X, i % X

    def peak_step(i, peak):
        a, b = parts(i)
        return jnp.maximum(peak, jnp.max(gall[a, b], axis=0))

    peak = jnp.full((2, 8, LANES), -jnp.inf, F32)
    for i in range(2 * X):
        peak = peak_step(i, peak)
    for rounds in range(HALVES // 2):
        top = jnp.max(peak, axis=1, keepdims=True)

        def noise_step(i, acc):
            a, b = parts(i)
            s = gall[a, b]
            if rounds:
                s = s + vbuf[a, b][:, None]
            return acc + jnp.sum(jnp.exp(s - top), axis=0)

        acc = jnp.zeros((2, 8, LANES), F32)
        for i in range(2 * X):
            acc = noise_step(i, acc)
        lse = top + jnp.log(jnp.sum(acc, axis=1, keepdims=True))
        u = jnp.concatenate([(log_a[h] - lse[h])[None] for h in range(2)], axis=0)

        def data_step(i, peak):
            a, b = parts(i)
            s = gall[a, b]
            w = s + u
            m = jnp.max(jnp.max(w, axis=1), axis=2, keepdims=True)
            e = jnp.sum(jnp.sum(jnp.exp(w - m[:, None]), axis=1), axis=2, keepdims=True)
            v = lbuf[a, b] - (m + jnp.log(e))
            vbuf[a, b] = v
            return jnp.maximum(peak, jnp.max(s + v[:, None], axis=0))

        peak = jnp.full((2, 8, LANES), -jnp.inf, F32)
        for i in range(2 * X):
            peak = data_step(i, peak)

    own_u = jnp.where(k == 0, u[0], u[1])
    for i in range(2 * X):
        a, b = parts(i)
        plan[a, b] = jnp.exp(gall[a, b, :, k] + own_u + vbuf[a, b])
    turned[...] = jnp.transpose(plan[...].reshape(C * 32, LANES), (1, 0))
    p = turned[pl.ds(pl.multiple_of(x * YL * 8, YL * 8), YL * 8), :]
    mass = jnp.sum(p, axis=1, keepdims=True)
    value = jnp.dot(
        p.astype(BF16), dfull[...].reshape(C * 32, FS), preferred_element_type=F32
    ) / mass
    tbuf[...] = value.reshape(YL, 8, FS).astype(BF16)

    def send_t(s, carry):
        t = lax.rem(yl + s, YL)
        pltpu.make_async_remote_copy(
            tbuf.at[t], out_ref.at[yl], os_, or_,
            device_id=(place(t, x, k), c), device_id_type=MESH,
        ).start()
        return carry

    lax.fori_loop(1, YL, send_t, 0)
    pltpu.make_async_copy(tbuf.at[yl], out_ref.at[yl], or_).start()

    mine = own_u[:, 0:8]
    for t in range(1, Q):
        mine = jnp.where(x * YL + yl == t, own_u[:, 8 * t:8 * t + 8], mine)
    npot[...] = mine * eps
    lanes4 = lax.broadcasted_iota(jnp.int32, (X, 8, LANES), 2)
    index4 = lax.broadcasted_iota(jnp.int32, (X, 8, LANES), 0) * 8 + lax.broadcasted_iota(
        jnp.int32, (X, 8, LANES), 1
    )
    block = jnp.where(lanes4 == index4, vbuf[yh, :, z], 0.0)
    block = jnp.sum(jnp.sum(block, axis=0), axis=0, keepdims=True)
    dpot[...] = block[:, 0:32] * eps
    pltpu.make_async_copy(npot, npot_ref, ps.at[0]).start()
    pltpu.make_async_copy(dpot, dpot_ref, ps.at[1]).start()
    finish()


def leave(targets_ref, npot_ref, dpot_ref, out_ref, nout_ref, dout_ref, held, npot, dpot, into, out):
    width = targets_ref.shape[2]
    sources = [npot_ref, dpot_ref] + [targets_ref.at[t] for t in range(YL)]
    places = [npot, dpot] + [held.at[t] for t in range(YL)]
    results = [nout_ref, dout_ref] + [
        out_ref.at[:, pl.ds(t * width, width)] for t in range(YL)
    ]
    count = len(places)
    first = [pltpu.make_async_copy(sources[i], places[i], into.at[i]) for i in range(count)]
    second = [pltpu.make_async_copy(places[i], results[i], out.at[i]) for i in range(count)]
    for copy in first:
        copy.start()
    for i in range(count):
        first[i].wait()
        second[i].start()
    for copy in second:
        copy.wait()


def per_device(noise, data, noise_weight, data_weight):
    width = noise.shape[1] * C
    FQ = width // (Q * C)
    FS = X * FQ
    anywhere = pl.BlockSpec(memory_space=pl.ANY)
    dma = pltpu.SemaphoreType.DMA
    targets, noise_pot, data_pot = pl.pallas_call(
        functools.partial(kernel, width),
        out_shape=(
            jax.ShapeDtypeStruct((YL, 8, FS), BF16),
            jax.ShapeDtypeStruct((1, 8), F32),
            jax.ShapeDtypeStruct((1, 32), F32),
        ),
        in_specs=[anywhere] * 4,
        out_specs=(anywhere, anywhere, anywhere),
        scratch_shapes=[
            pltpu.SMEM((8,), jnp.int32),
            pltpu.SMEM((32,), jnp.int32),
            pltpu.VMEM((YL, 8, FS + LANES), BF16),
            pltpu.VMEM((32, 2 * FS), BF16),
            pltpu.VMEM((2 * X, X, 8, FQ), BF16),
            pltpu.VMEM((Z, X, 8, FQ), BF16),
            pltpu.VMEM((1, LANES), F32),
            pltpu.VMEM((2, X, YL, 8, FS + LANES), BF16),
            pltpu.VMEM((2, 8 * Q, FS + LANES), BF16),
            pltpu.VMEM((Z, X, 8, FQ), BF16),
            pltpu.VMEM((2 * X, Z, X, 8, FQ), BF16),
            pltpu.VMEM((2 * X, Z * 8, FS), BF16),
            pltpu.VMEM((Z, YH, 1, LANES), F32),
            pltpu.VMEM((Y, 2, 8, LANES), F32),
            pltpu.VMEM((Y, 2, 8, LANES), F32),
            pltpu.VMEM((2, 8, LANES), F32),
            pltpu.VMEM((Z, 2, 8, LANES), F32),
            pltpu.VMEM((2, X, Y, 2, 8, LANES), F32),
            pltpu.VMEM((2, X, Y, 8, LANES), F32),
            pltpu.VMEM((2, X, Y, 8, LANES), F32),
            pltpu.VMEM((2, X, Z, 8, LANES), F32),
            pltpu.VMEM((LANES, C * 32), F32),
            pltpu.VMEM((YL, 8, FS), BF16),
            pltpu.VMEM((1, 8), F32),
            pltpu.VMEM((1, 32), F32),
            dma((3 + YL,)),
        ] + [dma] * 5 + [dma((Z,))] + [dma] * 8 + [dma((3,))] * 2 + [dma] * 5 + [dma((Y,)), dma, dma((X,)), dma, dma, dma((2,))],
        compiler_params=pltpu.CompilerParams(
            collective_id=0, has_side_effects=True, vmem_limit_bytes=60 * 1024 * 1024
        ),
    )(noise_weight, data_weight, noise, data)
    targets, noise_pot, data_pot = pl.pallas_call(
        leave,
        out_shape=(
            jax.ShapeDtypeStruct((8, YL * FS), BF16),
            jax.ShapeDtypeStruct((1, 8), F32),
            jax.ShapeDtypeStruct((1, 32), F32),
        ),
        in_specs=[anywhere] * 3,
        out_specs=(anywhere, anywhere, anywhere),
        scratch_shapes=[
            pltpu.VMEM((YL, 8, FS), BF16),
            pltpu.VMEM((1, 8), F32),
            pltpu.VMEM((1, 32), F32),
            dma((YL + 2,)),
            dma((YL + 2,)),
        ],
        compiler_params=pltpu.CompilerParams(vmem_limit_bytes=60 * 1024 * 1024),
    )(targets, noise_pot, data_pot)
    return (targets, noise_pot.reshape(8), data_pot.reshape(32))


def solution(mesh):
    placed = (P("row", "col"), P("col", "row"), P("row"), P("col"))
    return jax.shard_map(
        per_device,
        mesh=mesh,
        in_specs=placed,
        out_specs=(P("row", "col"), P("row"), P("col")),
        check_vma=False,
    )
```
